32 devices in a mesh: grp: 2 (over y), tp: 4 (over z), kv: 4 (over x, core).
Axes of the slice: x: 2, y: 2, z: 4, core: 2. Of those that a mesh axis runs over, the one named last changes fastest.
Arguments:
- queries: bfloat16 [64, 4, 16384], P('grp', None, 'kv'), parts along dimension 0, may hold values from -6 to 6
- fresh_keys: bfloat16 [64, 4, 1024], P(('grp', 'tp'), None, 'kv'), parts along dimension 0, may hold values from -6 to 6
- fresh_values: bfloat16 [64, 4, 1024], P(('grp', 'tp'), None, 'kv'), parts along dimension 0, may hold values from -6 to 6
- cache_keys: bfloat16 [16, 128, 4096], P(('grp', 'kv'), 'tp'), parts along dimension 0, may hold values from -6 to 6
- cache_values: bfloat16 [16, 128, 4096], P(('grp', 'kv'), 'tp'), parts along dimension 0, may hold values from -6 to 6
- page_counts: int32 [64], P('grp'), parts along dimension 0, may hold values from 1 to 64, 128 in all
- page_owner: int32 [16, 128], P(('grp', 'kv'), 'tp'), parts along dimension 0, may hold values from 0 to 3, as said below
- out_weight: bfloat16 [16384, 16384], P('kv', 'tp'), may hold values from -0.046875 to 0.046875
Outputs:
- attention_out: bfloat16 [64, 4, 16384], P(('grp', 'kv'), None, 'tp'), parts along dimension 0
- handed_keys: bfloat16 [16, 256, 4096], P(('grp', 'kv'), 'tp'), parts along dimension 0
- handed_values: bfloat16 [16, 256, 4096], P(('grp', 'kv'), 'tp'), parts along dimension 0
- slot_rows: int32 [16, 256], P(('grp', 'kv'), 'tp'), parts along dimension 0
The draws below stay inside these ranges and needn't reach their ends.
There are 2 independent parts, one for each index of `grp`. The reference program is written for one: setup_inputs(seed, part) draws one part's arguments, and reference() takes and returns one part's arrays. A program takes and returns all parts, laid end to end along the dimension named above; an argument that names none is the same for every part. Nothing has to cross between parts.
Inputs may be any that keep to these rules, and one draw needn't show every extreme that they name: `page_owner`: for each KV head and each prefill owner's block of 32 consecutive pages, no decode owner is listed more than 16 times; for each KV head one decode owner is listed exactly 16 times in every block. `page_counts`: the counts sum to 128; the pages of request r follow those of the requests before it in prefill order; the largest count is 64.
All inputs are finite; a program needn't handle non-finite values.
Results may differ from the reference program's by a relative error of at most 0.007.
Values may be sent and summed in bfloat16 or wider, within the bound.
No kernel may reach another device: no remote copies, remote signals or barrier semaphores. Data moves between devices by JAX's collectives and lax.ppermute only.
A program may use at most 128 MiB of HBM per device.

```python
import math
import jax
import jax.numpy as jnp
import numpy as np
from jax import lax

D = 16384
KVH = 8
GROUP = 16
HD = 128
PAGE = 32
ROWS = 32
STEPS = 4
PAGES_DEV = 32
QH = 128
PAGES = 128
CAP = 16
SLOTS_DEV = 64
DSLOTS = 256
MOST_PAGES = 64
N_TP = 4


def draw_queries(key, part):
    key = jax.random.fold_in(key, 11)
    values = jnp.clip(jax.random.normal(key, (ROWS, STEPS, QH * HD)), -6.0, 6.0)
    return values.astype(jnp.bfloat16)


def draw_fresh_keys(key, part):
    key = jax.random.fold_in(key, 13)
    values = jnp.clip(jax.random.normal(key, (ROWS, STEPS, KVH * HD)), -6.0, 6.0)
    return values.astype(jnp.bfloat16)


def draw_cache_keys(key, part):
    key = jax.random.fold_in(key, 19)
    values = jnp.clip(jax.random.normal(key, (KVH, PAGES, PAGE * HD)), -6.0, 6.0)
    return values.astype(jnp.bfloat16)


def one_block(block_key, hot_owner):
    key_order, key_shuffle = jax.random.split(block_key)
    slot_order = jax.random.permutation(key_order, N_TP * CAP)
    owners = slot_order // CAP
    colder = (owners != hot_owner).astype(jnp.int32)
    chosen = owners[jnp.argsort(colder, stable=True)][:PAGES_DEV]
    return chosen[jax.random.permutation(key_shuffle, PAGES_DEV)]


def draw_page_owner(key, part):
    key = jax.random.fold_in(key, 17)
    key_hot, key_blocks = jax.random.split(key)
    hot_owners = jax.random.randint(key_hot, (KVH,), 0, N_TP)

    def one_head(head_index, hot_owner):
        head_key = jax.random.fold_in(key_blocks, head_index)
        return jax.vmap(one_block, in_axes=(0, None))(jax.random.split(head_key, N_TP), hot_owner)
    owners = jax.vmap(one_head)(jnp.arange(KVH), hot_owners)
    return owners.reshape(KVH, PAGES).astype(jnp.int32)


def levels(own_key, dims, cuts, smallest, largest):
    factor_of, own = 1.0, jax.random.fold_in(own_key, 6)
    for dim, blocks in cuts:
        steps = jnp.exp(jax.random.uniform(jax.random.fold_in(own, dim), (blocks,), jnp.float32, smallest / len(cuts), largest / len(cuts)))
        factor_of = factor_of * jnp.repeat(steps, dims[dim] // blocks).reshape([-1 if axis == dim else 1 for axis in range(len(dims))])
    return factor_of


def length_profile(number_of, total, bound, lean):
    loads = [(1 << 20) // math.isqrt(standing ** lean) + 1 for standing in range(2, number_of + 1)]
    rest, given = total - bound - (number_of - 1), [1] * (number_of - 1)
    while rest > 0:
        free = [i for i in range(number_of - 1) if given[i] < bound]
        pool, left = sum([loads[i] for i in free]), rest
        for i in free:
            extra = min(bound - given[i], max(1, left * loads[i] // pool), rest)
            given[i] = given[i] + extra
            rest = rest - extra
    return np.array([bound] + given)


def ragged(own_key, count, total, reach, skew):
    if count == 2:
        one = jax.random.randint(own_key, (), max(1, total - reach), min(reach, total - 1) + 1)
        return jnp.stack([one, total - one])
    tallies = jnp.asarray(length_profile(count, total, reach, skew), jnp.int32)
    pairs = (count - 1) // 2
    source_of, taker = tallies[1:1 + 2 * pairs:2], tallies[2:2 + 2 * pairs:2]
    margin = jnp.minimum(source_of - 1, reach - taker)
    passed = jax.random.randint(jax.random.fold_in(own_key, 1), (pairs,), 0, 1 << 20) % (margin + 1)
    tallies = tallies.at[1:1 + 2 * pairs:2].set(source_of - passed).at[2:2 + 2 * pairs:2].set(taker + passed)
    return tallies[jax.random.permutation(jax.random.fold_in(own_key, 2), count)]


def normal_values(key, shape, scale, most, shards=(), kind=jnp.bfloat16):
    values = scale * jax.random.normal(key, shape, jnp.float32)
    if shards:
        values = values * levels(key, shape, shards, -0.22, 0.18)
    return jnp.clip(values, -most, most).astype(kind)


def setup_inputs(seed: int = 0, part: int = 0) -> dict:
    keys = jax.random.split(jax.random.key(seed), 9)
    part_splits = jax.random.split(jax.random.fold_in(keys[8], part), 9)
    queries = draw_queries(jax.random.fold_in(jax.random.fold_in(keys[8], part), 71), part)
    fresh_keys = draw_fresh_keys(jax.random.fold_in(jax.random.fold_in(keys[8], part), 71), part)
    fresh_values = normal_values(part_splits[2], (ROWS, STEPS, KVH * HD), 1.0, 6.0, ((0, 4), (2, 4)))
    cache_keys = draw_cache_keys(jax.random.fold_in(jax.random.fold_in(keys[8], part), 71), part)
    cache_values = normal_values(part_splits[4], (KVH, PAGES, PAGE * HD), 1.0, 6.0, ((0, 4), (1, 4)))
    page_counts = ragged(part_splits[5], ROWS, PAGES, MOST_PAGES, 2).astype(jnp.int32)
    page_owner = draw_page_owner(jax.random.fold_in(jax.random.fold_in(keys[8], part), 71), part)
    out_weight = normal_values(keys[7], (QH * HD, D), (QH * HD) ** -0.5, 0.046875, ((0, 4), (1, 4)))
    return dict(queries=queries, fresh_keys=fresh_keys, fresh_values=fresh_values, cache_keys=cache_keys, cache_values=cache_values, page_counts=page_counts, page_owner=page_owner, out_weight=out_weight)


NEGATIVE = -1.0e30


def place_slots(buffer, slot_index, entries):
    return buffer.at[slot_index].set(entries)


def reference(queries, fresh_keys, fresh_values, cache_keys, cache_values, page_counts, page_owner, out_weight):
    highest = lax.Precision.HIGHEST
    page_ids = jnp.arange(PAGES, dtype=jnp.int32)
    row_ends = jnp.cumsum(page_counts)
    page_row = jnp.sum((row_ends[None, :] <= page_ids[:, None]).astype(jnp.int32), axis=1).astype(jnp.int32)
    blocks = page_owner.reshape(KVH, N_TP, PAGES_DEV)
    owner_ids = jnp.arange(N_TP, dtype=jnp.int32)
    onehot = (blocks[:, :, :, None] == owner_ids[None, None, None, :]).astype(jnp.int32)
    page_rank = jnp.sum((jnp.cumsum(onehot, axis=2) - onehot) * onehot, axis=3)
    slot_index = (blocks * SLOTS_DEV + owner_ids[None, :, None] * CAP + page_rank).reshape(KVH, PAGES).astype(jnp.int32)
    handed_keys = jax.vmap(place_slots)(jnp.zeros((KVH, DSLOTS, PAGE * HD), jnp.bfloat16), slot_index, cache_keys)
    handed_values = jax.vmap(place_slots)(jnp.zeros((KVH, DSLOTS, PAGE * HD), jnp.bfloat16), slot_index, cache_values)
    slot_rows = jax.vmap(place_slots)(jnp.full((KVH, DSLOTS), -1, jnp.int32), slot_index, jnp.broadcast_to(page_row, (KVH, PAGES)))

    score_scale = HD ** -0.5
    query_all = queries.astype(jnp.float32).reshape(ROWS, STEPS, KVH, GROUP, HD)
    fresh_key_all = fresh_keys.astype(jnp.float32).reshape(ROWS, STEPS, KVH, HD)
    fresh_value_all = fresh_values.astype(jnp.float32).reshape(ROWS, STEPS, KVH, HD)
    steps_seen = jnp.arange(STEPS)
    causal = steps_seen[:, None] >= steps_seen[None, :]
    results = []
    for head_index in range(KVH):
        query_head = query_all[:, :, head_index]
        chosen = query_head.reshape(ROWS, STEPS * GROUP, HD)[page_row]
        key_block = cache_keys[head_index].astype(jnp.float32).reshape(PAGES, PAGE, HD)
        value_block = cache_values[head_index].astype(jnp.float32).reshape(PAGES, PAGE, HD)
        scores = jnp.einsum("pqd,ptd->pqt", chosen, key_block, precision=highest) * score_scale
        page_max = jnp.max(scores, axis=2)
        page_weight = jnp.exp(scores - page_max[:, :, None]).astype(jnp.bfloat16)
        page_weight = lax.optimization_barrier(page_weight).astype(jnp.float32)
        page_total = jnp.sum(page_weight, axis=2)
        page_numer = jnp.einsum("pqt,ptd->pqd", page_weight, value_block, precision=highest)
        fresh_scores = jnp.einsum("rsgd,rud->rsgu", query_head, fresh_key_all[:, :, head_index], precision=highest) * score_scale
        fresh_scores = jnp.where(causal[None, :, None, :], fresh_scores, NEGATIVE)
        fresh_max = jnp.max(fresh_scores, axis=3)
        fresh_weight = jnp.exp(fresh_scores - fresh_max[..., None]).astype(jnp.bfloat16)
        fresh_weight = lax.optimization_barrier(fresh_weight).astype(jnp.float32)
        fresh_total = jnp.sum(fresh_weight, axis=3)
        fresh_numer = jnp.einsum("rsgu,rud->rsgd", fresh_weight, fresh_value_all[:, :, head_index], precision=highest)
        row_max = jax.ops.segment_max(page_max, page_row, num_segments=ROWS).reshape(ROWS, STEPS, GROUP)
        row_max = jnp.maximum(row_max, fresh_max)
        flat_max = row_max.reshape(ROWS, STEPS * GROUP)
        page_factor = jnp.exp(page_max - flat_max[page_row])
        fresh_factor = jnp.exp(fresh_max - row_max)
        numer = jax.ops.segment_sum(page_numer * page_factor[:, :, None], page_row, num_segments=ROWS).reshape(ROWS, STEPS, GROUP, HD)
        numer = numer + fresh_numer * fresh_factor[..., None]
        denom = jax.ops.segment_sum(page_total * page_factor, page_row, num_segments=ROWS).reshape(ROWS, STEPS, GROUP)
        denom = denom + fresh_total * fresh_factor
        results.append(numer / denom[..., None])
    attended = jnp.stack(results, axis=2).reshape(ROWS, STEPS, QH * HD).astype(jnp.bfloat16)
    projected = jnp.dot(attended.reshape(ROWS * STEPS, QH * HD), out_weight, preferred_element_type=jnp.float32)
    attention_out = projected.reshape(ROWS, STEPS, D).astype(jnp.bfloat16)
    return (attention_out, handed_keys, handed_values, slot_rows)
```

```python
import functools

import jax
import jax.numpy as jnp
from jax import lax
from jax.experimental import pallas as pl
from jax.experimental.pallas import tpu as pltpu
from jax.sharding import PartitionSpec as P

HD = 128
LANES = 128
NEGATIVE = -1e30
HIGHEST = lax.Precision.HIGHEST
VMEM_BYTES = 24 * 1024 * 1024


def round_up(value, step):
    return -(-value // step) * step


def flip(size, bit):
    return [(i, i ^ bit) for i in range(size)]


def params():
    return pltpu.CompilerParams(vmem_limit_bytes=VMEM_BYTES)


def hand_kernel(cap, owner_ref, key_ref, value_ref, send_key_ref, send_value_ref):
    dest_count, head_count = send_key_ref.shape[0], send_key_ref.shape[1]
    page_count, width = key_ref.shape[1], key_ref.shape[2]
    dest_rows = max(8, dest_count)
    step = min(width, 1024)
    earlier = (
        lax.broadcasted_iota(jnp.int32, (page_count, page_count), 0)
        < lax.broadcasted_iota(jnp.int32, (page_count, page_count), 1)
    ).astype(jnp.bfloat16)
    for head in range(head_count):
        owner = owner_ref[head : head + 1, :]
        listed = (
            lax.broadcasted_iota(jnp.int32, (dest_rows, page_count), 0) == owner
        ).astype(jnp.float32)
        before = jnp.dot(
            listed.astype(jnp.bfloat16), earlier, preferred_element_type=jnp.float32
        )
        rank = jnp.sum(before * listed, axis=0, keepdims=True).astype(jnp.int32)
        slot = owner * cap + rank
        pick = (
            lax.broadcasted_iota(jnp.int32, (dest_count * cap, page_count), 0) == slot
        ).astype(jnp.bfloat16)
        for source, target in ((key_ref, send_key_ref), (value_ref, send_value_ref)):
            for start in range(0, width, step):
                placed = jnp.dot(
                    pick,
                    source[head, :, start : start + step],
                    preferred_element_type=jnp.float32,
                ).astype(jnp.bfloat16)
                for dest in range(dest_count):
                    target[dest, head, :, start : start + step] = placed[
                        dest * cap : (dest + 1) * cap
                    ]


def place_pages(page_owner, cache_keys, cache_values, dest_count, cap):
    head_count, _, width = cache_keys.shape
    shape = jax.ShapeDtypeStruct((dest_count, head_count, cap, width), jnp.bfloat16)
    return pl.pallas_call(
        functools.partial(hand_kernel, cap),
        out_shape=(shape, shape),
        compiler_params=params(),
        name="place_pages",
    )(page_owner, cache_keys, cache_values)


def list_slot_rows(page_owner, row_ends, tp_index, tp_size, cap):
    head_count, pages_here = page_owner.shape
    owners = lax.all_gather(page_owner, "tp", axis=1, tiled=False)
    ids = jnp.arange(pages_here, dtype=jnp.int32)
    same = (owners[..., :, None] == owners[..., None, :]) & (ids[:, None] < ids[None, :])
    rank = jnp.sum(same.astype(jnp.int32), axis=2)
    page_ids = jnp.arange(tp_size * pages_here, dtype=jnp.int32)
    page_row = jnp.sum((row_ends[None, :] <= page_ids[:, None]).astype(jnp.int32), axis=1)
    here = (owners == tp_index)[..., None, :] & (
        rank[..., None, :] == jnp.arange(cap, dtype=jnp.int32)[:, None]
    )
    marks = jnp.where(here, page_row.reshape(tp_size, 1, pages_here) + 1, 0)
    return (jnp.sum(marks, axis=3) - 1).reshape(head_count, tp_size * cap)


def attend_kernel(
    steps, has_earlier, last, chunks, *refs
):
    query_ref, tokens_ref, member_ref, member_t_ref = refs[:4]
    refs = refs[4:]
    if has_earlier:
        early_max_ref, early_total_ref, early_numer_ref = refs[:3]
        refs = refs[3:]
    if last:
        payload_refs, refs = refs[:chunks], refs[chunks:]
    else:
        out_max_ref, out_total_ref, out_numer_ref = refs[:3]
        refs = refs[3:]
    chosen, numers, high, low = refs

    row_lines, query_width = query_ref.shape
    group = query_width // HD
    member_lines = member_ref.shape[0]
    held, page_len = tokens_ref.shape[0] // 2, tokens_ref.shape[1]
    pages = held - 1
    page_lines = pages * steps
    used_lines = page_lines + page_len
    scale = HD ** (-0.5)
    lane = lax.broadcasted_iota(jnp.int32, (1, LANES), 1)

    chosen[...] = jnp.dot(
        member_ref[...], query_ref[...], preferred_element_type=jnp.float32
    ).astype(jnp.bfloat16)

    maxima, totals = [], []

    def one_block(first_line, lines, keys, values, mask):
        queries = jnp.concatenate(
            [
                chosen[first_line : first_line + lines, g * HD : (g + 1) * HD]
                for g in range(group)
            ],
            axis=0,
        )
        scores = (
            lax.dot_general(
                queries, keys, (((1,), (1,)), ((), ())), preferred_element_type=jnp.float32
            )
            * scale
        )
        scores = jnp.where(mask, scores, NEGATIVE)
        largest = jnp.max(scores, axis=1, keepdims=True)
        weights = jnp.exp(scores - largest).astype(jnp.bfloat16)
        total = jnp.sum(weights.astype(jnp.float32), axis=1, keepdims=True)
        numer = jnp.dot(weights, values, preferred_element_type=jnp.float32)
        block_max = jnp.zeros((lines, LANES), jnp.float32)
        block_total = jnp.zeros((lines, LANES), jnp.float32)
        for g in range(group):
            part = slice(g * lines, (g + 1) * lines)
            block_max = jnp.where(lane == g, largest[part], block_max)
            block_total = jnp.where(lane == g, total[part], block_total)
            numers[first_line : first_line + lines, g * HD : (g + 1) * HD] = numer[part]
        maxima.append(block_max)
        totals.append(block_total)

    batch = min(pages, max(1, 128 // page_len))
    lines = batch * steps
    line = lax.broadcasted_iota(jnp.int32, (group * lines, batch * page_len), 0)
    token = lax.broadcasted_iota(jnp.int32, (group * lines, batch * page_len), 1)
    mask = (line % lines) // steps == token // page_len
    for first in range(0, pages, batch):
        one_block(
            first * steps,
            lines,
            tokens_ref[first : first + batch].reshape(batch * page_len, HD),
            tokens_ref[held + first : held + first + batch].reshape(batch * page_len, HD),
            mask,
        )
    line = lax.broadcasted_iota(jnp.int32, (group * page_len, page_len), 0) % page_len
    token = lax.broadcasted_iota(jnp.int32, (group * page_len, page_len), 1)
    mask = (line // steps == token // steps) & (token % steps <= line % steps)
    one_block(page_lines, page_len, tokens_ref[pages], tokens_ref[held + pages], mask)

    spare = member_lines - used_lines
    if spare:
        maxima.append(jnp.zeros((spare, LANES), jnp.float32))
        totals.append(jnp.zeros((spare, LANES), jnp.float32))
    line_max = jnp.concatenate(maxima, axis=0)
    line_total = jnp.concatenate(totals, axis=0)

    member_t = member_t_ref[...]
    is_member = member_t > 0
    line_max_t = jnp.transpose(line_max)
    row_max = jnp.full((row_lines, LANES), NEGATIVE, jnp.float32)
    for g in range(group):
        best = jnp.max(
            jnp.where(is_member, line_max_t[g : g + 1, :], NEGATIVE), axis=1, keepdims=True
        )
        row_max = jnp.where(lane == g, best, row_max)
    spread = jnp.dot(
        member_ref[...].astype(jnp.float32),
        row_max,
        precision=HIGHEST,
        preferred_element_type=jnp.float32,
    )
    factor = jnp.exp(jnp.minimum(line_max - spread, 0.0))
    row_total = jnp.dot(
        member_t.astype(jnp.float32),
        line_total * factor,
        precision=HIGHEST,
        preferred_element_type=jnp.float32,
    )
    if spare:
        high[used_lines:, :] = jnp.zeros((spare, query_width), jnp.bfloat16)
        low[used_lines:, :] = jnp.zeros((spare, query_width), jnp.bfloat16)
    for g in range(group):
        columns = slice(g * HD, (g + 1) * HD)
        scaled = numers[:, columns] * factor[:used_lines, g : g + 1]
        rounded = scaled.astype(jnp.bfloat16)
        high[:used_lines, columns] = rounded
        low[:used_lines, columns] = (scaled - rounded.astype(jnp.float32)).astype(jnp.bfloat16)

    if has_earlier:
        early_max = early_max_ref[...]
        largest = jnp.maximum(row_max, early_max)
        scale_now = jnp.exp(row_max - largest)
        scale_early = jnp.exp(early_max - largest)
        row_total = row_total * scale_now + early_total_ref[...] * scale_early
        row_max = largest
    if last:
        present = row_total > 0
        inverse = jnp.where(present, 1.0 / jnp.where(present, row_total, 1.0), 0.0)
        log_sum = jnp.where(
            present & (lane < group),
            row_max + jnp.log(jnp.where(present, row_total, 1.0)),
            jnp.where(lane < group, NEGATIVE, 0.0),
        )
        if has_earlier:
            scale_now = scale_now * inverse
            scale_early = scale_early * inverse
        else:
            scale_now = inverse
        part = group // chunks
        for chunk in range(chunks):
            if chunk == 0:
                payload_refs[0][:, part * HD :] = split_sums(log_sum, group)
    for g in range(group):
        columns = slice(g * HD, (g + 1) * HD)
        numer = jnp.dot(
            member_t, high[:, columns], preferred_element_type=jnp.float32
        ) + jnp.dot(member_t, low[:, columns], preferred_element_type=jnp.float32)
        if has_earlier:
            numer = (
                numer * scale_now[:, g : g + 1]
                + early_numer_ref[:, columns] * scale_early[:, g : g + 1]
            )
        elif last:
            numer = numer * scale_now[:, g : g + 1]
        if last:
            place = g % part
            payload_refs[g // part][:, place * HD : (place + 1) * HD] = numer.astype(jnp.bfloat16)
        else:
            out_numer_ref[:, columns] = numer
    if not last:
        out_max_ref[...] = row_max
        out_total_ref[...] = row_total


def split_sums(value, group):
    first = value.astype(jnp.bfloat16).astype(jnp.float32)
    rest = value - first
    second = rest.astype(jnp.bfloat16).astype(jnp.float32)
    third = rest - second
    return (
        first + pltpu.roll(second, group, axis=1) + pltpu.roll(third, 2 * group, axis=1)
    ).astype(jnp.bfloat16)


def join_sums(parts, group):
    parts = parts.astype(jnp.float32)
    return (
        parts
        + pltpu.roll(parts, LANES - group, axis=1)
        + pltpu.roll(parts, LANES - 2 * group, axis=1)
    )


def attend(query, tokens, member, member_t, earlier, last, steps, chunks):
    row_lines, query_width = query.shape
    group = query_width // HD
    held, page_len = tokens.shape[0] // 2, tokens.shape[1]
    member_lines = member.shape[0]
    used_lines = (held - 1) * steps + page_len
    stat = jax.ShapeDtypeStruct((row_lines, LANES), jnp.float32)
    if last:
        part = group // chunks * HD
        out_shape = tuple(
            jax.ShapeDtypeStruct((row_lines, part + (LANES if c == 0 else 0)), jnp.bfloat16)
            for c in range(chunks)
        )
    else:
        out_shape = (stat, stat, jax.ShapeDtypeStruct((row_lines, query_width), jnp.float32))
    return pl.pallas_call(
        functools.partial(attend_kernel, steps, earlier is not None, last, chunks),
        out_shape=out_shape,
        scratch_shapes=[
            pltpu.VMEM((member_lines, query_width), jnp.bfloat16),
            pltpu.VMEM((used_lines, query_width), jnp.float32),
            pltpu.VMEM((member_lines, query_width), jnp.bfloat16),
            pltpu.VMEM((member_lines, query_width), jnp.bfloat16),
        ],
        compiler_params=params(),
        cost_estimate=pl.CostEstimate(
            flops=4 * 1024 * 1024 * 1024, bytes_accessed=4 * 1024 * 1024, transcendentals=0
        ),
        name="attend",
    )(query, tokens, member, member_t, *(earlier or ()))


def combine_kernel(group, first_group, sums_ref, their_sums_ref, mine_ref, theirs_ref, out_ref):
    wide = out_ref.shape[1]
    sums = join_sums(sums_ref[...], group)
    their_sums = join_sums(their_sums_ref[...], group)
    largest = jnp.maximum(sums, their_sums)
    weight = jnp.exp(sums - largest)
    their_weight = jnp.exp(their_sums - largest)
    inverse = 1.0 / (weight + their_weight)
    weight = weight * inverse
    their_weight = their_weight * inverse
    for place in range(wide // HD):
        g = first_group + place
        columns = slice(place * HD, (place + 1) * HD)
        out_ref[:, columns] = (
            mine_ref[:, columns].astype(jnp.float32) * weight[:, g : g + 1]
            + theirs_ref[:, columns].astype(jnp.float32) * their_weight[:, g : g + 1]
        ).astype(jnp.bfloat16)


def combine(group, first_group, sums, their_sums, mine, theirs, wide):
    row_lines = mine.shape[0]
    return pl.pallas_call(
        functools.partial(combine_kernel, group, first_group),
        out_shape=jax.ShapeDtypeStruct((row_lines, wide), jnp.bfloat16),
        compiler_params=params(),
        name="combine",
    )(sums, their_sums, mine, theirs)


def project_kernel(has_total, chunk_lines, place_ref, *refs):
    input_ref, weight_ref = refs[:2]
    refs = refs[2:]
    product = jnp.dot(input_ref[...], weight_ref[...], preferred_element_type=jnp.float32)
    if has_total:
        product = product + refs[0][...]
        refs = refs[1:]
    if chunk_lines is None:
        refs[0][...] = product
        return
    keep_ref, send_ref = refs
    core = place_ref[1]
    for pair in range(keep_ref.shape[0]):
        first = product[2 * pair * chunk_lines : (2 * pair + 1) * chunk_lines]
        second = product[(2 * pair + 1) * chunk_lines : (2 * pair + 2) * chunk_lines]
        keep_ref[pair] = jnp.where(core == 0, first, second)
        send_ref[pair] = jnp.where(core == 0, second, first).astype(send_ref.dtype)


def project(place, inputs, weight, total, columns, chunk_lines):
    row_lines, depth = inputs.shape
    first, width = columns
    block = min(width, 512)
    offset = first // block
    in_specs = [
        pl.BlockSpec((row_lines, depth), lambda n, place: (0, 0)),
        pl.BlockSpec((depth, block), lambda n, place: (place[0], n + offset)),
    ]
    operands = [inputs, weight]
    if total is not None:
        in_specs.append(pl.BlockSpec((row_lines, block), lambda n, place: (0, n + offset)))
        operands.append(total)
    if chunk_lines is None:
        out_shape = jax.ShapeDtypeStruct((row_lines, width), jnp.float32)
        out_specs = pl.BlockSpec((row_lines, block), lambda n, place: (0, n))
    else:
        pairs = row_lines // (2 * chunk_lines)
        shape = (pairs, chunk_lines, width)
        out_shape = (
            jax.ShapeDtypeStruct(shape, jnp.float32),
            jax.ShapeDtypeStruct(shape, jnp.bfloat16),
        )
        spec = pl.BlockSpec((pairs, chunk_lines, block), lambda n, place: (0, 0, n))
        out_specs = (spec, spec)
    return pl.pallas_call(
        functools.partial(project_kernel, total is not None, chunk_lines),
        grid_spec=pltpu.PrefetchScalarGridSpec(
            num_scalar_prefetch=1,
            grid=(width // block,),
            in_specs=in_specs,
            out_specs=out_specs,
        ),
        out_shape=out_shape,
        compiler_params=params(),
        cost_estimate=pl.CostEstimate(
            flops=2 * row_lines * depth * width,
            bytes_accessed=2 * depth * width,
            transcendentals=0,
        ),
        name="project",
    )(place, *operands)


def sum_heads(keep, send, kv_index, kv_size):
    total = keep + lax.ppermute(send, "kv", flip(kv_size, 1)).astype(jnp.float32)
    half = kv_index // 2
    result = lax.dynamic_index_in_dim(total, half, 0, keepdims=False)
    for step in range(1, kv_size // 2):
        part = lax.dynamic_index_in_dim(total, half ^ step, 0, keepdims=False)
        got = lax.ppermute(part.astype(jnp.bfloat16), "kv", flip(kv_size, 2 * step))
        result = result + got.astype(jnp.float32)
    return result.astype(jnp.bfloat16)


def body(
    queries, fresh_keys, fresh_values, cache_keys, cache_values, page_counts, page_owner, out_weight
):
    tp_size, kv_size = lax.axis_size("tp"), lax.axis_size("kv")
    tp_index, kv_index = lax.axis_index("tp"), lax.axis_index("kv")
    head_count, pages_here, page_width = cache_keys.shape
    row_count, step_count, query_width = queries.shape
    own_rows = fresh_keys.shape[0]
    page_len = page_width // HD
    row_lines = row_count * step_count
    head_width = query_width // head_count
    group = head_width // HD
    cap = max(2, (2 * pages_here + tp_size - 1) // tp_size)
    rows = jnp.arange(row_count, dtype=jnp.int32)

    own_head = tp_index % head_count
    spare = page_len - own_rows * step_count

    def by_head(fresh):
        split = fresh.reshape(own_rows * step_count, head_count, HD).transpose(1, 0, 2)
        return jnp.pad(split, ((0, 0), (0, spare), (0, 0)))[:, None]

    def paged(cache):
        return cache.reshape(head_count, pages_here, page_len, HD)

    tokens = jnp.concatenate(
        [paged(cache_keys), by_head(fresh_keys), paged(cache_values), by_head(fresh_values)], axis=1
    )
    own_tokens = lax.dynamic_index_in_dim(tokens, own_head, 0, keepdims=False)
    if head_count == 2:
        other_tokens = lax.dynamic_index_in_dim(tokens, 1 - own_head, 0, keepdims=False)
        near_tokens = lax.ppermute(other_tokens, "tp", flip(tp_size, 1))

    row_ends = jnp.sum(jnp.where(rows[None, :] <= rows[:, None], page_counts[None, :], 0), axis=1)
    send_keys, send_values = place_pages(page_owner, cache_keys, cache_values, tp_size, cap)

    def hand_over(pages):
        got = lax.all_to_all(pages, "tp", split_axis=0, concat_axis=0, tiled=True)
        return got.transpose(1, 0, 2, 3).reshape(head_count, tp_size * cap, page_width)

    slot_keys = hand_over(send_keys)
    slot_values = hand_over(send_values)
    slot_rows = list_slot_rows(page_owner, row_ends, tp_index, tp_size, cap)

    page_lines = pages_here * step_count
    member_lines = round_up(page_lines + page_len, LANES)
    line = jnp.arange(member_lines, dtype=jnp.int32)
    query_line = jnp.arange(row_lines, dtype=jnp.int32)
    query_row = query_line // step_count
    ends = jnp.sum(jnp.where(rows[None, :] <= query_row[:, None], page_counts[None, :], 0), axis=1)
    counts = jnp.sum(jnp.where(rows[None, :] == query_row[:, None], page_counts[None, :], 0), axis=1)

    def membership(owner, line, query_line, ends, starts):
        page = owner * pages_here + line // step_count
        in_row = (starts <= page) & (page < ends) & (line % step_count == query_line % step_count)
        own_line = line - page_lines
        is_own = (
            (own_line >= 0)
            & (own_line < own_rows * step_count)
            & (query_line == owner * own_rows * step_count + own_line)
        )
        return (((line < page_lines) & in_row) | is_own).astype(jnp.bfloat16)

    def members(owner):
        starts = ends - counts
        return (
            membership(owner, line[:, None], query_line[None, :], ends[None, :], starts[None, :]),
            membership(owner, line[None, :], query_line[:, None], ends[:, None], starts[:, None]),
        )

    own_query = lax.dynamic_slice_in_dim(
        queries.reshape(row_lines, query_width), own_head * head_width, head_width, 1
    )
    outer = tp_size // head_count
    chunks = 2 if outer == 2 and group % 2 == 0 else 1
    if head_count == 2:
        earlier = attend(own_query, own_tokens, *members(tp_index), None, False, step_count, chunks)
        payload = attend(
            own_query, near_tokens, *members(tp_index ^ 1), earlier, True, step_count, chunks
        )
    else:
        payload = attend(own_query, own_tokens, *members(tp_index), None, True, step_count, chunks)

    part = head_width // chunks
    own_parts, near_parts = [], []
    if outer == 2:
        far = [lax.ppermute(p, "tp", flip(tp_size, head_count)) for p in payload]
        for c in range(chunks):
            own_parts.append(
                combine(
                    group,
                    c * (group // chunks),
                    payload[0][:, part:],
                    far[0][:, part:],
                    payload[c][:, :part],
                    far[c][:, :part],
                    part,
                )
            )
    else:
        raw = payload[0][:, part:].astype(jnp.float32)
        sums = raw[:, :group] + raw[:, group : 2 * group] + raw[:, 2 * group : 3 * group]
        weight = jnp.exp(sums - lax.pmax(sums, "tp"))
        numer = payload[0][:, :part].astype(jnp.float32).reshape(row_lines, group, HD)
        numer = lax.psum(numer * weight[..., None], "tp")
        joined = numer / lax.psum(weight, "tp")[..., None]
        own_parts.append(joined.reshape(row_lines, head_width).astype(jnp.bfloat16))
    if head_count == 2:
        near_parts = [lax.ppermute(p, "tp", flip(tp_size, 1)) for p in own_parts]

    core = kv_index % 2
    chunk_lines = row_lines // kv_size
    out_width = out_weight.shape[1]
    own_place = jnp.stack([own_head, core]).astype(jnp.int32)
    own_input = jnp.concatenate(own_parts, axis=1)
    results = []
    if head_count == 2:
        total = project(own_place, own_input, out_weight, None, (0, out_width), None)
        near_place = jnp.stack([1 - own_head, core]).astype(jnp.int32)
        near_input = jnp.concatenate(near_parts, axis=1)
        for first in (0, out_width // 2):
            keep, send = project(
                near_place, near_input, out_weight, total, (first, out_width // 2), chunk_lines
            )
            results.append(sum_heads(keep, send, kv_index, kv_size))
    else:
        keep, send = project(own_place, own_input, out_weight, None, (0, out_width), chunk_lines)
        results.append(sum_heads(keep, send, kv_index, kv_size))
    attention_out = jnp.concatenate(results, axis=1).reshape(-1, step_count, out_width)
    return (attention_out, slot_keys, slot_values, slot_rows)


def solution(mesh):
    return jax.shard_map(
        body,
        mesh=mesh,
        in_specs=(
            P("grp", None, "kv"),
            P(("grp", "tp"), None, "kv"),
            P(("grp", "tp"), None, "kv"),
            P(("grp", "kv"), "tp", None),
            P(("grp", "kv"), "tp", None),
            P("grp"),
            P(("grp", "kv"), "tp"),
            P("kv", "tp"),
        ),
        out_specs=(
            P(("grp", "kv"), None, "tp"),
            P(("grp", "kv"), "tp", None),
            P(("grp", "kv"), "tp", None),
            P(("grp", "kv"), "tp"),
        ),
        check_vma=False,
    )
```

```python
import functools

import jax
import jax.numpy as jnp
from jax import lax
from jax.experimental import pallas as pl
from jax.experimental.pallas import tpu as pltpu
from jax.sharding import PartitionSpec as P

HD = 128
LANES = 128
NEGATIVE = -1e30
HIGHEST = lax.Precision.HIGHEST
MIB = 1024 * 1024


def round_up(value, step):
    return -(-value // step) * step


def flip(size, bit):
    return [(i, i ^ bit) for i in range(size)]


def params(mib):
    return pltpu.CompilerParams(vmem_limit_bytes=mib * MIB)


def in_hbm(*arrays):
    return [pltpu.with_memory_space_constraint(array, pltpu.HBM) for array in arrays]


def vmem():
    return pl.BlockSpec(memory_space=pltpu.VMEM)


def hbm():
    return pl.BlockSpec(memory_space=pltpu.HBM)


def anywhere():
    return pl.BlockSpec(memory_space=pl.ANY)


def call(kernel, operands, in_specs, follows=(), **rest):
    count, extra = len(operands), len(follows)

    def without_extra(*refs):
        kernel(*refs[:count], *refs[count + extra :])

    return pl.pallas_call(
        without_extra,
        in_specs=list(in_specs) + [anywhere()] * extra,
        cost_estimate=pl.CostEstimate(flops=0, bytes_accessed=0, transcendentals=0),
        **rest,
    )(*operands, *follows)


def tie(value, *follows):
    return call(
        lambda value_ref, out_ref: None,
        (value,),
        [anywhere()],
        follows,
        out_specs=anywhere(),
        out_shape=jax.ShapeDtypeStruct(value.shape, value.dtype),
        input_output_aliases={0: 0},
        compiler_params=params(1),
        name="tie",
    )


def earlier_pages(page_count):
    first = lax.broadcasted_iota(jnp.int32, (page_count, page_count), 0)
    second = lax.broadcasted_iota(jnp.int32, (page_count, page_count), 1)
    return (first < second).astype(jnp.bfloat16)


def rank_pages(away, earlier, dest_rows):
    ways = lax.broadcasted_iota(jnp.int32, (dest_rows, away.shape[1]), 0)
    listed = (ways == away).astype(jnp.float32)
    before = jnp.dot(listed.astype(jnp.bfloat16), earlier, preferred_element_type=jnp.float32)
    return jnp.sum(before * listed, axis=0, keepdims=True).astype(jnp.int32)


def slot_picks(owners, me, distances, cap, tp_size):
    head_count, page_count = owners.shape
    earlier = earlier_pages(page_count)
    row = lax.broadcasted_iota(jnp.int32, (cap, page_count), 0)
    picks = []
    for head in range(head_count):
        away = owners[head : head + 1, :] ^ me
        rank = rank_pages(away, earlier, round_up(tp_size, 8))
        picks.append([((away == d) & (rank == row)).astype(jnp.float32) for d in distances])
    return picks


def place_rows(pages_ref, pick, targets):
    width, cap = pages_ref.shape[1], pick[0].shape[0]
    step = min(width, 1024)
    for start in range(0, width, step):
        columns = slice(start, start + step)
        placed = jnp.dot(
            jnp.concatenate(pick).astype(jnp.bfloat16),
            pages_ref[:, columns],
            preferred_element_type=jnp.float32,
        ).astype(jnp.bfloat16)
        for which, target in enumerate(targets):
            target[:, columns] = placed[which * cap : (which + 1) * cap]


def place_kernel(cap, jobs, by_index, tp_size, owner_ref, *refs):
    count = (len(refs) - 2 - len(jobs)) // 2
    sources, targets = refs[:count], refs[count : count + len(jobs)]
    held, owners, arrived = refs[count + len(jobs) : -2], refs[-2], refs[-1]
    head_count = sources[0].shape[0]
    copies = [
        pltpu.make_async_copy(source, target, arrived.at[i])
        for i, (source, target) in enumerate(zip((owner_ref, *sources), (owners, *held)))
    ]
    for copy in copies:
        copy.start()
    copies[0].wait()
    me = 0 if by_index else lax.axis_index("tp")
    own_head = lax.rem(me, head_count)
    picks = slot_picks(owners, me, [d for d, _ in jobs], cap, tp_size)

    def place(index, head, pick, target_of):
        place_rows(held[index].at[head], pick, target_of)

    shared = [i for i, (_, every) in enumerate(jobs) if every]
    single = [i for i, (_, every) in enumerate(jobs) if not every]
    for index in range(count):
        copies[index + 1].wait()
        for head in range(head_count):
            if shared:
                pick = [picks[head][i] for i in shared]
                place(index, head, pick, [targets[i].at[index, head] for i in shared])
        if single:
            pick = []
            for i in single:
                chosen = picks[0][i]
                for head in range(1, head_count):
                    chosen = jnp.where(own_head == head, picks[head][i], chosen)
                pick.append(chosen)
            place(index, own_head, pick, [targets[i].at[index] for i in single])


def place_pages(page_owner, caches, jobs, cap, tp_size, by_index, follows=()):
    head_count, page_count, width = caches[0].shape
    return call(
        functools.partial(place_kernel, cap, jobs, by_index, tp_size),
        in_hbm(page_owner, *caches),
        [hbm()] * (1 + len(caches)),
        follows,
        out_specs=tuple(vmem() for _ in jobs),
        out_shape=tuple(
            jax.ShapeDtypeStruct(
                (len(caches),) + ((head_count,) if every else ()) + (cap, width), jnp.bfloat16
            )
            for _, every in jobs
        ),
        scratch_shapes=[pltpu.VMEM(cache.shape, cache.dtype) for cache in caches]
        + [
            pltpu.VMEM(page_owner.shape, jnp.int32),
            pltpu.SemaphoreType.DMA((1 + len(caches),)),
        ],
        compiler_params=params(8),
        name="place_pages",
    )


def place_near_kernel(tp_size, head_count, tokens_ref, out_ref):
    cap, width = out_ref.shape[1:]
    held, page_len = (tokens_ref.shape[0] - 1) // 2, tokens_ref.shape[1]
    pages = held - 1
    me = lax.axis_index("tp")
    head = lax.rem(me, head_count)
    lists = tokens_ref[2 * held].astype(jnp.float32)[:, :pages].astype(jnp.int32)
    owner = lists[0:1]
    for which in range(1, head_count):
        owner = jnp.where(head == which, lists[which : which + 1], owner)
    rank = rank_pages(owner, earlier_pages(pages), round_up(tp_size, 8))
    row = lax.broadcasted_iota(jnp.int32, (cap, pages), 0)
    pick = ((owner == me) & (rank == row)).astype(jnp.bfloat16)
    for index in range(2):
        paged = tokens_ref[index * held : index * held + pages].reshape(pages, page_len * HD)
        out_ref[index] = jnp.dot(pick, paged, preferred_element_type=jnp.float32).astype(
            jnp.bfloat16
        )


def place_near(tokens, head_count, cap, tp_size):
    pages, page_len = (tokens.shape[0] - 1) // 2 - 1, tokens.shape[1]
    return call(
        functools.partial(place_near_kernel, tp_size, head_count),
        (tokens,),
        [vmem()],
        out_specs=vmem(),
        out_shape=jax.ShapeDtypeStruct((2, cap, page_len * HD), jnp.bfloat16),
        compiler_params=params(8),
        name="place_near",
    )


def settle_kernel(plan, *refs):
    count = len(plan)
    parts, arrived = refs[:count], refs[-1]
    key_ref, value_ref, done_ref = refs[-4:-1]
    head_count, cap = key_ref.shape[0], parts[0].shape[-2]
    me = lax.axis_index("tp")

    def copies_of(place):
        distance, _, other = plan[place]
        first = pl.multiple_of((me ^ distance) * cap, cap)
        copies = []
        for index, target in enumerate((key_ref, value_ref)):
            for head in range(head_count if other is None else 1):
                source = parts[place].at[index]
                if other is None:
                    source = source.at[head]
                else:
                    head = lax.rem(me + other, head_count)
                copies.append(
                    pltpu.make_async_copy(
                        source,
                        target.at[head, pl.ds(first, cap)],
                        arrived.at[place * 2 * head_count + len(copies)],
                    )
                )
        return copies

    def move(place, action):
        holders = plan[place][1]
        if holders is None:
            for copy in copies_of(place):
                action(copy)
            return
        holds = functools.reduce(lambda a, b: a | b, [me == holder for holder in holders])

        @pl.when(holds)
        def _():
            for copy in copies_of(place):
                action(copy)

    for place in range(count):
        move(place, lambda copy: copy.start())
    done_ref[...] = jnp.zeros_like(done_ref)
    for place in range(count):
        move(place, lambda copy: copy.wait())


def settle(parts, plan, head_count, slots, settled=(), follows=()):
    width = parts[0].shape[-1]
    shape = jax.ShapeDtypeStruct((head_count, slots, width), jnp.bfloat16)
    count = len(parts)
    return call(
        functools.partial(settle_kernel, plan),
        (*parts, *settled),
        [vmem()] * count + [hbm()] * len(settled),
        follows,
        out_specs=(hbm(), hbm(), vmem()),
        out_shape=(shape, shape, jax.ShapeDtypeStruct((8, LANES), jnp.float32)),
        input_output_aliases={count: 0, count + 1: 1} if settled else {},
        scratch_shapes=[pltpu.SemaphoreType.DMA((2 * count * head_count,))],
        compiler_params=params(6),
        name="settle",
    )


def slot_rows_kernel(
    cap, pages, first_lane, page_len, steps, bounds_ref, own_ref, far_ref, out_ref
):
    head_count, slots = out_ref.shape
    tp_size = slots // cap
    me = lax.axis_index("tp")
    earlier = earlier_pages(pages)
    ends = bounds_ref[1:2, :]
    ids = lax.broadcasted_iota(jnp.int32, (pages, ends.shape[1]), 0)
    row = lax.broadcasted_iota(jnp.int32, (cap, pages), 0)
    ones = jnp.ones((8, ends.shape[1]), jnp.bfloat16)
    lines = [[] for _ in range(head_count)]
    for distance in range(tp_size):
        block = me ^ distance
        marks = lax.dot_general(
            ones,
            (ends <= block * pages + ids).astype(jnp.bfloat16),
            (((1,), (1,)), ((), ())),
            preferred_element_type=jnp.float32,
        )
        marks = marks / steps + 1
        source = own_ref if distance < 2 else far_ref
        line = (distance % 2) * page_len
        notes = source[line : line + page_len, -LANES:].astype(jnp.float32)
        notes = pltpu.roll(notes, LANES - first_lane, axis=1)
        for head in range(head_count):
            owner = notes[head : head + 1, :pages].astype(jnp.int32)
            rank = rank_pages(owner, earlier, round_up(tp_size, 8))
            pick = ((owner == me) & (rank == row)).astype(jnp.bfloat16)
            found = lax.dot_general(
                marks.astype(jnp.bfloat16),
                pick,
                (((1,), (1,)), ((), ())),
                preferred_element_type=jnp.float32,
            )
            found = jnp.concatenate([found, jnp.zeros((8, LANES - cap), jnp.float32)], axis=1)
            lines[head].append(pltpu.roll(found, block * cap, axis=1)[:1])
    for head in range(head_count):
        total = lines[head][0]
        for line in lines[head][1:]:
            total = total + line
        out_ref[head : head + 1, :] = total[:, :slots].astype(jnp.int32) - 1


def slot_rows_near(bounds, own, far, pages, first_lane, page_len, cap, shape, steps, follows):
    return call(
        functools.partial(slot_rows_kernel, cap, pages, first_lane, page_len, steps),
        (bounds, own, far),
        [vmem()] * 3,
        follows,
        out_specs=vmem(),
        out_shape=jax.ShapeDtypeStruct(shape, jnp.int32),
        compiler_params=params(2),
        name="slot_rows",
    )


def slot_rows_gathered(page_owner, page_counts, cap):
    owners = lax.all_gather(page_owner, "tp", axis=0, tiled=False)
    tp_size, head_count, pages_here = owners.shape
    rows = jnp.arange(page_counts.shape[0], dtype=jnp.int32)
    row_ends = jnp.sum(jnp.where(rows[None, :] <= rows[:, None], page_counts[None, :], 0), axis=1)
    ids = jnp.arange(pages_here, dtype=jnp.int32)
    same = (owners[..., :, None] == owners[..., None, :]) & (ids[:, None] < ids[None, :])
    rank = jnp.sum(same.astype(jnp.int32), axis=2)
    blocks = jnp.arange(tp_size, dtype=jnp.int32)
    page_ids = blocks[:, None] * pages_here + ids
    page_row = jnp.sum((row_ends <= page_ids[..., None]).astype(jnp.int32), axis=-1)
    slot = jnp.where(owners == lax.axis_index("tp"), blocks[:, None, None] * cap + rank, -1)
    slot_ids = jnp.arange(tp_size * cap, dtype=jnp.int32)
    marks = jnp.where(slot[..., None] == slot_ids, page_row[:, None, :, None] + 1, 0)
    return jnp.sum(marks, axis=(0, 2)) - 1


def gather_tokens_kernel(other, with_queries, handing, *refs):
    key_ref, value_ref, fresh_key_ref, fresh_value_ref, owner_ref = refs[:5]
    arrived = refs[-1]
    if with_queries:
        all_query_ref, count_ref, out_ref, query_ref, bounds_ref = refs[5:10]
        held, fresh, owners, queries, counts = refs[10:15]
    elif handing:
        out_ref, hand_ref, held, fresh, owners = refs[5:10]
    else:
        out_ref, held, fresh, owners = refs[5:9]
    pages, page_len = key_ref.shape[1], out_ref.shape[1]
    head_count, own_rows, steps = key_ref.shape[0], fresh.shape[1], fresh.shape[2]
    me = lax.axis_index("tp")
    head = lax.rem(me + other, head_count)
    pairs = [
        (owner_ref, owners),
        (fresh_key_ref, fresh.at[0]),
        (fresh_value_ref, fresh.at[1]),
    ]
    if handing:
        pairs += [(key_ref, held.at[0]), (value_ref, held.at[1])]
    else:
        pairs += [(key_ref.at[head], held.at[0, 0]), (value_ref.at[head], held.at[1, 0])]
    if with_queries:
        width = query_ref.shape[1]
        columns = pl.ds(pl.multiple_of(head * width, LANES), width)
        pairs += [(count_ref, counts), (all_query_ref.at[:, :, columns], queries)]
    copies = [
        pltpu.make_async_copy(source, target, arrived.at[i])
        for i, (source, target) in enumerate(pairs)
    ]
    for copy in copies:
        copy.start()
    copies[0].wait()
    out_ref[2 * pages + 2] = owner_page(owners[...], page_len).astype(jnp.bfloat16)
    if handing:
        cap = hand_ref.shape[2]
        picks = slot_picks(owners, me, [handing], cap, lax.axis_size("tp"))
    for i in range(2):
        copies[1 + i].wait()
        new = fresh[i]
        part = new[:, :, :HD]
        for which in range(1, head_count):
            part = jnp.where(head == which, new[:, :, which * HD : (which + 1) * HD], part)
        lines = part.reshape(own_rows * steps, HD)
        if own_rows * steps < page_len:
            spare = jnp.zeros((page_len - own_rows * steps, HD), jnp.bfloat16)
            lines = jnp.concatenate([lines, spare])
        out_ref[pages + i * (pages + 1)] = lines
    for i in range(2):
        copies[3 + i].wait()
        first = i * (pages + 1)
        paged = held[i, head] if handing else held[i, 0]
        out_ref[first : first + pages] = paged.reshape(pages, page_len, HD)
    if handing:
        for i in range(2):
            for which in range(head_count):
                place_rows(held.at[i, which], picks[which], [hand_ref.at[i, which]])
    if with_queries:
        copies[5].wait()
        row_lines = query_ref.shape[0]
        row = lax.broadcasted_iota(jnp.int32, (1, row_lines), 1) // steps
        starts = jnp.zeros((1, row_lines), jnp.int32)
        ends = jnp.zeros((1, row_lines), jnp.int32)
        for r in range(counts.shape[0]):
            starts = starts + jnp.where(row > r, counts[r], 0)
            ends = ends + jnp.where(row >= r, counts[r], 0)
        line = lax.broadcasted_iota(jnp.int32, (8, row_lines), 0)
        bounds_ref[...] = jnp.where(line == 0, starts, ends)
        copies[6].wait()
        query_ref[...] = queries[...].reshape(row_lines, query_ref.shape[1])


def owner_page(owners, lines):
    head_count, pages = owners.shape
    page = jnp.concatenate(
        [owners.astype(jnp.float32), jnp.zeros((head_count, LANES - pages), jnp.float32)], axis=1
    )
    return jnp.concatenate([page, jnp.zeros((lines - head_count, LANES), jnp.float32)])


def gather_tokens(
    other, caches, fresh, owner, queries=None, counts=None, handing=0, cap=0, follows=()
):
    head_count, pages, width = caches[0].shape
    page_len = width // HD
    with_queries = queries is not None
    operands = [*caches, *fresh, owner]
    out_shape = [jax.ShapeDtypeStruct((2 * pages + 3, page_len, HD), jnp.bfloat16)]
    scratch = [
        pltpu.VMEM((2, head_count if handing else 1, pages, width), jnp.bfloat16),
        pltpu.VMEM((2,) + fresh[0].shape, jnp.bfloat16),
        pltpu.VMEM(owner.shape, jnp.int32),
    ]
    if handing:
        out_shape.append(jax.ShapeDtypeStruct((2, head_count, cap, width), jnp.bfloat16))
    if with_queries:
        operands += [queries, counts]
        rows, steps, query_width = queries.shape
        query_width = query_width // head_count
        out_shape += [
            jax.ShapeDtypeStruct((rows * steps, query_width), jnp.bfloat16),
            jax.ShapeDtypeStruct((8, rows * steps), jnp.int32),
        ]
        scratch += [
            pltpu.VMEM((rows, steps, query_width), jnp.bfloat16),
            pltpu.SMEM(counts.shape, jnp.int32),
        ]
    return call(
        functools.partial(gather_tokens_kernel, other, with_queries, handing),
        in_hbm(*operands),
        [hbm()] * len(operands),
        follows,
        out_specs=[vmem()] * len(out_shape),
        out_shape=out_shape,
        scratch_shapes=scratch + [pltpu.SemaphoreType.DMA((len(operands),))],
        compiler_params=params(6),
        name="gather_tokens",
    )


def membership(bounds, owner, pages, own_lines, member_lines, row_lines, steps):
    query_line = lax.broadcasted_iota(jnp.int32, (1, row_lines), 1)
    starts, ends = bounds[0:1, :], bounds[1:2, :]
    page_lines = pages * steps
    line = lax.broadcasted_iota(jnp.int32, (member_lines, row_lines), 0)
    page = owner * pages + line // steps
    in_row = (starts <= page) & (page < ends) & (line % steps == query_line % steps)
    own_line = line - page_lines
    is_own = (
        (own_line >= 0) & (own_line < own_lines) & (query_line == owner * own_lines + own_line)
    )
    member = (((line < page_lines) & in_row) | is_own).astype(jnp.float32)
    return member, jnp.transpose(member)


def attend_kernel(steps, own_lines, neighbour, has_earlier, last, *refs):
    bounds_ref, query_ref, tokens_ref = refs[:3]
    refs = refs[3:]
    if has_earlier:
        early_max_ref, early_total_ref, early_numer_ref = refs[:3]
        refs = refs[3:]
    if last:
        if has_earlier:
            own_tokens_ref, refs = refs[0], refs[1:]
        payload_ref, refs = refs[0], refs[1:]
    else:
        out_max_ref, out_total_ref, out_numer_ref = refs[:3]
        refs = refs[3:]
    chosen, numers, high, low = refs

    row_lines, query_width = query_ref.shape
    group = query_width // HD
    held, page_len = (tokens_ref.shape[0] - 1) // 2, tokens_ref.shape[1]
    pages = held - 1
    page_lines = pages * steps
    used_lines = page_lines + page_len
    member_lines = chosen.shape[0]
    scale = HD ** (-0.5)
    lane = lax.broadcasted_iota(jnp.int32, (1, LANES), 1)
    me = lax.axis_index("tp")
    member, member_t = membership(
        bounds_ref[...], me ^ neighbour, pages, own_lines, member_lines, row_lines, steps
    )
    is_member = member_t > 0
    chosen[...] = jnp.dot(
        member.astype(jnp.bfloat16), query_ref[...], preferred_element_type=jnp.float32
    ).astype(jnp.bfloat16)

    maxima, totals = [], []

    def one_block(first_line, lines, keys, values, mask):
        queries = jnp.concatenate(
            [
                chosen[first_line : first_line + lines, g * HD : (g + 1) * HD]
                for g in range(group)
            ],
            axis=0,
        )
        scores = (
            lax.dot_general(
                queries, keys, (((1,), (1,)), ((), ())), preferred_element_type=jnp.float32
            )
            * scale
        )
        scores = jnp.where(mask, scores, NEGATIVE)
        largest = jnp.max(scores, axis=1, keepdims=True)
        weights = jnp.exp(scores - largest).astype(jnp.bfloat16)
        total = jnp.sum(weights.astype(jnp.float32), axis=1, keepdims=True)
        numer = jnp.dot(weights, values, preferred_element_type=jnp.float32)
        block_max = jnp.zeros((lines, LANES), jnp.float32)
        block_total = jnp.zeros((lines, LANES), jnp.float32)
        for g in range(group):
            part = slice(g * lines, (g + 1) * lines)
            block_max = jnp.where(lane == g, largest[part], block_max)
            block_total = jnp.where(lane == g, total[part], block_total)
            numers[first_line : first_line + lines, g * HD : (g + 1) * HD] = numer[part]
        maxima.append(block_max)
        totals.append(block_total)

    batch = min(pages, max(1, 128 // page_len))
    lines = batch * steps
    line = lax.broadcasted_iota(jnp.int32, (group * lines, batch * page_len), 0)
    token = lax.broadcasted_iota(jnp.int32, (group * lines, batch * page_len), 1)
    mask = (line % lines) // steps == token // page_len
    for first in range(0, pages, batch):
        one_block(
            first * steps,
            lines,
            tokens_ref[first : first + batch].reshape(batch * page_len, HD),
            tokens_ref[held + first : held + first + batch].reshape(batch * page_len, HD),
            mask,
        )
    line = lax.broadcasted_iota(jnp.int32, (group * page_len, page_len), 0) % page_len
    token = lax.broadcasted_iota(jnp.int32, (group * page_len, page_len), 1)
    mask = (line // steps == token // steps) & (token % steps <= line % steps)
    one_block(page_lines, page_len, tokens_ref[pages], tokens_ref[held + pages], mask)

    spare = member_lines - used_lines
    if spare:
        maxima.append(jnp.zeros((spare, LANES), jnp.float32))
        totals.append(jnp.zeros((spare, LANES), jnp.float32))
    line_max = jnp.concatenate(maxima, axis=0)
    line_total = jnp.concatenate(totals, axis=0)

    line_max_t = jnp.transpose(line_max)
    row_max = jnp.full((row_lines, LANES), NEGATIVE, jnp.float32)
    for g in range(group):
        best = jnp.max(
            jnp.where(is_member, line_max_t[g : g + 1, :], NEGATIVE), axis=1, keepdims=True
        )
        row_max = jnp.where(lane == g, best, row_max)
    spread = jnp.dot(
        member,
        row_max,
        precision=HIGHEST,
        preferred_element_type=jnp.float32,
    )
    factor = jnp.exp(jnp.minimum(line_max - spread, 0.0))
    row_total = jnp.dot(
        member_t,
        line_total * factor,
        precision=HIGHEST,
        preferred_element_type=jnp.float32,
    )
    turned = member_t.astype(jnp.bfloat16)
    if spare:
        high[used_lines:, :] = jnp.zeros((spare, query_width), jnp.bfloat16)
        low[used_lines:, :] = jnp.zeros((spare, query_width), jnp.bfloat16)
    for g in range(group):
        columns = slice(g * HD, (g + 1) * HD)
        scaled = numers[:, columns] * factor[:used_lines, g : g + 1]
        rounded = scaled.astype(jnp.bfloat16)
        high[:used_lines, columns] = rounded
        low[:used_lines, columns] = (scaled - rounded.astype(jnp.float32)).astype(jnp.bfloat16)

    if has_earlier:
        early_max = early_max_ref[...]
        largest = jnp.maximum(row_max, early_max)
        scale_now = jnp.exp(row_max - largest)
        scale_early = jnp.exp(early_max - largest)
        row_total = row_total * scale_now + early_total_ref[...] * scale_early
        row_max = largest
    if last:
        present = row_total > 0
        inverse = jnp.where(present, 1.0 / jnp.where(present, row_total, 1.0), 0.0)
        log_sum = jnp.where(
            present & (lane < group),
            row_max + jnp.log(jnp.where(present, row_total, 1.0)),
            jnp.where(lane < group, NEGATIVE, 0.0),
        )
        if has_earlier:
            scale_now = scale_now * inverse
            scale_early = scale_early * inverse
        else:
            scale_now = inverse
        lanes = split_sums(log_sum, group)
        if has_earlier:
            lanes = lanes + owner_notes(
                own_tokens_ref[2 * held], tokens_ref[2 * held], row_lines, 3 * group
            )
        payload_ref[:, query_width:] = lanes.astype(jnp.bfloat16)
    for g in range(group):
        columns = slice(g * HD, (g + 1) * HD)
        numer = jnp.dot(
            turned, high[:, columns], preferred_element_type=jnp.float32
        ) + jnp.dot(turned, low[:, columns], preferred_element_type=jnp.float32)
        if has_earlier:
            numer = (
                numer * scale_now[:, g : g + 1]
                + early_numer_ref[:, columns] * scale_early[:, g : g + 1]
            )
        elif last:
            numer = numer * scale_now[:, g : g + 1]
        if last:
            payload_ref[:, columns] = numer.astype(jnp.bfloat16)
        else:
            out_numer_ref[:, columns] = numer
    if not last:
        out_max_ref[...] = row_max
        out_total_ref[...] = row_total


def split_sums(value, group):
    first = value.astype(jnp.bfloat16).astype(jnp.float32)
    rest = value - first
    second = rest.astype(jnp.bfloat16).astype(jnp.float32)
    third = rest - second
    return first + pltpu.roll(second, group, axis=1) + pltpu.roll(third, 2 * group, axis=1)


def owner_notes(own, near_page, row_lines, first_lane):
    lines = near_page.shape[0]
    notes = jnp.concatenate(
        [
            own.astype(jnp.float32),
            near_page.astype(jnp.float32),
            jnp.zeros((row_lines - 2 * lines, LANES), jnp.float32),
        ]
    )
    return pltpu.roll(notes, first_lane, axis=1)


def join_sums(parts, group):
    parts = parts.astype(jnp.float32)
    return (
        parts
        + pltpu.roll(parts, LANES - group, axis=1)
        + pltpu.roll(parts, LANES - 2 * group, axis=1)
    )


def attend(
    bounds, query, tokens, neighbour, own_lines, steps, earlier, own_tokens, last, follows=()
):
    row_lines, query_width = query.shape
    group = query_width // HD
    held, page_len = (tokens.shape[0] - 1) // 2, tokens.shape[1]
    used_lines = (held - 1) * steps + page_len
    member_lines = round_up(used_lines, LANES)
    stat = jax.ShapeDtypeStruct((row_lines, LANES), jnp.float32)
    if last:
        out_shape = (jax.ShapeDtypeStruct((row_lines, query_width + LANES), jnp.bfloat16),)
    else:
        out_shape = (stat, stat, jax.ShapeDtypeStruct((row_lines, query_width), jnp.float32))
    operands = (bounds, query, tokens, *earlier, *own_tokens)
    return call(
        functools.partial(
            attend_kernel, steps, own_lines, neighbour, bool(earlier), last
        ),
        operands,
        [vmem()] * len(operands),
        follows,
        out_specs=tuple(vmem() for _ in out_shape),
        out_shape=out_shape,
        scratch_shapes=[
            pltpu.VMEM((member_lines, query_width), jnp.bfloat16),
            pltpu.VMEM((used_lines, query_width), jnp.float32),
            pltpu.VMEM((member_lines, query_width), jnp.bfloat16),
            pltpu.VMEM((member_lines, query_width), jnp.bfloat16),
        ],
        compiler_params=params(12),
        name="attend",
    )


def combine_kernel(group, mine_ref, theirs_ref, *out_refs):
    sums = join_sums(mine_ref[:, -LANES:], group)
    their_sums = join_sums(theirs_ref[:, -LANES:], group)
    largest = jnp.maximum(sums, their_sums)
    weight = jnp.exp(sums - largest)
    their_weight = jnp.exp(their_sums - largest)
    inverse = 1.0 / (weight + their_weight)
    weight = weight * inverse
    their_weight = their_weight * inverse
    part = group // len(out_refs)
    for g in range(group):
        columns = slice(g * HD, (g + 1) * HD)
        place = g % part
        out_refs[g // part][:, place * HD : (place + 1) * HD] = (
            mine_ref[:, columns].astype(jnp.float32) * weight[:, g : g + 1]
            + theirs_ref[:, columns].astype(jnp.float32) * their_weight[:, g : g + 1]
        ).astype(jnp.bfloat16)


def combine(mine, theirs, chunks, follows=()):
    row_lines, width = mine.shape
    group = (width - LANES) // HD
    shape = jax.ShapeDtypeStruct((row_lines, group // chunks * HD), jnp.bfloat16)
    return call(
        functools.partial(combine_kernel, group),
        (mine, theirs),
        [vmem()] * 2,
        follows,
        out_specs=[vmem()] * chunks,
        out_shape=[shape] * chunks,
        compiler_params=params(4),
        name="combine",
    )


def block_row(own, chunk, chunks, head_count, depth):
    head = lax.rem(lax.axis_index("tp") + (0 if own else 1), head_count)
    return pl.multiple_of((head * chunks + chunk) * depth, depth)


def fetch_kernel(blocks, chunks, head_count, weight_ref, held_ref, done_ref, arrived):
    depth = held_ref.shape[0] // len(blocks)
    pieces = arrived.shape[0] // len(blocks)
    size = depth // pieces
    copies = []
    for place, (own, chunk) in enumerate(blocks):
        base = block_row(own, chunk, chunks, head_count, depth)
        for piece in range(pieces):
            copies.append(
                pltpu.make_async_copy(
                    weight_ref.at[pl.ds(pl.multiple_of(base + piece * size, size), size)],
                    held_ref.at[pl.ds(place * depth + piece * size, size)],
                    arrived.at[place * pieces + piece],
                )
            )
    for copy in copies:
        copy.start()
    done_ref[...] = jnp.zeros_like(done_ref)
    for copy in copies:
        copy.wait()


def fetch(weight, blocks, chunks, head_count, depth, follows):
    pieces = 4
    return call(
        functools.partial(fetch_kernel, blocks, chunks, head_count),
        in_hbm(weight),
        [hbm()],
        follows,
        out_specs=(vmem(), vmem()),
        out_shape=(
            pltpu.VMEM((len(blocks) * depth, weight.shape[1]), weight.dtype),
            jax.ShapeDtypeStruct((8, LANES), jnp.float32),
        ),
        scratch_shapes=[pltpu.SemaphoreType.DMA((len(blocks) * pieces,))],
        compiler_params=params(1),
        name="fetch",
    )


def project_kernel(parts, has_total, chunk_lines, first, offsets, chunks, head_count, *refs):
    input_refs, weight_ref, refs = refs[:parts], refs[parts], refs[parts + 1 :]
    streamed = offsets is None
    if streamed:
        held, arrived = refs[-2:]
        refs = refs[:-2]
    outs = refs[1:] if has_total else refs
    depth, width = input_refs[0].shape[1], outs[0].shape[-1]
    block = min(width, 512)
    count = width // block

    def piece(index):
        return pltpu.make_async_copy(
            weight_ref.at[
                pl.ds(block_row(True, 0, chunks, head_count, depth), depth),
                pl.ds(first + index * block, block),
            ],
            held.at[:, pl.ds(index * block, block)],
            arrived.at[index],
        )

    if streamed:
        for index in range(count):
            piece(index).start()
    for index in range(count):
        start = index * block
        columns = slice(first + start, first + start + block)
        product = refs[0][:, columns] if has_total else 0.0
        if streamed:
            piece(index).wait()
            product = product + jnp.dot(
                input_refs[0][...],
                held[:, start : start + block],
                preferred_element_type=jnp.float32,
            )
        else:
            for input_ref, offset in zip(input_refs, offsets):
                product = product + jnp.dot(
                    input_ref[...],
                    weight_ref[offset * depth : (offset + 1) * depth, columns],
                    preferred_element_type=jnp.float32,
                )
        if chunk_lines is None:
            outs[0][:, start : start + block] = product
            continue
        core = lax.rem(lax.axis_index("kv"), 2)
        keep_ref, send_ref = outs
        for pair in range(keep_ref.shape[0]):
            even = product[2 * pair * chunk_lines : (2 * pair + 1) * chunk_lines]
            odd = product[(2 * pair + 1) * chunk_lines : (2 * pair + 2) * chunk_lines]
            keep_ref[pair, :, start : start + block] = jnp.where(core == 0, even, odd)
            send_ref[pair, :, start : start + block] = jnp.where(core == 0, odd, even).astype(
                send_ref.dtype
            )


def project(inputs, weight, offsets, chunks, head_count, total, columns, chunk_lines, follows=()):
    row_lines, depth = inputs[0].shape
    first, width = columns
    in_specs = [vmem()] * len(inputs) + [hbm() if offsets is None else vmem()]
    operands = [*inputs, *(in_hbm(weight) if offsets is None else [weight])]
    if total is not None:
        in_specs.append(vmem())
        operands.append(total)
    if chunk_lines is None:
        out_shape = jax.ShapeDtypeStruct((row_lines, width), jnp.float32)
        out_specs = vmem()
    else:
        pairs = row_lines // (2 * chunk_lines)
        shape = (pairs, chunk_lines, width)
        out_shape = (
            jax.ShapeDtypeStruct(shape, jnp.float32),
            jax.ShapeDtypeStruct(shape, jnp.bfloat16),
        )
        out_specs = (vmem(), vmem())
    scratch = []
    if offsets is None:
        scratch = [
            pltpu.VMEM((depth, width), weight.dtype),
            pltpu.SemaphoreType.DMA((max(1, width // 512),)),
        ]
    return call(
        functools.partial(
            project_kernel,
            len(inputs),
            total is not None,
            chunk_lines,
            first,
            offsets,
            chunks,
            head_count,
        ),
        operands,
        in_specs,
        follows,
        out_specs=out_specs,
        out_shape=out_shape,
        scratch_shapes=scratch,
        compiler_params=params(16 if offsets is None else 8),
        name="project",
    )


def add_core_kernel(keep_ref, got_ref, own_ref, *send_refs):
    half = lax.axis_index("kv") // 2
    own_ref[...] = keep_ref[half] + got_ref[half].astype(jnp.float32)
    for step, send_ref in enumerate(send_refs, 1):
        part = keep_ref[half ^ step] + got_ref[half ^ step].astype(jnp.float32)
        send_ref[...] = part.astype(send_ref.dtype)


def sum_heads(keep, send, kv_size):
    got = lax.ppermute(send, "kv", flip(kv_size, 1))
    shape = keep.shape[1:]
    own, *sends = call(
        add_core_kernel,
        (keep, got),
        [vmem(), vmem()],
        out_specs=[vmem()] * (kv_size // 2),
        out_shape=[jax.ShapeDtypeStruct(shape, jnp.float32)]
        + [jax.ShapeDtypeStruct(shape, jnp.bfloat16)] * (kv_size // 2 - 1),
        compiler_params=params(4),
        name="add_core",
    )
    return [own] + [
        lax.ppermute(part, "kv", flip(kv_size, 2 * step)) for step, part in enumerate(sends, 1)
    ]


def finish_kernel(pieces, *refs):
    parts, out_ref, done_ref = refs[:-2], refs[-2], refs[-1]
    done_ref[...] = jnp.zeros_like(done_ref)
    each = len(parts) // pieces
    steps, width = out_ref.shape[1], out_ref.shape[2] // pieces
    for piece in range(pieces):
        total = parts[piece * each][...]
        for part in parts[piece * each + 1 : (piece + 1) * each]:
            total = total + part[...].astype(jnp.float32)
        out_ref[:, :, piece * width : (piece + 1) * width] = total.astype(jnp.bfloat16).reshape(
            -1, steps, width
        )


def finish(results, steps):
    lines, width = results[0][0].shape
    parts = [part for pieces in results for part in pieces]
    return call(
        functools.partial(finish_kernel, len(results)),
        parts,
        [vmem()] * len(parts),
        out_specs=(vmem(), vmem()),
        out_shape=(
            jax.ShapeDtypeStruct((lines // steps, steps, width * len(results)), jnp.bfloat16),
            jax.ShapeDtypeStruct((8, LANES), jnp.float32),
        ),
        compiler_params=params(4),
        name="finish",
    )


def body(
    queries, fresh_keys, fresh_values, cache_keys, cache_values, page_counts, page_owner, out_weight
):
    tp_size, kv_size = lax.axis_size("tp"), lax.axis_size("kv")
    head_count, pages_here, page_width = cache_keys.shape
    row_count, step_count, query_width = queries.shape
    own_lines = fresh_keys.shape[0] * step_count
    page_len = page_width // HD
    row_lines = row_count * step_count
    head_width = query_width // head_count
    group = head_width // HD
    cap = max(2, (2 * pages_here + tp_size - 1) // tp_size)
    out_width = out_weight.shape[1]
    chunk_lines = row_lines // kv_size
    caches = (cache_keys, cache_values)
    fresh = (fresh_keys, fresh_values)

    paired = head_count == 2 and tp_size == 4 and group % 2 == 0 and cap % 16 == 0
    paired = paired and 3 * group + pages_here <= LANES and 2 * page_len <= row_lines
    chunks = 2 if paired else 1
    part = head_width // chunks
    everything = (0, out_width)

    if paired:
        tokens, send_last = gather_tokens(1, caches, fresh, page_owner, handing=3, cap=cap)
        near_tokens = lax.ppermute(tokens, "tp", flip(tp_size, 1))
        got_inner = lax.ppermute(send_last, "tp", [(1, 2), (2, 1)])
        own_tokens, query, bounds = gather_tokens(
            0, caches, fresh, page_owner, queries, page_counts, follows=(send_last,)
        )
        shapes = (own_lines, step_count)
        earlier = attend(bounds, query, own_tokens, 0, *shapes, (), (), False)
        jobs = ((2, True), (1, False), (0, True))
        send_far, send_near, kept = place_pages(
            page_owner, caches, jobs, cap, tp_size, False, (earlier[0],)
        )
        (payload,) = attend(
            bounds, query, near_tokens, 1, *shapes, earlier, (own_tokens,), True, (kept,)
        )
        payload = tie(payload, got_inner)
        theirs = lax.ppermute(payload, "tp", flip(tp_size, 2))
        blocks = ((True, 1), (False, 0), (False, 1))
        held, held_done = fetch(out_weight, blocks, chunks, head_count, part, (payload,))
        got_near = lax.ppermute(tie(send_near, held_done), "tp", flip(tp_size, 1))
        near_pages = place_near(near_tokens, head_count, cap, tp_size)
        own_parts = combine(payload, theirs, chunks, (got_near,))
        near_parts = [lax.ppermute(p, "tp", flip(tp_size, 1)) for p in own_parts]
        got_far = lax.ppermute(tie(send_far, own_parts[0]), "tp", flip(tp_size, 2))
        got_outer = lax.ppermute(tie(send_last, own_parts[0]), "tp", [(0, 3), (3, 0)])
        total = project(
            own_parts[:1], out_weight, None, chunks, head_count, None, everything, None
        )
        plan = ((0, None, None), (1, None, 0), (1, None, 1), (3, (1, 2), None))
        *settled, settled_done = settle(
            [kept, near_pages, got_near, got_inner], plan, head_count, tp_size * cap, (), (total,)
        )
        total = project(
            [own_parts[1], near_parts[0]],
            held,
            (0, 1),
            chunks,
            head_count,
            total,
            everything,
            None,
            (settled_done,),
        )
        results = []
        for first in (0, out_width // 2):
            columns = (first, out_width // 2)
            keep, send = project(
                [near_parts[1]], held, (2,), chunks, head_count, total, columns, chunk_lines
            )
            results.append(sum_heads(keep, send, kv_size))
        attention_out, finished = finish(results, step_count)
        slot_rows = slot_rows_near(
            bounds,
            payload,
            theirs,
            pages_here,
            3 * group,
            page_len,
            cap,
            (head_count, tp_size * cap),
            step_count,
            (results[1][0],),
        )
        plan = ((2, None, None), (3, (0, 3), None))
        slot_keys, slot_values, _ = settle(
            [got_far, got_outer], plan, head_count, tp_size * cap, settled, (finished,)
        )
        return (attention_out, slot_keys, slot_values, slot_rows)

    def hand_over(cache):
        jobs = tuple((d, True) for d in range(tp_size))
        sent = place_pages(page_owner, (cache,), jobs, cap, tp_size, True)
        got = lax.all_to_all(
            jnp.concatenate(sent), "tp", split_axis=0, concat_axis=0, tiled=True
        )
        return got.transpose(1, 0, 2, 3).reshape(head_count, tp_size * cap, page_width)

    slot_keys, slot_values = hand_over(cache_keys), hand_over(cache_values)
    slot_rows = slot_rows_gathered(page_owner, page_counts, cap)
    attended = []
    for head in range(head_count):
        cut = slice(head, head + 1)
        lanes = slice(head * HD, (head + 1) * HD)
        tokens, query, bounds = gather_tokens(
            0,
            [cache[cut] for cache in caches],
            [new[:, :, lanes] for new in fresh],
            page_owner[cut],
            queries[:, :, head * head_width : (head + 1) * head_width],
            page_counts,
        )
        (payload,) = attend(
            bounds, query, tokens, 0, own_lines, step_count, (), (), True
        )
        raw = payload[:, part:].astype(jnp.float32)
        sums = raw[:, :group] + raw[:, group : 2 * group] + raw[:, 2 * group : 3 * group]
        weight = jnp.exp(sums - lax.pmax(sums, "tp"))
        numer = payload[:, :part].astype(jnp.float32).reshape(row_lines, group, HD)
        numer = lax.psum(numer * weight[..., None], "tp")
        joined = numer / lax.psum(weight, "tp")[..., None]
        attended.append(joined.reshape(row_lines, head_width).astype(jnp.bfloat16))
    keep, send = project(
        [jnp.concatenate(attended, axis=1)], out_weight, None, 1, 1, None, everything, chunk_lines
    )
    attention_out, _ = finish([sum_heads(keep, send, kv_size)], step_count)
    return (attention_out, slot_keys, slot_values, slot_rows)


def solution(mesh):
    return jax.shard_map(
        body,
        mesh=mesh,
        in_specs=(
            P("grp", None, "kv"),
            P(("grp", "tp"), None, "kv"),
            P(("grp", "tp"), None, "kv"),
            P(("grp", "kv"), "tp", None),
            P(("grp", "kv"), "tp", None),
            P("grp"),
            P(("grp", "kv"), "tp"),
            P("kv", "tp"),
        ),
        out_specs=(
            P(("grp", "kv"), None, "tp"),
            P(("grp", "kv"), "tp", None),
            P(("grp", "kv"), "tp", None),
            P(("grp", "kv"), "tp"),
        ),
        check_vma=False,
    )
```

```python
import functools

import jax
import jax.numpy as jnp
from jax import lax
from jax.experimental import pallas as pl
from jax.experimental.pallas import tpu as pltpu
from jax.sharding import PartitionSpec as P

HD = 128
LANES = 128
NEGATIVE = -1e30
HIGHEST = lax.Precision.HIGHEST
MIB = 1024 * 1024


def round_up(value, step):
    return -(-value // step) * step


def flip(size, bit):
    return [(i, i ^ bit) for i in range(size)]


def params(mib):
    return pltpu.CompilerParams(vmem_limit_bytes=mib * MIB)


def in_hbm(*arrays):
    return [pltpu.with_memory_space_constraint(array, pltpu.HBM) for array in arrays]


def vmem():
    return pl.BlockSpec(memory_space=pltpu.VMEM)


def hbm():
    return pl.BlockSpec(memory_space=pltpu.HBM)


def anywhere():
    return pl.BlockSpec(memory_space=pl.ANY)


def call(kernel, operands, in_specs, follows=(), flops=0, **rest):
    count, extra = len(operands), len(follows)

    def without_extra(*refs):
        kernel(*refs[:count], *refs[count + extra :])

    return pl.pallas_call(
        without_extra,
        in_specs=list(in_specs) + [anywhere()] * extra,
        cost_estimate=pl.CostEstimate(flops=flops, bytes_accessed=0, transcendentals=0),
        **rest,
    )(*operands, *follows)


def tie(value, *follows):
    return call(
        lambda value_ref, out_ref: None,
        (value,),
        [anywhere()],
        follows,
        out_specs=anywhere(),
        out_shape=jax.ShapeDtypeStruct(value.shape, value.dtype),
        input_output_aliases={0: 0},
        compiler_params=params(1),
        name="tie",
    )


def earlier_pages(page_count):
    first = lax.broadcasted_iota(jnp.int32, (page_count, page_count), 0)
    second = lax.broadcasted_iota(jnp.int32, (page_count, page_count), 1)
    return (first < second).astype(jnp.bfloat16)


def rank_pages(away, earlier, dest_rows):
    ways = lax.broadcasted_iota(jnp.int32, (dest_rows, away.shape[1]), 0)
    listed = (ways == away).astype(jnp.float32)
    before = jnp.dot(listed.astype(jnp.bfloat16), earlier, preferred_element_type=jnp.float32)
    return jnp.sum(before * listed, axis=0, keepdims=True).astype(jnp.int32)


def slot_picks(owners, me, distances, cap, tp_size):
    head_count, page_count = owners.shape
    earlier = earlier_pages(page_count)
    row = lax.broadcasted_iota(jnp.int32, (cap, page_count), 0)
    picks = []
    for head in range(head_count):
        away = owners[head : head + 1, :] ^ me
        rank = rank_pages(away, earlier, round_up(tp_size, 8))
        picks.append([((away == d) & (rank == row)).astype(jnp.float32) for d in distances])
    return picks


def place_rows(pages_ref, pick, targets):
    width, cap = pages_ref.shape[1], pick[0].shape[0]
    step = min(width, 1024)
    for start in range(0, width, step):
        columns = slice(start, start + step)
        placed = jnp.dot(
            jnp.concatenate(pick).astype(jnp.bfloat16),
            pages_ref[:, columns],
            preferred_element_type=jnp.float32,
        ).astype(jnp.bfloat16)
        for which, target in enumerate(targets):
            target[:, columns] = placed[which * cap : (which + 1) * cap]


def place_kernel(cap, jobs, by_index, tp_size, owner_ref, *refs):
    count = (len(refs) - 2 - len(jobs)) // 2
    sources, targets = refs[:count], refs[count : count + len(jobs)]
    held, owners, arrived = refs[count + len(jobs) : -2], refs[-2], refs[-1]
    head_count = sources[0].shape[0]
    copies = [
        pltpu.make_async_copy(source, target, arrived.at[i])
        for i, (source, target) in enumerate(zip((owner_ref, *sources), (owners, *held)))
    ]
    for copy in copies:
        copy.start()
    copies[0].wait()
    me = 0 if by_index else lax.axis_index("tp")
    own_head = lax.rem(me, head_count)
    picks = slot_picks(owners, me, [d for d, _ in jobs], cap, tp_size)

    def place(index, head, pick, target_of):
        place_rows(held[index].at[head], pick, target_of)

    shared = [i for i, (_, every) in enumerate(jobs) if every]
    single = [i for i, (_, every) in enumerate(jobs) if not every]
    for index in range(count):
        copies[index + 1].wait()
        for head in range(head_count):
            if shared:
                pick = [picks[head][i] for i in shared]
                place(index, head, pick, [targets[i].at[index, head] for i in shared])
        if single:
            pick = []
            for i in single:
                chosen = picks[0][i]
                for head in range(1, head_count):
                    chosen = jnp.where(own_head == head, picks[head][i], chosen)
                pick.append(chosen)
            place(index, own_head, pick, [targets[i].at[index] for i in single])


def place_pages(page_owner, caches, jobs, cap, tp_size, by_index, follows=()):
    head_count, page_count, width = caches[0].shape
    return call(
        functools.partial(place_kernel, cap, jobs, by_index, tp_size),
        in_hbm(page_owner, *caches),
        [hbm()] * (1 + len(caches)),
        follows,
        out_specs=tuple(vmem() for _ in jobs),
        out_shape=tuple(
            jax.ShapeDtypeStruct(
                (len(caches),) + ((head_count,) if every else ()) + (cap, width), jnp.bfloat16
            )
            for _, every in jobs
        ),
        scratch_shapes=[pltpu.VMEM(cache.shape, cache.dtype) for cache in caches]
        + [
            pltpu.VMEM(page_owner.shape, jnp.int32),
            pltpu.SemaphoreType.DMA((1 + len(caches),)),
        ],
        compiler_params=params(8),
        name="place_pages",
    )


def place_near_kernel(tp_size, head_count, keys_ref, values_ref, out_ref):
    cap, width = out_ref.shape[1:]
    pages, page_len = values_ref.shape[0] - 1, values_ref.shape[1]
    me = lax.axis_index("tp")
    head = lax.rem(me, head_count)
    lists = keys_ref[pages + 1].astype(jnp.float32)[:, :pages].astype(jnp.int32)
    owner = lists[0:1]
    for which in range(1, head_count):
        owner = jnp.where(head == which, lists[which : which + 1], owner)
    rank = rank_pages(owner, earlier_pages(pages), round_up(tp_size, 8))
    row = lax.broadcasted_iota(jnp.int32, (cap, pages), 0)
    pick = ((owner == me) & (rank == row)).astype(jnp.bfloat16)
    for index, source in enumerate((keys_ref, values_ref)):
        paged = source[:pages].reshape(pages, page_len * HD)
        out_ref[index] = jnp.dot(pick, paged, preferred_element_type=jnp.float32).astype(
            jnp.bfloat16
        )


def place_near(keys, values, head_count, cap, tp_size):
    page_len = keys.shape[1]
    return call(
        functools.partial(place_near_kernel, tp_size, head_count),
        (keys, values),
        [vmem()] * 2,
        out_specs=vmem(),
        out_shape=jax.ShapeDtypeStruct((2, cap, page_len * HD), jnp.bfloat16),
        compiler_params=params(8),
        name="place_near",
    )


def settle_kernel(plan, *refs):
    count = len(plan)
    parts, arrived = refs[:count], refs[-1]
    key_ref, value_ref, done_ref = refs[-4:-1]
    head_count, cap = key_ref.shape[0], parts[0].shape[-2]
    me = lax.axis_index("tp")

    def copies_of(place):
        distance, _, other = plan[place]
        first = pl.multiple_of((me ^ distance) * cap, cap)
        copies = []
        for index, target in enumerate((key_ref, value_ref)):
            for head in range(head_count if other is None else 1):
                source = parts[place].at[index]
                if other is None:
                    source = source.at[head]
                else:
                    head = lax.rem(me + other, head_count)
                copies.append(
                    pltpu.make_async_copy(
                        source,
                        target.at[head, pl.ds(first, cap)],
                        arrived.at[place * 2 * head_count + len(copies)],
                    )
                )
        return copies

    def move(place, action):
        holders = plan[place][1]
        if holders is None:
            for copy in copies_of(place):
                action(copy)
            return
        holds = functools.reduce(lambda a, b: a | b, [me == holder for holder in holders])

        @pl.when(holds)
        def _():
            for copy in copies_of(place):
                action(copy)

    for place in range(count):
        move(place, lambda copy: copy.start())
    done_ref[...] = jnp.zeros_like(done_ref)
    for place in range(count):
        move(place, lambda copy: copy.wait())


def settle(parts, plan, head_count, slots, settled=(), follows=()):
    width = parts[0].shape[-1]
    shape = jax.ShapeDtypeStruct((head_count, slots, width), jnp.bfloat16)
    count = len(parts)
    return call(
        functools.partial(settle_kernel, plan),
        (*parts, *settled),
        [vmem()] * count + [hbm()] * len(settled),
        follows,
        out_specs=(hbm(), hbm(), vmem()),
        out_shape=(shape, shape, jax.ShapeDtypeStruct((8, LANES), jnp.float32)),
        input_output_aliases={count: 0, count + 1: 1} if settled else {},
        scratch_shapes=[pltpu.SemaphoreType.DMA((2 * count * head_count,))],
        compiler_params=params(6),
        name="settle",
    )


def slot_rows_kernel(
    cap, pages, first_lane, page_len, steps, bounds_ref, own_ref, far_ref, out_ref
):
    head_count, slots = out_ref.shape
    tp_size = slots // cap
    me = lax.axis_index("tp")
    earlier = earlier_pages(pages)
    ends = bounds_ref[1:2, :]
    ids = lax.broadcasted_iota(jnp.int32, (pages, ends.shape[1]), 0)
    row = lax.broadcasted_iota(jnp.int32, (cap, pages), 0)
    ones = jnp.ones((8, ends.shape[1]), jnp.bfloat16)
    lines = [[] for _ in range(head_count)]
    for distance in range(tp_size):
        block = me ^ distance
        marks = lax.dot_general(
            ones,
            (ends <= block * pages + ids).astype(jnp.bfloat16),
            (((1,), (1,)), ((), ())),
            preferred_element_type=jnp.float32,
        )
        marks = marks / steps + 1
        source = own_ref if distance < 2 else far_ref
        line = (distance % 2) * page_len
        notes = source[line : line + page_len, -LANES:].astype(jnp.float32)
        notes = pltpu.roll(notes, LANES - first_lane, axis=1)
        for head in range(head_count):
            owner = notes[head : head + 1, :pages].astype(jnp.int32)
            rank = rank_pages(owner, earlier, round_up(tp_size, 8))
            pick = ((owner == me) & (rank == row)).astype(jnp.bfloat16)
            found = lax.dot_general(
                marks.astype(jnp.bfloat16),
                pick,
                (((1,), (1,)), ((), ())),
                preferred_element_type=jnp.float32,
            )
            found = jnp.concatenate([found, jnp.zeros((8, LANES - cap), jnp.float32)], axis=1)
            lines[head].append(pltpu.roll(found, block * cap, axis=1)[:1])
    for head in range(head_count):
        total = lines[head][0]
        for line in lines[head][1:]:
            total = total + line
        out_ref[head : head + 1, :] = total[:, :slots].astype(jnp.int32) - 1


def slot_rows_near(bounds, own, far, pages, first_lane, page_len, cap, shape, steps, follows):
    return call(
        functools.partial(slot_rows_kernel, cap, pages, first_lane, page_len, steps),
        (bounds, own, far),
        [vmem()] * 3,
        follows,
        out_specs=vmem(),
        out_shape=jax.ShapeDtypeStruct(shape, jnp.int32),
        compiler_params=params(2),
        name="slot_rows",
    )


def slot_rows_gathered(page_owner, page_counts, cap):
    owners = lax.all_gather(page_owner, "tp", axis=0, tiled=False)
    tp_size, head_count, pages_here = owners.shape
    rows = jnp.arange(page_counts.shape[0], dtype=jnp.int32)
    row_ends = jnp.sum(jnp.where(rows[None, :] <= rows[:, None], page_counts[None, :], 0), axis=1)
    ids = jnp.arange(pages_here, dtype=jnp.int32)
    same = (owners[..., :, None] == owners[..., None, :]) & (ids[:, None] < ids[None, :])
    rank = jnp.sum(same.astype(jnp.int32), axis=2)
    blocks = jnp.arange(tp_size, dtype=jnp.int32)
    page_ids = blocks[:, None] * pages_here + ids
    page_row = jnp.sum((row_ends <= page_ids[..., None]).astype(jnp.int32), axis=-1)
    slot = jnp.where(owners == lax.axis_index("tp"), blocks[:, None, None] * cap + rank, -1)
    slot_ids = jnp.arange(tp_size * cap, dtype=jnp.int32)
    marks = jnp.where(slot[..., None] == slot_ids, page_row[:, None, :, None] + 1, 0)
    return jnp.sum(marks, axis=(0, 2)) - 1


def gather_tokens_kernel(other, with_queries, handing, *refs):
    key_ref, value_ref, fresh_key_ref, fresh_value_ref, owner_ref = refs[:5]
    arrived = refs[-1]
    if with_queries:
        all_query_ref, count_ref, *outs, query_ref, bounds_ref = refs[5:11]
        held, fresh, owners, queries, counts = refs[11:16]
    elif handing:
        *outs, hand_ref, held, fresh, owners = refs[5:11]
    else:
        *outs, held, fresh, owners = refs[5:10]
    pages, page_len = key_ref.shape[1], outs[0].shape[1]
    head_count, own_rows, steps = key_ref.shape[0], fresh.shape[1], fresh.shape[2]
    me = lax.axis_index("tp")
    head = lax.rem(me + other, head_count)
    pairs = [
        (owner_ref, owners),
        (fresh_key_ref, fresh.at[0]),
        (fresh_value_ref, fresh.at[1]),
    ]
    if handing:
        pairs += [(key_ref, held.at[0]), (value_ref, held.at[1])]
    else:
        pairs += [(key_ref.at[head], held.at[0, 0]), (value_ref.at[head], held.at[1, 0])]
    if with_queries:
        width = query_ref.shape[1]
        columns = pl.ds(pl.multiple_of(head * width, LANES), width)
        pairs += [(count_ref, counts), (all_query_ref.at[:, :, columns], queries)]
    copies = [
        pltpu.make_async_copy(source, target, arrived.at[i])
        for i, (source, target) in enumerate(pairs)
    ]
    for copy in copies:
        copy.start()
    copies[0].wait()
    outs[0][pages + 1] = owner_page(owners[...], page_len).astype(jnp.bfloat16)
    if handing:
        cap = hand_ref.shape[2]
        picks = slot_picks(owners, me, [handing], cap, lax.axis_size("tp"))
    for i in range(2):
        copies[1 + i].wait()
        new = fresh[i]
        part = new[:, :, :HD]
        for which in range(1, head_count):
            part = jnp.where(head == which, new[:, :, which * HD : (which + 1) * HD], part)
        lines = part.reshape(own_rows * steps, HD)
        if own_rows * steps < page_len:
            spare = jnp.zeros((page_len - own_rows * steps, HD), jnp.bfloat16)
            lines = jnp.concatenate([lines, spare])
        outs[i][pages] = lines
    for i in range(2):
        copies[3 + i].wait()
        paged = held[i, head] if handing else held[i, 0]
        outs[i][:pages] = paged.reshape(pages, page_len, HD)
    if handing:
        for i in range(2):
            for which in range(head_count):
                place_rows(held.at[i, which], picks[which], [hand_ref.at[i, which]])
    if with_queries:
        copies[5].wait()
        row_lines = query_ref.shape[0]
        row = lax.broadcasted_iota(jnp.int32, (1, row_lines), 1) // steps
        starts = jnp.zeros((1, row_lines), jnp.int32)
        ends = jnp.zeros((1, row_lines), jnp.int32)
        for r in range(counts.shape[0]):
            starts = starts + jnp.where(row > r, counts[r], 0)
            ends = ends + jnp.where(row >= r, counts[r], 0)
        line = lax.broadcasted_iota(jnp.int32, (8, row_lines), 0)
        bounds_ref[...] = jnp.where(line == 0, starts, ends)
        copies[6].wait()
        query_ref[...] = queries[...].reshape(row_lines, query_ref.shape[1])


def owner_page(owners, lines):
    head_count, pages = owners.shape
    page = jnp.concatenate(
        [owners.astype(jnp.float32), jnp.zeros((head_count, LANES - pages), jnp.float32)], axis=1
    )
    return jnp.concatenate([page, jnp.zeros((lines - head_count, LANES), jnp.float32)])


def gather_tokens(
    other, caches, fresh, owner, queries=None, counts=None, handing=0, cap=0, follows=()
):
    head_count, pages, width = caches[0].shape
    page_len = width // HD
    with_queries = queries is not None
    operands = [*caches, *fresh, owner]
    out_shape = [
        jax.ShapeDtypeStruct((pages + extra, page_len, HD), jnp.bfloat16) for extra in (2, 1)
    ]
    scratch = [
        pltpu.VMEM((2, head_count if handing else 1, pages, width), jnp.bfloat16),
        pltpu.VMEM((2,) + fresh[0].shape, jnp.bfloat16),
        pltpu.VMEM(owner.shape, jnp.int32),
    ]
    if handing:
        out_shape.append(jax.ShapeDtypeStruct((2, head_count, cap, width), jnp.bfloat16))
    if with_queries:
        operands += [queries, counts]
        rows, steps, query_width = queries.shape
        query_width = query_width // head_count
        out_shape += [
            jax.ShapeDtypeStruct((rows * steps, query_width), jnp.bfloat16),
            jax.ShapeDtypeStruct((8, rows * steps), jnp.int32),
        ]
        scratch += [
            pltpu.VMEM((rows, steps, query_width), jnp.bfloat16),
            pltpu.SMEM(counts.shape, jnp.int32),
        ]
    return call(
        functools.partial(gather_tokens_kernel, other, with_queries, handing),
        in_hbm(*operands),
        [hbm()] * len(operands),
        follows,
        out_specs=[vmem()] * len(out_shape),
        out_shape=out_shape,
        scratch_shapes=scratch + [pltpu.SemaphoreType.DMA((len(operands),))],
        compiler_params=params(6),
        name="gather_tokens",
    )


def membership(bounds, owner, pages, own_lines, member_lines, row_lines, steps):
    query_line = lax.broadcasted_iota(jnp.int32, (1, row_lines), 1)
    starts, ends = bounds[0:1, :], bounds[1:2, :]
    page_lines = pages * steps
    line = lax.broadcasted_iota(jnp.int32, (member_lines, row_lines), 0)
    page = owner * pages + line // steps
    in_row = (starts <= page) & (page < ends) & (line % steps == query_line % steps)
    own_line = line - page_lines
    is_own = (
        (own_line >= 0) & (own_line < own_lines) & (query_line == owner * own_lines + own_line)
    )
    member = (((line < page_lines) & in_row) | is_own).astype(jnp.float32)
    return member, jnp.transpose(member)


def prepare_kernel(steps, own_lines, page_len, neighbours, bounds_ref, query_ref, *refs):
    row_lines = query_ref.shape[0]
    for place, neighbour in enumerate(neighbours):
        chosen_ref, member_ref, turned_ref = refs[3 * place : 3 * place + 3]
        member_lines = member_ref.shape[0]
        pages = (member_lines - round_up(page_len, LANES)) // steps
        member, turned = membership(
            bounds_ref[...],
            lax.axis_index("tp") ^ neighbour,
            pages,
            own_lines,
            member_lines,
            row_lines,
            steps,
        )
        chosen_ref[...] = jnp.dot(
            member.astype(jnp.bfloat16), query_ref[...], preferred_element_type=jnp.float32
        ).astype(jnp.bfloat16)
        member_ref[...] = member
        turned_ref[...] = turned


def prepare(bounds, query, neighbours, pages, page_len, own_lines, steps):
    row_lines, query_width = query.shape
    member_lines = pages * steps + round_up(page_len, LANES)
    shapes = (
        jax.ShapeDtypeStruct((member_lines, query_width), jnp.bfloat16),
        jax.ShapeDtypeStruct((member_lines, row_lines), jnp.float32),
        jax.ShapeDtypeStruct((row_lines, member_lines), jnp.float32),
    )
    out = call(
        functools.partial(prepare_kernel, steps, own_lines, page_len, neighbours),
        (bounds, query),
        [vmem()] * 2,
        out_specs=[vmem()] * (3 * len(neighbours)),
        out_shape=shapes * len(neighbours),
        compiler_params=params(8),
        name="prepare",
    )
    return [out[3 * place : 3 * place + 3] for place in range(len(neighbours))]


def page_batch(pages, page_len):
    return min(pages, max(1, LANES // page_len))


def score_kernel(steps, has_earlier, chosen, member_ref, turned_ref, keys_ref, *refs):
    if has_earlier:
        early_max_ref, early_total_ref = refs[:2]
        refs = refs[2:]
    weights_ref, fresh_ref, max_ref, total_ref, scores, fresh_scores = refs
    row_lines, query_width = turned_ref.shape[0], chosen.shape[1]
    group = query_width // HD
    page_len = keys_ref.shape[1]
    batch = weights_ref.shape[2] // page_len
    blocks, lines = weights_ref.shape[0], batch * steps
    pages = blocks * batch
    spare = member_ref.shape[0] - pages * steps - page_len
    scale = HD ** (-0.5)
    lane = lax.broadcasted_iota(jnp.int32, (1, LANES), 1)
    member, turned = member_ref[...], turned_ref[...]
    is_member = turned > 0

    line = lax.broadcasted_iota(jnp.int32, (group * lines, batch * page_len), 0)
    token = lax.broadcasted_iota(jnp.int32, (group * lines, batch * page_len), 1)
    page_mask = (line % lines) // steps == token // page_len
    line = lax.broadcasted_iota(jnp.int32, (group * page_len, page_len), 0) % page_len
    token = lax.broadcasted_iota(jnp.int32, (group * page_len, page_len), 1)
    fresh_mask = (line // steps == token // steps) & (token % steps <= line % steps)

    def score(first_line, count, keys, mask):
        rows = slice(first_line, first_line + count)
        queries = jnp.concatenate(
            [chosen[rows, g * HD : (g + 1) * HD] for g in range(group)], axis=0
        )
        found = lax.dot_general(
            queries, keys, (((1,), (1,)), ((), ())), preferred_element_type=jnp.float32
        )
        found = jnp.where(mask, found * scale, NEGATIVE)
        largest = jnp.max(found, axis=1, keepdims=True)
        block_max = jnp.zeros((count, LANES), jnp.float32)
        for g in range(group):
            block_max = jnp.where(lane == g, largest[g * count : (g + 1) * count], block_max)
        return found, block_max

    maxima = []
    for block in range(blocks):
        keys = keys_ref[block * batch : (block + 1) * batch].reshape(batch * page_len, HD)
        scores[block], block_max = score(block * lines, lines, keys, page_mask)
        maxima.append(block_max)
    fresh_scores[...], block_max = score(pages * steps, page_len, keys_ref[pages], fresh_mask)
    maxima.append(block_max)
    if spare:
        maxima.append(jnp.zeros((spare, LANES), jnp.float32))

    line_max = jnp.transpose(jnp.concatenate(maxima, axis=0))
    row_max = jnp.full((row_lines, LANES), NEGATIVE, jnp.float32)
    for g in range(group):
        best = jnp.max(
            jnp.where(is_member, line_max[g : g + 1, :], NEGATIVE), axis=1, keepdims=True
        )
        row_max = jnp.where(lane == g, best, row_max)
    if has_earlier:
        row_max = jnp.maximum(row_max, early_max_ref[...])
    spread = jnp.dot(
        member, row_max, precision=HIGHEST, preferred_element_type=jnp.float32
    )

    def weigh(first_line, count, found, mask):
        rows = spread[first_line : first_line + count]
        shift = jnp.concatenate([rows[:, g : g + 1] for g in range(group)], axis=0)
        weights = jnp.where(mask, jnp.exp(jnp.minimum(found - shift, 0.0)), 0.0)
        weights = weights.astype(jnp.bfloat16)
        total = jnp.sum(weights.astype(jnp.float32), axis=1, keepdims=True)
        block_total = jnp.zeros((count, LANES), jnp.float32)
        for g in range(group):
            block_total = jnp.where(lane == g, total[g * count : (g + 1) * count], block_total)
        return weights, block_total

    totals = []
    for block in range(blocks):
        weights_ref[block], total = weigh(block * lines, lines, scores[block], page_mask)
        totals.append(total)
    fresh_ref[...], total = weigh(pages * steps, page_len, fresh_scores[...], fresh_mask)
    totals.append(total)
    if spare:
        totals.append(jnp.zeros((spare, LANES), jnp.float32))
    row_total = jnp.dot(
        turned,
        jnp.concatenate(totals, axis=0),
        precision=HIGHEST,
        preferred_element_type=jnp.float32,
    )
    if has_earlier:
        row_total = row_total + early_total_ref[...] * jnp.exp(early_max_ref[...] - row_max)
    max_ref[...] = row_max
    total_ref[...] = row_total


def score(choice, keys, steps, earlier=(), flops=0):
    (member_lines, query_width), row_lines = choice[0].shape, choice[2].shape[0]
    group = query_width // HD
    page_len = keys.shape[1]
    pages = (member_lines - round_up(page_len, LANES)) // steps
    batch = page_batch(pages, page_len)
    blocks = pages // batch
    shapes = ((blocks, group * batch * steps, batch * page_len), (group * page_len, page_len))
    stat = jax.ShapeDtypeStruct((row_lines, LANES), jnp.float32)
    operands = (*choice, keys, *earlier)
    return call(
        functools.partial(score_kernel, steps, bool(earlier)),
        operands,
        [vmem()] * len(operands),
        flops=flops,
        out_specs=[vmem()] * 4,
        out_shape=[jax.ShapeDtypeStruct(shape, jnp.bfloat16) for shape in shapes] + [stat, stat],
        scratch_shapes=[pltpu.VMEM(shape, jnp.float32) for shape in shapes],
        compiler_params=params(12),
        name="score",
    )


def value_kernel(steps, chunk, chunks, has_earlier, has_notes, last, *refs):
    weights_ref, fresh_ref, turned_ref, values_ref, max_ref, total_ref = refs[:6]
    refs = refs[6:]
    if has_earlier:
        early_max_ref, early_numer_ref = refs[:2]
        refs = refs[2:]
    if has_notes:
        own_keys_ref, near_keys_ref = refs[:2]
        refs = refs[2:]
    out_ref, high, low = refs
    row_lines, member_lines = turned_ref.shape
    page_len = values_ref.shape[1]
    blocks, batch = weights_ref.shape[0], weights_ref.shape[2] // page_len
    lines, pages = batch * steps, blocks * batch
    all_groups = weights_ref.shape[1] // lines
    group = all_groups // chunks
    first = chunk * group
    used = pages * steps + page_len

    def gain(first_line, count, weights, values):
        numer = jnp.dot(weights, values, preferred_element_type=jnp.float32)
        rounded = numer.astype(jnp.bfloat16)
        rest = (numer - rounded.astype(jnp.float32)).astype(jnp.bfloat16)
        for g in range(group):
            part = slice(g * count, (g + 1) * count)
            columns = slice(g * HD, (g + 1) * HD)
            high[first_line : first_line + count, columns] = rounded[part]
            low[first_line : first_line + count, columns] = rest[part]

    for block in range(blocks):
        weights = weights_ref[block, first * lines : (first + group) * lines]
        values = values_ref[block * batch : (block + 1) * batch].reshape(batch * page_len, HD)
        gain(block * lines, lines, weights, values)
    weights = fresh_ref[first * page_len : (first + group) * page_len]
    gain(pages * steps, page_len, weights, values_ref[pages])
    if member_lines > used:
        high[used:, :] = jnp.zeros((member_lines - used, group * HD), jnp.bfloat16)
        low[used:, :] = jnp.zeros((member_lines - used, group * HD), jnp.bfloat16)

    lane = lax.broadcasted_iota(jnp.int32, (1, LANES), 1)
    row_max, row_total = max_ref[...], total_ref[...]
    present = row_total > 0
    inverse = jnp.where(present, 1.0 / jnp.where(present, row_total, 1.0), 0.0)
    if has_earlier:
        scale_early = jnp.exp(early_max_ref[...] - row_max)
    if last and chunk == 0:
        log_sum = jnp.where(
            present & (lane < all_groups),
            row_max + jnp.log(jnp.where(present, row_total, 1.0)),
            jnp.where(lane < all_groups, NEGATIVE, 0.0),
        )
        lanes = split_sums(log_sum, all_groups)
        if has_notes:
            lanes = lanes + owner_notes(
                own_keys_ref[pages + 1], near_keys_ref[pages + 1], row_lines, 3 * all_groups
            )
        out_ref[:, group * HD :] = lanes.astype(jnp.bfloat16)
    turned = turned_ref[...].astype(jnp.bfloat16)
    for g in range(group):
        columns = slice(g * HD, (g + 1) * HD)
        which = slice(first + g, first + g + 1)
        numer = jnp.dot(turned, high[:, columns], preferred_element_type=jnp.float32) + jnp.dot(
            turned, low[:, columns], preferred_element_type=jnp.float32
        )
        if has_earlier:
            early = early_numer_ref[:, (first + g) * HD : (first + g + 1) * HD]
            numer = numer + early * scale_early[:, which]
        if last:
            numer = numer * inverse[:, which]
        out_ref[:, columns] = numer.astype(out_ref.dtype)


def value(scored, turned, values, steps, chunk, chunks, last, earlier=(), notes=(), follows=()):
    row_lines, member_lines = turned.shape
    page_len = values.shape[1]
    group = scored[1].shape[0] // page_len // chunks
    wide = group * HD + (LANES if last and chunk == 0 else 0)
    operands = (*scored[:2], turned, values, *scored[2:], *earlier, *notes)
    return call(
        functools.partial(value_kernel, steps, chunk, chunks, bool(earlier), bool(notes), last),
        operands,
        [vmem()] * len(operands),
        follows,
        out_specs=vmem(),
        out_shape=jax.ShapeDtypeStruct(
            (row_lines, wide), jnp.bfloat16 if last else jnp.float32
        ),
        scratch_shapes=[pltpu.VMEM((member_lines, group * HD), jnp.bfloat16)] * 2,
        compiler_params=params(8),
        name="value",
    )


def split_sums(value, group):
    first = value.astype(jnp.bfloat16).astype(jnp.float32)
    rest = value - first
    second = rest.astype(jnp.bfloat16).astype(jnp.float32)
    third = rest - second
    return first + pltpu.roll(second, group, axis=1) + pltpu.roll(third, 2 * group, axis=1)


def owner_notes(own, near_page, row_lines, first_lane):
    lines = near_page.shape[0]
    notes = jnp.concatenate(
        [
            own.astype(jnp.float32),
            near_page.astype(jnp.float32),
            jnp.zeros((row_lines - 2 * lines, LANES), jnp.float32),
        ]
    )
    return pltpu.roll(notes, first_lane, axis=1)


def join_sums(parts, group):
    parts = parts.astype(jnp.float32)
    return (
        parts
        + pltpu.roll(parts, LANES - group, axis=1)
        + pltpu.roll(parts, LANES - 2 * group, axis=1)
    )


def combine_kernel(group, first, sums_ref, their_sums_ref, mine_ref, theirs_ref, out_ref):
    sums = join_sums(sums_ref[:, -LANES:], group)
    their_sums = join_sums(their_sums_ref[:, -LANES:], group)
    largest = jnp.maximum(sums, their_sums)
    weight = jnp.exp(sums - largest)
    their_weight = jnp.exp(their_sums - largest)
    inverse = 1.0 / (weight + their_weight)
    weight = weight * inverse
    their_weight = their_weight * inverse
    for place in range(out_ref.shape[1] // HD):
        g = first + place
        columns = slice(place * HD, (place + 1) * HD)
        out_ref[:, columns] = (
            mine_ref[:, columns].astype(jnp.float32) * weight[:, g : g + 1]
            + theirs_ref[:, columns].astype(jnp.float32) * their_weight[:, g : g + 1]
        ).astype(jnp.bfloat16)


def combine(mine, theirs, chunk, follows=()):
    row_lines, width = mine[0].shape
    width -= LANES
    group = width // HD * len(mine)
    return call(
        functools.partial(combine_kernel, group, chunk * width // HD),
        (mine[0], theirs[0], mine[chunk], theirs[chunk]),
        [vmem()] * 4,
        follows,
        out_specs=vmem(),
        out_shape=jax.ShapeDtypeStruct((row_lines, width), jnp.bfloat16),
        compiler_params=params(4),
        name="combine",
    )


def block_row(own, chunk, chunks, head_count, depth):
    head = lax.rem(lax.axis_index("tp") + (0 if own else 1), head_count)
    return pl.multiple_of((head * chunks + chunk) * depth, depth)


def fetch_kernel(blocks, chunks, head_count, weight_ref, held_ref, done_ref, arrived):
    depth = held_ref.shape[0] // len(blocks)
    pieces = arrived.shape[0] // len(blocks)
    size = depth // pieces
    copies = []
    for place, (own, chunk) in enumerate(blocks):
        base = block_row(own, chunk, chunks, head_count, depth)
        for piece in range(pieces):
            copies.append(
                pltpu.make_async_copy(
                    weight_ref.at[pl.ds(pl.multiple_of(base + piece * size, size), size)],
                    held_ref.at[pl.ds(place * depth + piece * size, size)],
                    arrived.at[place * pieces + piece],
                )
            )
    for copy in copies:
        copy.start()
    done_ref[...] = jnp.zeros_like(done_ref)
    for copy in copies:
        copy.wait()


def fetch(weight, blocks, chunks, head_count, depth, follows):
    pieces = 4
    return call(
        functools.partial(fetch_kernel, blocks, chunks, head_count),
        in_hbm(weight),
        [hbm()],
        follows,
        out_specs=(vmem(), vmem()),
        out_shape=(
            pltpu.VMEM((len(blocks) * depth, weight.shape[1]), weight.dtype),
            jax.ShapeDtypeStruct((8, LANES), jnp.float32),
        ),
        scratch_shapes=[pltpu.SemaphoreType.DMA((len(blocks) * pieces,))],
        compiler_params=params(1),
        name="fetch",
    )


def project_kernel(parts, has_total, chunk_lines, first, offsets, chunks, head_count, *refs):
    input_refs, weight_ref, refs = refs[:parts], refs[parts], refs[parts + 1 :]
    streamed = offsets is None
    if streamed:
        held, arrived = refs[-2:]
        refs = refs[:-2]
    outs = refs[1:] if has_total else refs
    depth, width = input_refs[0].shape[1], outs[0].shape[-1]
    block = min(width, 512)
    count = width // block

    def piece(index):
        return pltpu.make_async_copy(
            weight_ref.at[
                pl.ds(block_row(True, 0, chunks, head_count, depth), depth),
                pl.ds(first + index * block, block),
            ],
            held.at[:, pl.ds(index * block, block)],
            arrived.at[index],
        )

    if streamed:
        for index in range(count):
            piece(index).start()
    for index in range(count):
        start = index * block
        columns = slice(first + start, first + start + block)
        product = refs[0][:, columns] if has_total else 0.0
        if streamed:
            piece(index).wait()
            product = product + jnp.dot(
                input_refs[0][...],
                held[:, start : start + block],
                preferred_element_type=jnp.float32,
            )
        else:
            for input_ref, offset in zip(input_refs, offsets):
                product = product + jnp.dot(
                    input_ref[...],
                    weight_ref[offset * depth : (offset + 1) * depth, columns],
                    preferred_element_type=jnp.float32,
                )
        if chunk_lines is None:
            outs[0][:, start : start + block] = product
            continue
        core = lax.rem(lax.axis_index("kv"), 2)
        keep_ref, send_ref = outs
        for pair in range(keep_ref.shape[0]):
            even = product[2 * pair * chunk_lines : (2 * pair + 1) * chunk_lines]
            odd = product[(2 * pair + 1) * chunk_lines : (2 * pair + 2) * chunk_lines]
            keep_ref[pair, :, start : start + block] = jnp.where(core == 0, even, odd)
            send_ref[pair, :, start : start + block] = jnp.where(core == 0, odd, even).astype(
                send_ref.dtype
            )


def project(inputs, weight, offsets, chunks, head_count, total, columns, chunk_lines, follows=()):
    row_lines, depth = inputs[0].shape
    first, width = columns
    in_specs = [vmem()] * len(inputs) + [hbm() if offsets is None else vmem()]
    operands = [*inputs, *(in_hbm(weight) if offsets is None else [weight])]
    if total is not None:
        in_specs.append(vmem())
        operands.append(total)
    if chunk_lines is None:
        out_shape = jax.ShapeDtypeStruct((row_lines, width), jnp.float32)
        out_specs = vmem()
    else:
        pairs = row_lines // (2 * chunk_lines)
        shape = (pairs, chunk_lines, width)
        out_shape = (
            jax.ShapeDtypeStruct(shape, jnp.float32),
            jax.ShapeDtypeStruct(shape, jnp.bfloat16),
        )
        out_specs = (vmem(), vmem())
    scratch = []
    if offsets is None:
        scratch = [
            pltpu.VMEM((depth, width), weight.dtype),
            pltpu.SemaphoreType.DMA((max(1, width // 512),)),
        ]
    return call(
        functools.partial(
            project_kernel,
            len(inputs),
            total is not None,
            chunk_lines,
            first,
            offsets,
            chunks,
            head_count,
        ),
        operands,
        in_specs,
        follows,
        out_specs=out_specs,
        out_shape=out_shape,
        scratch_shapes=scratch,
        compiler_params=params(16 if offsets is None else 8),
        name="project",
    )


def add_core_kernel(keep_ref, got_ref, own_ref, *send_refs):
    half = lax.axis_index("kv") // 2
    own_ref[...] = keep_ref[half] + got_ref[half].astype(jnp.float32)
    for step, send_ref in enumerate(send_refs, 1):
        part = keep_ref[half ^ step] + got_ref[half ^ step].astype(jnp.float32)
        send_ref[...] = part.astype(send_ref.dtype)


def sum_heads(keep, send, kv_size):
    got = lax.ppermute(send, "kv", flip(kv_size, 1))
    shape = keep.shape[1:]
    own, *sends = call(
        add_core_kernel,
        (keep, got),
        [vmem(), vmem()],
        out_specs=[vmem()] * (kv_size // 2),
        out_shape=[jax.ShapeDtypeStruct(shape, jnp.float32)]
        + [jax.ShapeDtypeStruct(shape, jnp.bfloat16)] * (kv_size // 2 - 1),
        compiler_params=params(4),
        name="add_core",
    )
    return [own] + [
        lax.ppermute(part, "kv", flip(kv_size, 2 * step)) for step, part in enumerate(sends, 1)
    ]


def finish_kernel(pieces, *refs):
    parts, out_ref, done_ref = refs[:-2], refs[-2], refs[-1]
    done_ref[...] = jnp.zeros_like(done_ref)
    each = len(parts) // pieces
    steps, width = out_ref.shape[1], out_ref.shape[2] // pieces
    for piece in range(pieces):
        total = parts[piece * each][...]
        for part in parts[piece * each + 1 : (piece + 1) * each]:
            total = total + part[...].astype(jnp.float32)
        out_ref[:, :, piece * width : (piece + 1) * width] = total.astype(jnp.bfloat16).reshape(
            -1, steps, width
        )


def finish(results, steps):
    lines, width = results[0][0].shape
    parts = [part for pieces in results for part in pieces]
    return call(
        functools.partial(finish_kernel, len(results)),
        parts,
        [vmem()] * len(parts),
        out_specs=(vmem(), vmem()),
        out_shape=(
            jax.ShapeDtypeStruct((lines // steps, steps, width * len(results)), jnp.bfloat16),
            jax.ShapeDtypeStruct((8, LANES), jnp.float32),
        ),
        compiler_params=params(4),
        name="finish",
    )


def body(
    queries, fresh_keys, fresh_values, cache_keys, cache_values, page_counts, page_owner, out_weight
):
    tp_size, kv_size = lax.axis_size("tp"), lax.axis_size("kv")
    head_count, pages_here, page_width = cache_keys.shape
    row_count, step_count, query_width = queries.shape
    own_lines = fresh_keys.shape[0] * step_count
    page_len = page_width // HD
    row_lines = row_count * step_count
    head_width = query_width // head_count
    group = head_width // HD
    cap = max(2, (2 * pages_here + tp_size - 1) // tp_size)
    out_width = out_weight.shape[1]
    chunk_lines = row_lines // kv_size
    caches = (cache_keys, cache_values)
    fresh = (fresh_keys, fresh_values)

    paired = head_count == 2 and tp_size == 4 and group % 2 == 0 and cap % 16 == 0
    paired = paired and 3 * group + pages_here <= LANES and 2 * page_len <= row_lines
    chunks = 2 if paired else 1
    part = head_width // chunks
    everything = (0, out_width)

    if paired:
        keys, values, send_last = gather_tokens(1, caches, fresh, page_owner, handing=3, cap=cap)
        near_keys = lax.ppermute(keys, "tp", flip(tp_size, 1))
        got_inner = lax.ppermute(send_last, "tp", [(1, 2), (2, 1)])
        own_keys, own_values, query, bounds = gather_tokens(
            0, caches, fresh, page_owner, queries, page_counts, follows=(send_last,)
        )
        near_values = lax.ppermute(tie(values, bounds), "tp", flip(tp_size, 1))
        own_choice, near_choice = prepare(
            bounds, query, (0, 1), pages_here, page_len, own_lines, step_count
        )
        scored = score(own_choice, own_keys, step_count)
        early_numer = value(scored, own_choice[2], own_values, step_count, 0, 1, False)
        early_max, early_total = scored[2:]
        scored = score(near_choice, near_keys, step_count, (early_max, early_total), 1 << 34)
        payload = [
            value(
                scored,
                near_choice[2],
                near_values,
                step_count,
                chunk,
                chunks,
                True,
                (early_max, early_numer),
                () if chunk else (own_keys, near_keys),
            )
            for chunk in range(chunks)
        ]
        jobs = ((2, True), (1, False), (0, True))
        send_far, send_near, kept = place_pages(
            page_owner, caches, jobs, cap, tp_size, False, (payload[1],)
        )
        blocks = ((True, 1), (False, 0), (False, 1))
        held, held_done = fetch(out_weight, blocks, chunks, head_count, part, payload[1:])
        payload[1] = tie(payload[1], held_done)
        theirs = [lax.ppermute(p, "tp", flip(tp_size, 2)) for p in payload]
        got_near = lax.ppermute(tie(send_near, held_done), "tp", flip(tp_size, 1))
        near_pages = place_near(near_keys, near_values, head_count, cap, tp_size)
        first_part = combine(payload, theirs, 0, (got_inner,))
        near_first = lax.ppermute(first_part, "tp", flip(tp_size, 1))
        total = project([first_part], out_weight, None, chunks, head_count, None, everything, None)
        got_far = lax.ppermute(tie(send_far, total), "tp", flip(tp_size, 2))
        got_outer = lax.ppermute(tie(send_last, total), "tp", [(0, 3), (3, 0)])
        second_part = combine(payload, theirs, 1, (got_near, total))
        near_second = lax.ppermute(second_part, "tp", flip(tp_size, 1))
        own_parts, near_parts = (first_part, second_part), (near_first, near_second)
        plan = ((0, None, None), (1, None, 0), (1, None, 1), (3, (1, 2), None))
        *settled, settled_done = settle(
            [kept, near_pages, got_near, got_inner], plan, head_count, tp_size * cap, (), (total,)
        )
        total = project(
            [own_parts[1], near_parts[0]],
            held,
            (0, 1),
            chunks,
            head_count,
            total,
            everything,
            None,
            (settled_done,),
        )
        results = []
        for first in (0, out_width // 2):
            columns = (first, out_width // 2)
            keep, send = project(
                [near_parts[1]],
                held,
                (2,),
                chunks,
                head_count,
                total,
                columns,
                chunk_lines,
            )
            results.append(sum_heads(keep, send, kv_size))
        attention_out, finished = finish(results, step_count)
        slot_rows = slot_rows_near(
            bounds,
            payload[0],
            theirs[0],
            pages_here,
            3 * group,
            page_len,
            cap,
            (head_count, tp_size * cap),
            step_count,
            (results[1][0],),
        )
        plan = ((2, None, None), (3, (0, 3), None))
        slot_keys, slot_values, _ = settle(
            [got_far, got_outer], plan, head_count, tp_size * cap, settled, (finished,)
        )
        return (attention_out, slot_keys, slot_values, slot_rows)

    def hand_over(cache):
        jobs = tuple((d, True) for d in range(tp_size))
        sent = place_pages(page_owner, (cache,), jobs, cap, tp_size, True)
        got = lax.all_to_all(
            jnp.concatenate(sent), "tp", split_axis=0, concat_axis=0, tiled=True
        )
        return got.transpose(1, 0, 2, 3).reshape(head_count, tp_size * cap, page_width)

    slot_keys, slot_values = hand_over(cache_keys), hand_over(cache_values)
    slot_rows = slot_rows_gathered(page_owner, page_counts, cap)
    attended = []
    for head in range(head_count):
        cut = slice(head, head + 1)
        lanes = slice(head * HD, (head + 1) * HD)
        keys, values, query, bounds = gather_tokens(
            0,
            [cache[cut] for cache in caches],
            [new[:, :, lanes] for new in fresh],
            page_owner[cut],
            queries[:, :, head * head_width : (head + 1) * head_width],
            page_counts,
        )
        (choice,) = prepare(
            bounds, query, (0,), pages_here, page_len, own_lines, step_count
        )
        scored = score(choice, keys, step_count)
        payload = value(scored, choice[2], values, step_count, 0, 1, True)
        raw = payload[:, part:].astype(jnp.float32)
        sums = raw[:, :group] + raw[:, group : 2 * group] + raw[:, 2 * group : 3 * group]
        weight = jnp.exp(sums - lax.pmax(sums, "tp"))
        numer = payload[:, :part].astype(jnp.float32).reshape(row_lines, group, HD)
        numer = lax.psum(numer * weight[..., None], "tp")
        joined = numer / lax.psum(weight, "tp")[..., None]
        attended.append(joined.reshape(row_lines, head_width).astype(jnp.bfloat16))
    keep, send = project(
        [jnp.concatenate(attended, axis=1)], out_weight, None, 1, 1, None, everything, chunk_lines
    )
    attention_out, _ = finish([sum_heads(keep, send, kv_size)], step_count)
    return (attention_out, slot_keys, slot_values, slot_rows)


def solution(mesh):
    return jax.shard_map(
        body,
        mesh=mesh,
        in_specs=(
            P("grp", None, "kv"),
            P(("grp", "tp"), None, "kv"),
            P(("grp", "tp"), None, "kv"),
            P(("grp", "kv"), "tp", None),
            P(("grp", "kv"), "tp", None),
            P("grp"),
            P(("grp", "kv"), "tp"),
            P("kv", "tp"),
        ),
        out_specs=(
            P(("grp", "kv"), None, "tp"),
            P(("grp", "kv"), "tp", None),
            P(("grp", "kv"), "tp", None),
            P(("grp", "kv"), "tp"),
        ),
        check_vma=False,
    )
```

```python
import functools

import jax
import jax.numpy as jnp
from jax import lax
from jax.experimental import pallas as pl
from jax.experimental.pallas import tpu as pltpu
from jax.sharding import PartitionSpec as P

HD = 128
LANES = 128
NEGATIVE = -1e30
HIGHEST = lax.Precision.HIGHEST
MIB = 1024 * 1024


def round_up(value, step):
    return -(-value // step) * step


def flip(size, bit):
    return [(i, i ^ bit) for i in range(size)]


def params(mib):
    return pltpu.CompilerParams(vmem_limit_bytes=mib * MIB)


def in_hbm(*arrays):
    return [pltpu.with_memory_space_constraint(array, pltpu.HBM) for array in arrays]


def vmem():
    return pl.BlockSpec(memory_space=pltpu.VMEM)


def hbm():
    return pl.BlockSpec(memory_space=pltpu.HBM)


def anywhere():
    return pl.BlockSpec(memory_space=pl.ANY)


def call(kernel, operands, in_specs, follows=(), flops=0, **rest):
    count, extra = len(operands), len(follows)

    def without_extra(*refs):
        kernel(*refs[:count], *refs[count + extra :])

    return pl.pallas_call(
        without_extra,
        in_specs=list(in_specs) + [anywhere()] * extra,
        cost_estimate=pl.CostEstimate(flops=flops, bytes_accessed=0, transcendentals=0),
        **rest,
    )(*operands, *follows)


def tie(value, *follows):
    return call(
        lambda value_ref, out_ref: None,
        (value,),
        [anywhere()],
        follows,
        out_specs=anywhere(),
        out_shape=jax.ShapeDtypeStruct(value.shape, value.dtype),
        input_output_aliases={0: 0},
        compiler_params=params(1),
        name="tie",
    )


def earlier_pages(page_count):
    first = lax.broadcasted_iota(jnp.int32, (page_count, page_count), 0)
    second = lax.broadcasted_iota(jnp.int32, (page_count, page_count), 1)
    return (first < second).astype(jnp.bfloat16)


def rank_pages(away, earlier, dest_rows):
    ways = lax.broadcasted_iota(jnp.int32, (dest_rows, away.shape[1]), 0)
    listed = (ways == away).astype(jnp.float32)
    before = jnp.dot(listed.astype(jnp.bfloat16), earlier, preferred_element_type=jnp.float32)
    return jnp.sum(before * listed, axis=0, keepdims=True).astype(jnp.int32)


def slot_picks(owners, me, distances, cap, tp_size):
    head_count, page_count = owners.shape
    earlier = earlier_pages(page_count)
    row = lax.broadcasted_iota(jnp.int32, (cap, page_count), 0)
    picks = []
    for head in range(head_count):
        away = owners[head : head + 1, :] ^ me
        rank = rank_pages(away, earlier, round_up(tp_size, 8))
        picks.append([((away == d) & (rank == row)).astype(jnp.float32) for d in distances])
    return picks


def place_rows(pages_ref, pick, targets):
    width, cap = pages_ref.shape[1], pick[0].shape[0]
    step = min(width, 1024)
    for start in range(0, width, step):
        columns = slice(start, start + step)
        placed = jnp.dot(
            jnp.concatenate(pick).astype(jnp.bfloat16),
            pages_ref[:, columns],
            preferred_element_type=jnp.float32,
        ).astype(jnp.bfloat16)
        for which, target in enumerate(targets):
            target[:, columns] = placed[which * cap : (which + 1) * cap]


def place_kernel(cap, jobs, by_index, tp_size, owner_ref, *refs):
    count = (len(refs) - 2 - len(jobs)) // 2
    sources, targets = refs[:count], refs[count : count + len(jobs)]
    held, owners, arrived = refs[count + len(jobs) : -2], refs[-2], refs[-1]
    head_count = sources[0].shape[0]
    copies = [
        pltpu.make_async_copy(source, target, arrived.at[i])
        for i, (source, target) in enumerate(zip((owner_ref, *sources), (owners, *held)))
    ]
    for copy in copies:
        copy.start()
    copies[0].wait()
    me = 0 if by_index else lax.axis_index("tp")
    own_head = lax.rem(me, head_count)
    picks = slot_picks(owners, me, [d for d, _ in jobs], cap, tp_size)

    def place(index, head, pick, target_of):
        place_rows(held[index].at[head], pick, target_of)

    shared = [i for i, (_, every) in enumerate(jobs) if every]
    single = [i for i, (_, every) in enumerate(jobs) if not every]
    for index in range(count):
        copies[index + 1].wait()
        for head in range(head_count):
            if shared:
                pick = [picks[head][i] for i in shared]
                place(index, head, pick, [targets[i].at[index, head] for i in shared])
        if single:
            pick = []
            for i in single:
                chosen = picks[0][i]
                for head in range(1, head_count):
                    chosen = jnp.where(own_head == head, picks[head][i], chosen)
                pick.append(chosen)
            place(index, own_head, pick, [targets[i].at[index] for i in single])


def place_pages(page_owner, caches, jobs, cap, tp_size, by_index, follows=()):
    head_count, page_count, width = caches[0].shape
    return call(
        functools.partial(place_kernel, cap, jobs, by_index, tp_size),
        in_hbm(page_owner, *caches),
        [hbm()] * (1 + len(caches)),
        follows,
        out_specs=tuple(vmem() for _ in jobs),
        out_shape=tuple(
            jax.ShapeDtypeStruct(
                (len(caches),) + ((head_count,) if every else ()) + (cap, width), jnp.bfloat16
            )
            for _, every in jobs
        ),
        scratch_shapes=[pltpu.VMEM(cache.shape, cache.dtype) for cache in caches]
        + [
            pltpu.VMEM(page_owner.shape, jnp.int32),
            pltpu.SemaphoreType.DMA((1 + len(caches),)),
        ],
        compiler_params=params(8),
        name="place_pages",
    )


def place_near_kernel(tp_size, head_count, keys_ref, values_ref, out_ref):
    cap, width = out_ref.shape[1:]
    pages, page_len = values_ref.shape[0] - 1, values_ref.shape[1]
    me = lax.axis_index("tp")
    head = lax.rem(me, head_count)
    lists = keys_ref[pages + 1].astype(jnp.float32)[:, :pages].astype(jnp.int32)
    owner = lists[0:1]
    for which in range(1, head_count):
        owner = jnp.where(head == which, lists[which : which + 1], owner)
    rank = rank_pages(owner, earlier_pages(pages), round_up(tp_size, 8))
    row = lax.broadcasted_iota(jnp.int32, (cap, pages), 0)
    pick = ((owner == me) & (rank == row)).astype(jnp.bfloat16)
    for index, source in enumerate((keys_ref, values_ref)):
        paged = source[:pages].reshape(pages, page_len * HD)
        out_ref[index] = jnp.dot(pick, paged, preferred_element_type=jnp.float32).astype(
            jnp.bfloat16
        )


def place_near(keys, values, head_count, cap, tp_size):
    page_len = keys.shape[1]
    return call(
        functools.partial(place_near_kernel, tp_size, head_count),
        (keys, values),
        [vmem()] * 2,
        out_specs=vmem(),
        out_shape=jax.ShapeDtypeStruct((2, cap, page_len * HD), jnp.bfloat16),
        compiler_params=params(8),
        name="place_near",
    )


def settle_kernel(plan, *refs):
    count = len(plan)
    parts, arrived = refs[:count], refs[-1]
    key_ref, value_ref, done_ref = refs[-4:-1]
    head_count, cap = key_ref.shape[0], parts[0].shape[-2]
    me = lax.axis_index("tp")

    def copies_of(place):
        distance, _, other = plan[place]
        first = pl.multiple_of((me ^ distance) * cap, cap)
        copies = []
        for index, target in enumerate((key_ref, value_ref)):
            for head in range(head_count if other is None else 1):
                source = parts[place].at[index]
                if other is None:
                    source = source.at[head]
                else:
                    head = lax.rem(me + other, head_count)
                copies.append(
                    pltpu.make_async_copy(
                        source,
                        target.at[head, pl.ds(first, cap)],
                        arrived.at[place * 2 * head_count + len(copies)],
                    )
                )
        return copies

    def move(place, action):
        holders = plan[place][1]
        if holders is None:
            for copy in copies_of(place):
                action(copy)
            return
        holds = functools.reduce(lambda a, b: a | b, [me == holder for holder in holders])

        @pl.when(holds)
        def _():
            for copy in copies_of(place):
                action(copy)

    for place in range(count):
        move(place, lambda copy: copy.start())
    done_ref[...] = jnp.zeros_like(done_ref)
    for place in range(count):
        move(place, lambda copy: copy.wait())


def settle(parts, plan, head_count, slots, settled=(), follows=()):
    width = parts[0].shape[-1]
    shape = jax.ShapeDtypeStruct((head_count, slots, width), jnp.bfloat16)
    count = len(parts)
    return call(
        functools.partial(settle_kernel, plan),
        (*parts, *settled),
        [vmem()] * count + [hbm()] * len(settled),
        follows,
        out_specs=(hbm(), hbm(), vmem()),
        out_shape=(shape, shape, jax.ShapeDtypeStruct((8, LANES), jnp.float32)),
        input_output_aliases={count: 0, count + 1: 1} if settled else {},
        scratch_shapes=[pltpu.SemaphoreType.DMA((2 * count * head_count,))],
        compiler_params=params(6),
        name="settle",
    )


def slot_rows_kernel(
    cap, pages, first_lane, page_len, steps, bounds_ref, own_ref, far_ref, out_ref
):
    head_count, slots = out_ref.shape
    tp_size = slots // cap
    me = lax.axis_index("tp")
    earlier = earlier_pages(pages)
    ends = bounds_ref[1:2, :]
    ids = lax.broadcasted_iota(jnp.int32, (pages, ends.shape[1]), 0)
    row = lax.broadcasted_iota(jnp.int32, (cap, pages), 0)
    ones = jnp.ones((8, ends.shape[1]), jnp.bfloat16)
    lines = [[] for _ in range(head_count)]
    for distance in range(tp_size):
        block = me ^ distance
        marks = lax.dot_general(
            ones,
            (ends <= block * pages + ids).astype(jnp.bfloat16),
            (((1,), (1,)), ((), ())),
            preferred_element_type=jnp.float32,
        )
        marks = marks / steps + 1
        source = own_ref if distance < 2 else far_ref
        line = (distance % 2) * page_len
        notes = source[line : line + page_len, -LANES:].astype(jnp.float32)
        notes = pltpu.roll(notes, LANES - first_lane, axis=1)
        for head in range(head_count):
            owner = notes[head : head + 1, :pages].astype(jnp.int32)
            rank = rank_pages(owner, earlier, round_up(tp_size, 8))
            pick = ((owner == me) & (rank == row)).astype(jnp.bfloat16)
            found = lax.dot_general(
                marks.astype(jnp.bfloat16),
                pick,
                (((1,), (1,)), ((), ())),
                preferred_element_type=jnp.float32,
            )
            found = jnp.concatenate([found, jnp.zeros((8, LANES - cap), jnp.float32)], axis=1)
            lines[head].append(pltpu.roll(found, block * cap, axis=1)[:1])
    for head in range(head_count):
        total = lines[head][0]
        for line in lines[head][1:]:
            total = total + line
        out_ref[head : head + 1, :] = total[:, :slots].astype(jnp.int32) - 1


def slot_rows_near(bounds, own, far, pages, first_lane, page_len, cap, shape, steps, follows):
    return call(
        functools.partial(slot_rows_kernel, cap, pages, first_lane, page_len, steps),
        (bounds, own, far),
        [vmem()] * 3,
        follows,
        out_specs=vmem(),
        out_shape=jax.ShapeDtypeStruct(shape, jnp.int32),
        compiler_params=params(2),
        name="slot_rows",
    )


def slot_rows_gathered(page_owner, page_counts, cap):
    owners = lax.all_gather(page_owner, "tp", axis=0, tiled=False)
    tp_size, head_count, pages_here = owners.shape
    rows = jnp.arange(page_counts.shape[0], dtype=jnp.int32)
    row_ends = jnp.sum(jnp.where(rows[None, :] <= rows[:, None], page_counts[None, :], 0), axis=1)
    ids = jnp.arange(pages_here, dtype=jnp.int32)
    same = (owners[..., :, None] == owners[..., None, :]) & (ids[:, None] < ids[None, :])
    rank = jnp.sum(same.astype(jnp.int32), axis=2)
    blocks = jnp.arange(tp_size, dtype=jnp.int32)
    page_ids = blocks[:, None] * pages_here + ids
    page_row = jnp.sum((row_ends <= page_ids[..., None]).astype(jnp.int32), axis=-1)
    slot = jnp.where(owners == lax.axis_index("tp"), blocks[:, None, None] * cap + rank, -1)
    slot_ids = jnp.arange(tp_size * cap, dtype=jnp.int32)
    marks = jnp.where(slot[..., None] == slot_ids, page_row[:, None, :, None] + 1, 0)
    return jnp.sum(marks, axis=(0, 2)) - 1


def gather_tokens_kernel(other, with_queries, handing, *refs):
    key_ref, value_ref, fresh_key_ref, fresh_value_ref, owner_ref = refs[:5]
    arrived = refs[-1]
    if with_queries:
        all_query_ref, count_ref, *outs, query_ref, bounds_ref = refs[5:11]
        held, fresh, owners, queries, counts = refs[11:16]
    elif handing:
        *outs, hand_ref, held, fresh, owners = refs[5:11]
    else:
        *outs, held, fresh, owners = refs[5:10]
    pages, page_len = key_ref.shape[1], outs[0].shape[1]
    head_count, own_rows, steps = key_ref.shape[0], fresh.shape[1], fresh.shape[2]
    me = lax.axis_index("tp")
    head = lax.rem(me + other, head_count)
    pairs = [
        (owner_ref, owners),
        (fresh_key_ref, fresh.at[0]),
        (fresh_value_ref, fresh.at[1]),
    ]
    if handing:
        pairs += [(key_ref, held.at[0]), (value_ref, held.at[1])]
    else:
        pairs += [(key_ref.at[head], held.at[0, 0]), (value_ref.at[head], held.at[1, 0])]
    if with_queries:
        width = query_ref.shape[1]
        columns = pl.ds(pl.multiple_of(head * width, LANES), width)
        pairs += [(count_ref, counts), (all_query_ref.at[:, :, columns], queries)]
    copies = [
        pltpu.make_async_copy(source, target, arrived.at[i])
        for i, (source, target) in enumerate(pairs)
    ]
    for copy in copies:
        copy.start()
    copies[0].wait()
    outs[0][pages + 1] = owner_page(owners[...], page_len).astype(jnp.bfloat16)
    if handing:
        cap = hand_ref.shape[2]
        picks = slot_picks(owners, me, [handing], cap, lax.axis_size("tp"))
    for i in range(2):
        copies[1 + i].wait()
        new = fresh[i]
        part = new[:, :, :HD]
        for which in range(1, head_count):
            part = jnp.where(head == which, new[:, :, which * HD : (which + 1) * HD], part)
        lines = part.reshape(own_rows * steps, HD)
        if own_rows * steps < page_len:
            spare = jnp.zeros((page_len - own_rows * steps, HD), jnp.bfloat16)
            lines = jnp.concatenate([lines, spare])
        outs[i][pages] = lines
    for i in range(2):
        copies[3 + i].wait()
        paged = held[i, head] if handing else held[i, 0]
        outs[i][:pages] = paged.reshape(pages, page_len, HD)
    if handing:
        for i in range(2):
            for which in range(head_count):
                place_rows(held.at[i, which], picks[which], [hand_ref.at[i, which]])
    if with_queries:
        copies[5].wait()
        row_lines = query_ref.shape[0]
        row = lax.broadcasted_iota(jnp.int32, (1, row_lines), 1) // steps
        starts = jnp.zeros((1, row_lines), jnp.int32)
        ends = jnp.zeros((1, row_lines), jnp.int32)
        for r in range(counts.shape[0]):
            starts = starts + jnp.where(row > r, counts[r], 0)
            ends = ends + jnp.where(row >= r, counts[r], 0)
        line = lax.broadcasted_iota(jnp.int32, (8, row_lines), 0)
        bounds_ref[...] = jnp.where(line == 0, starts, ends)
        copies[6].wait()
        query_ref[...] = queries[...].reshape(row_lines, query_ref.shape[1])


def owner_page(owners, lines):
    head_count, pages = owners.shape
    page = jnp.concatenate(
        [owners.astype(jnp.float32), jnp.zeros((head_count, LANES - pages), jnp.float32)], axis=1
    )
    return jnp.concatenate([page, jnp.zeros((lines - head_count, LANES), jnp.float32)])


def gather_tokens(
    other, caches, fresh, owner, queries=None, counts=None, handing=0, cap=0, follows=()
):
    head_count, pages, width = caches[0].shape
    page_len = width // HD
    with_queries = queries is not None
    operands = [*caches, *fresh, owner]
    out_shape = [
        jax.ShapeDtypeStruct((pages + extra, page_len, HD), jnp.bfloat16) for extra in (2, 1)
    ]
    scratch = [
        pltpu.VMEM((2, head_count if handing else 1, pages, width), jnp.bfloat16),
        pltpu.VMEM((2,) + fresh[0].shape, jnp.bfloat16),
        pltpu.VMEM(owner.shape, jnp.int32),
    ]
    if handing:
        out_shape.append(jax.ShapeDtypeStruct((2, head_count, cap, width), jnp.bfloat16))
    if with_queries:
        operands += [queries, counts]
        rows, steps, query_width = queries.shape
        query_width = query_width // head_count
        out_shape += [
            jax.ShapeDtypeStruct((rows * steps, query_width), jnp.bfloat16),
            jax.ShapeDtypeStruct((8, rows * steps), jnp.int32),
        ]
        scratch += [
            pltpu.VMEM((rows, steps, query_width), jnp.bfloat16),
            pltpu.SMEM(counts.shape, jnp.int32),
        ]
    return call(
        functools.partial(gather_tokens_kernel, other, with_queries, handing),
        in_hbm(*operands),
        [hbm()] * len(operands),
        follows,
        out_specs=[vmem()] * len(out_shape),
        out_shape=out_shape,
        scratch_shapes=scratch + [pltpu.SemaphoreType.DMA((len(operands),))],
        compiler_params=params(6),
        name="gather_tokens",
    )


def membership(bounds, owner, pages, own_lines, member_lines, row_lines, steps):
    query_line = lax.broadcasted_iota(jnp.int32, (1, row_lines), 1)
    starts, ends = bounds[0:1, :], bounds[1:2, :]
    page_lines = pages * steps
    line = lax.broadcasted_iota(jnp.int32, (member_lines, row_lines), 0)
    page = owner * pages + line // steps
    in_row = (starts <= page) & (page < ends) & (line % steps == query_line % steps)
    own_line = line - page_lines
    is_own = (
        (own_line >= 0) & (own_line < own_lines) & (query_line == owner * own_lines + own_line)
    )
    member = (((line < page_lines) & in_row) | is_own).astype(jnp.float32)
    return member, jnp.transpose(member)


def prepare_kernel(steps, own_lines, page_len, neighbours, bounds_ref, query_ref, *refs):
    row_lines = query_ref.shape[0]
    for place, neighbour in enumerate(neighbours):
        chosen_ref, member_ref, turned_ref = refs[3 * place : 3 * place + 3]
        member_lines = member_ref.shape[0]
        pages = (member_lines - round_up(page_len, LANES)) // steps
        member, turned = membership(
            bounds_ref[...],
            lax.axis_index("tp") ^ neighbour,
            pages,
            own_lines,
            member_lines,
            row_lines,
            steps,
        )
        chosen_ref[...] = jnp.dot(
            member.astype(jnp.bfloat16), query_ref[...], preferred_element_type=jnp.float32
        ).astype(jnp.bfloat16)
        member_ref[...] = member
        turned_ref[...] = turned


def prepare(bounds, query, neighbours, pages, page_len, own_lines, steps):
    row_lines, query_width = query.shape
    member_lines = pages * steps + round_up(page_len, LANES)
    shapes = (
        jax.ShapeDtypeStruct((member_lines, query_width), jnp.bfloat16),
        jax.ShapeDtypeStruct((member_lines, row_lines), jnp.float32),
        jax.ShapeDtypeStruct((row_lines, member_lines), jnp.float32),
    )
    out = call(
        functools.partial(prepare_kernel, steps, own_lines, page_len, neighbours),
        (bounds, query),
        [vmem()] * 2,
        out_specs=[vmem()] * (3 * len(neighbours)),
        out_shape=shapes * len(neighbours),
        compiler_params=params(8),
        name="prepare",
    )
    return [out[3 * place : 3 * place + 3] for place in range(len(neighbours))]


def page_batch(pages, page_len):
    return min(pages, max(1, LANES // page_len))


def score_kernel(steps, has_earlier, chosen, member_ref, turned_ref, keys_ref, *refs):
    if has_earlier:
        early_max_ref, early_total_ref = refs[:2]
        refs = refs[2:]
    weights_ref, fresh_ref, max_ref, total_ref, scores, fresh_scores = refs
    row_lines, query_width = turned_ref.shape[0], chosen.shape[1]
    group = query_width // HD
    page_len = keys_ref.shape[1]
    batch = weights_ref.shape[2] // page_len
    blocks, lines = weights_ref.shape[0], batch * steps
    pages = blocks * batch
    spare = member_ref.shape[0] - pages * steps - page_len
    scale = HD ** (-0.5)
    lane = lax.broadcasted_iota(jnp.int32, (1, LANES), 1)
    member, turned = member_ref[...], turned_ref[...]
    is_member = turned > 0

    line = lax.broadcasted_iota(jnp.int32, (group * lines, batch * page_len), 0)
    token = lax.broadcasted_iota(jnp.int32, (group * lines, batch * page_len), 1)
    page_mask = (line % lines) // steps == token // page_len
    line = lax.broadcasted_iota(jnp.int32, (group * page_len, page_len), 0) % page_len
    token = lax.broadcasted_iota(jnp.int32, (group * page_len, page_len), 1)
    fresh_mask = (line // steps == token // steps) & (token % steps <= line % steps)

    def score(first_line, count, keys, mask):
        rows = slice(first_line, first_line + count)
        queries = jnp.concatenate(
            [chosen[rows, g * HD : (g + 1) * HD] for g in range(group)], axis=0
        )
        found = lax.dot_general(
            queries, keys, (((1,), (1,)), ((), ())), preferred_element_type=jnp.float32
        )
        found = jnp.where(mask, found * scale, NEGATIVE)
        largest = jnp.max(found, axis=1, keepdims=True)
        block_max = jnp.zeros((count, LANES), jnp.float32)
        for g in range(group):
            block_max = jnp.where(lane == g, largest[g * count : (g + 1) * count], block_max)
        return found, block_max

    maxima = []
    for block in range(blocks):
        keys = keys_ref[block * batch : (block + 1) * batch].reshape(batch * page_len, HD)
        scores[block], block_max = score(block * lines, lines, keys, page_mask)
        maxima.append(block_max)
    fresh_scores[...], block_max = score(pages * steps, page_len, keys_ref[pages], fresh_mask)
    maxima.append(block_max)
    if spare:
        maxima.append(jnp.zeros((spare, LANES), jnp.float32))

    line_max = jnp.transpose(jnp.concatenate(maxima, axis=0))
    row_max = jnp.full((row_lines, LANES), NEGATIVE, jnp.float32)
    for g in range(group):
        best = jnp.max(
            jnp.where(is_member, line_max[g : g + 1, :], NEGATIVE), axis=1, keepdims=True
        )
        row_max = jnp.where(lane == g, best, row_max)
    if has_earlier:
        row_max = jnp.maximum(row_max, early_max_ref[...])
    spread = jnp.dot(
        member, row_max, precision=HIGHEST, preferred_element_type=jnp.float32
    )

    def weigh(first_line, count, found, mask):
        rows = spread[first_line : first_line + count]
        shift = jnp.concatenate([rows[:, g : g + 1] for g in range(group)], axis=0)
        weights = jnp.where(mask, jnp.exp(jnp.minimum(found - shift, 0.0)), 0.0)
        weights = weights.astype(jnp.bfloat16)
        ones = jnp.ones((weights.shape[1], LANES), jnp.bfloat16)
        total = jnp.dot(weights, ones, preferred_element_type=jnp.float32)
        block_total = jnp.zeros((count, LANES), jnp.float32)
        for g in range(group):
            block_total = jnp.where(lane == g, total[g * count : (g + 1) * count], block_total)
        return weights, block_total

    totals = []
    for block in range(blocks):
        weights_ref[block], total = weigh(block * lines, lines, scores[block], page_mask)
        totals.append(total)
    fresh_ref[...], total = weigh(pages * steps, page_len, fresh_scores[...], fresh_mask)
    totals.append(total)
    if spare:
        totals.append(jnp.zeros((spare, LANES), jnp.float32))
    row_total = jnp.dot(
        turned,
        jnp.concatenate(totals, axis=0),
        precision=HIGHEST,
        preferred_element_type=jnp.float32,
    )
    if has_earlier:
        row_total = row_total + early_total_ref[...] * jnp.exp(early_max_ref[...] - row_max)
    max_ref[...] = row_max
    total_ref[...] = row_total


def score(choice, keys, steps, earlier=(), flops=0):
    (member_lines, query_width), row_lines = choice[0].shape, choice[2].shape[0]
    group = query_width // HD
    page_len = keys.shape[1]
    pages = (member_lines - round_up(page_len, LANES)) // steps
    batch = page_batch(pages, page_len)
    blocks = pages // batch
    shapes = ((blocks, group * batch * steps, batch * page_len), (group * page_len, page_len))
    stat = jax.ShapeDtypeStruct((row_lines, LANES), jnp.float32)
    operands = (*choice, keys, *earlier)
    return call(
        functools.partial(score_kernel, steps, bool(earlier)),
        operands,
        [vmem()] * len(operands),
        flops=flops,
        out_specs=[vmem()] * 4,
        out_shape=[jax.ShapeDtypeStruct(shape, jnp.bfloat16) for shape in shapes] + [stat, stat],
        scratch_shapes=[pltpu.VMEM(shape, jnp.float32) for shape in shapes],
        compiler_params=params(12),
        name="score",
    )


def value_kernel(steps, chunk, chunks, has_earlier, has_notes, last, *refs):
    weights_ref, fresh_ref, turned_ref, values_ref, max_ref, total_ref = refs[:6]
    refs = refs[6:]
    if has_earlier:
        early_max_ref, early_numer_ref = refs[:2]
        refs = refs[2:]
    if has_notes:
        own_keys_ref, near_keys_ref = refs[:2]
        refs = refs[2:]
    out_ref, high, low = refs
    row_lines, member_lines = turned_ref.shape
    page_len = values_ref.shape[1]
    blocks, batch = weights_ref.shape[0], weights_ref.shape[2] // page_len
    lines, pages = batch * steps, blocks * batch
    all_groups = weights_ref.shape[1] // lines
    group = all_groups // chunks
    first = chunk * group
    used = pages * steps + page_len

    def gain(first_line, count, weights, values):
        numer = jnp.dot(weights, values, preferred_element_type=jnp.float32)
        rounded = numer.astype(jnp.bfloat16)
        rest = (numer - rounded.astype(jnp.float32)).astype(jnp.bfloat16)
        for g in range(group):
            part = slice(g * count, (g + 1) * count)
            columns = slice(g * HD, (g + 1) * HD)
            high[first_line : first_line + count, columns] = rounded[part]
            low[first_line : first_line + count, columns] = rest[part]

    for block in range(blocks):
        weights = weights_ref[block, first * lines : (first + group) * lines]
        values = values_ref[block * batch : (block + 1) * batch].reshape(batch * page_len, HD)
        gain(block * lines, lines, weights, values)
    weights = fresh_ref[first * page_len : (first + group) * page_len]
    gain(pages * steps, page_len, weights, values_ref[pages])
    if member_lines > used:
        high[used:, :] = jnp.zeros((member_lines - used, group * HD), jnp.bfloat16)
        low[used:, :] = jnp.zeros((member_lines - used, group * HD), jnp.bfloat16)

    lane = lax.broadcasted_iota(jnp.int32, (1, LANES), 1)
    row_max, row_total = max_ref[...], total_ref[...]
    present = row_total > 0
    inverse = jnp.where(present, 1.0 / jnp.where(present, row_total, 1.0), 0.0)
    if has_earlier:
        scale_early = jnp.exp(early_max_ref[...] - row_max)
    if last and chunk == 0:
        log_sum = jnp.where(
            present & (lane < all_groups),
            row_max + jnp.log(jnp.where(present, row_total, 1.0)),
            jnp.where(lane < all_groups, NEGATIVE, 0.0),
        )
        lanes = split_sums(log_sum, all_groups)
        if has_notes:
            lanes = lanes + owner_notes(
                own_keys_ref[pages + 1], near_keys_ref[pages + 1], row_lines, 3 * all_groups
            )
        out_ref[:, group * HD :] = lanes.astype(jnp.bfloat16)
    turned = turned_ref[...].astype(jnp.bfloat16)
    for g in range(group):
        columns = slice(g * HD, (g + 1) * HD)
        which = slice(first + g, first + g + 1)
        numer = jnp.dot(turned, high[:, columns], preferred_element_type=jnp.float32) + jnp.dot(
            turned, low[:, columns], preferred_element_type=jnp.float32
        )
        if has_earlier:
            early = early_numer_ref[:, (first + g) * HD : (first + g + 1) * HD]
            numer = numer + early * scale_early[:, which]
        if last:
            numer = numer * inverse[:, which]
        out_ref[:, columns] = numer.astype(out_ref.dtype)


def value(scored, turned, values, steps, chunk, chunks, last, earlier=(), notes=(), follows=()):
    row_lines, member_lines = turned.shape
    page_len = values.shape[1]
    group = scored[1].shape[0] // page_len // chunks
    wide = group * HD + (LANES if last and chunk == 0 else 0)
    operands = (*scored[:2], turned, values, *scored[2:], *earlier, *notes)
    return call(
        functools.partial(value_kernel, steps, chunk, chunks, bool(earlier), bool(notes), last),
        operands,
        [vmem()] * len(operands),
        follows,
        out_specs=vmem(),
        out_shape=jax.ShapeDtypeStruct(
            (row_lines, wide), jnp.bfloat16 if last else jnp.float32
        ),
        scratch_shapes=[pltpu.VMEM((member_lines, group * HD), jnp.bfloat16)] * 2,
        compiler_params=params(8),
        name="value",
    )


def split_sums(value, group):
    first = value.astype(jnp.bfloat16).astype(jnp.float32)
    rest = value - first
    second = rest.astype(jnp.bfloat16).astype(jnp.float32)
    third = rest - second
    return first + pltpu.roll(second, group, axis=1) + pltpu.roll(third, 2 * group, axis=1)


def owner_notes(own, near_page, row_lines, first_lane):
    lines = near_page.shape[0]
    notes = jnp.concatenate(
        [
            own.astype(jnp.float32),
            near_page.astype(jnp.float32),
            jnp.zeros((row_lines - 2 * lines, LANES), jnp.float32),
        ]
    )
    return pltpu.roll(notes, first_lane, axis=1)


def join_sums(parts, group):
    parts = parts.astype(jnp.float32)
    return (
        parts
        + pltpu.roll(parts, LANES - group, axis=1)
        + pltpu.roll(parts, LANES - 2 * group, axis=1)
    )


def combine_kernel(group, first, sums_ref, their_sums_ref, mine_ref, theirs_ref, out_ref):
    sums = join_sums(sums_ref[:, -LANES:], group)
    their_sums = join_sums(their_sums_ref[:, -LANES:], group)
    largest = jnp.maximum(sums, their_sums)
    weight = jnp.exp(sums - largest)
    their_weight = jnp.exp(their_sums - largest)
    inverse = 1.0 / (weight + their_weight)
    weight = weight * inverse
    their_weight = their_weight * inverse
    for place in range(out_ref.shape[1] // HD):
        g = first + place
        columns = slice(place * HD, (place + 1) * HD)
        out_ref[:, columns] = (
            mine_ref[:, columns].astype(jnp.float32) * weight[:, g : g + 1]
            + theirs_ref[:, columns].astype(jnp.float32) * their_weight[:, g : g + 1]
        ).astype(jnp.bfloat16)


def combine(mine, theirs, chunk, follows=()):
    row_lines, width = mine[0].shape
    width -= LANES
    group = width // HD * len(mine)
    return call(
        functools.partial(combine_kernel, group, chunk * width // HD),
        (mine[0], theirs[0], mine[chunk], theirs[chunk]),
        [vmem()] * 4,
        follows,
        out_specs=vmem(),
        out_shape=jax.ShapeDtypeStruct((row_lines, width), jnp.bfloat16),
        compiler_params=params(4),
        name="combine",
    )


def block_row(own, chunk, chunks, head_count, depth):
    head = lax.rem(lax.axis_index("tp") + (0 if own else 1), head_count)
    return pl.multiple_of((head * chunks + chunk) * depth, depth)


def fetch_kernel(blocks, chunks, head_count, weight_ref, held_ref, done_ref, arrived):
    depth = held_ref.shape[0] // len(blocks)
    pieces = arrived.shape[0] // len(blocks)
    size = depth // pieces
    copies = []
    for place, (own, chunk) in enumerate(blocks):
        base = block_row(own, chunk, chunks, head_count, depth)
        for piece in range(pieces):
            copies.append(
                pltpu.make_async_copy(
                    weight_ref.at[pl.ds(pl.multiple_of(base + piece * size, size), size)],
                    held_ref.at[pl.ds(place * depth + piece * size, size)],
                    arrived.at[place * pieces + piece],
                )
            )
    for copy in copies:
        copy.start()
    done_ref[...] = jnp.zeros_like(done_ref)
    for copy in copies:
        copy.wait()


def fetch(weight, blocks, chunks, head_count, depth, follows):
    pieces = 4
    return call(
        functools.partial(fetch_kernel, blocks, chunks, head_count),
        in_hbm(weight),
        [hbm()],
        follows,
        out_specs=(vmem(), vmem()),
        out_shape=(
            pltpu.VMEM((len(blocks) * depth, weight.shape[1]), weight.dtype),
            jax.ShapeDtypeStruct((8, LANES), jnp.float32),
        ),
        scratch_shapes=[pltpu.SemaphoreType.DMA((len(blocks) * pieces,))],
        compiler_params=params(1),
        name="fetch",
    )


def project_kernel(parts, has_total, chunk_lines, first, offsets, chunks, head_count, *refs):
    input_refs, weight_ref, refs = refs[:parts], refs[parts], refs[parts + 1 :]
    streamed = offsets is None
    if streamed:
        held, arrived = refs[-2:]
        refs = refs[:-2]
    outs = refs[1:] if has_total else refs
    depth, width = input_refs[0].shape[1], outs[0].shape[-1]
    block = min(width, 512)
    count = width // block

    def piece(index):
        return pltpu.make_async_copy(
            weight_ref.at[
                pl.ds(block_row(True, 0, chunks, head_count, depth), depth),
                pl.ds(first + index * block, block),
            ],
            held.at[:, pl.ds(index * block, block)],
            arrived.at[index],
        )

    if streamed:
        for index in range(count):
            piece(index).start()
    for index in range(count):
        start = index * block
        columns = slice(first + start, first + start + block)
        product = refs[0][:, columns] if has_total else 0.0
        if streamed:
            piece(index).wait()
            product = product + jnp.dot(
                input_refs[0][...],
                held[:, start : start + block],
                preferred_element_type=jnp.float32,
            )
        else:
            for input_ref, offset in zip(input_refs, offsets):
                product = product + jnp.dot(
                    input_ref[...],
                    weight_ref[offset * depth : (offset + 1) * depth, columns],
                    preferred_element_type=jnp.float32,
                )
        if chunk_lines is None:
            outs[0][:, start : start + block] = product
            continue
        core = lax.rem(lax.axis_index("kv"), 2)
        keep_ref, send_ref = outs
        for pair in range(keep_ref.shape[0]):
            even = product[2 * pair * chunk_lines : (2 * pair + 1) * chunk_lines]
            odd = product[(2 * pair + 1) * chunk_lines : (2 * pair + 2) * chunk_lines]
            keep_ref[pair, :, start : start + block] = jnp.where(core == 0, even, odd)
            send_ref[pair, :, start : start + block] = jnp.where(core == 0, odd, even).astype(
                send_ref.dtype
            )


def project(inputs, weight, offsets, chunks, head_count, total, columns, chunk_lines, follows=()):
    row_lines, depth = inputs[0].shape
    first, width = columns
    in_specs = [vmem()] * len(inputs) + [hbm() if offsets is None else vmem()]
    operands = [*inputs, *(in_hbm(weight) if offsets is None else [weight])]
    if total is not None:
        in_specs.append(vmem())
        operands.append(total)
    if chunk_lines is None:
        out_shape = jax.ShapeDtypeStruct((row_lines, width), jnp.float32)
        out_specs = vmem()
    else:
        pairs = row_lines // (2 * chunk_lines)
        shape = (pairs, chunk_lines, width)
        out_shape = (
            jax.ShapeDtypeStruct(shape, jnp.float32),
            jax.ShapeDtypeStruct(shape, jnp.bfloat16),
        )
        out_specs = (vmem(), vmem())
    scratch = []
    if offsets is None:
        scratch = [
            pltpu.VMEM((depth, width), weight.dtype),
            pltpu.SemaphoreType.DMA((max(1, width // 512),)),
        ]
    return call(
        functools.partial(
            project_kernel,
            len(inputs),
            total is not None,
            chunk_lines,
            first,
            offsets,
            chunks,
            head_count,
        ),
        operands,
        in_specs,
        follows,
        out_specs=out_specs,
        out_shape=out_shape,
        scratch_shapes=scratch,
        compiler_params=params(16 if offsets is None else 8),
        name="project",
    )


def add_core_kernel(keep_ref, got_ref, own_ref, *send_refs):
    half = lax.axis_index("kv") // 2
    own_ref[...] = keep_ref[half] + got_ref[half].astype(jnp.float32)
    for step, send_ref in enumerate(send_refs, 1):
        part = keep_ref[half ^ step] + got_ref[half ^ step].astype(jnp.float32)
        send_ref[...] = part.astype(send_ref.dtype)


def sum_heads(keep, send, kv_size):
    got = lax.ppermute(send, "kv", flip(kv_size, 1))
    shape = keep.shape[1:]
    own, *sends = call(
        add_core_kernel,
        (keep, got),
        [vmem(), vmem()],
        out_specs=[vmem()] * (kv_size // 2),
        out_shape=[jax.ShapeDtypeStruct(shape, jnp.float32)]
        + [jax.ShapeDtypeStruct(shape, jnp.bfloat16)] * (kv_size // 2 - 1),
        compiler_params=params(4),
        name="add_core",
    )
    return [own] + [
        lax.ppermute(part, "kv", flip(kv_size, 2 * step)) for step, part in enumerate(sends, 1)
    ]


def finish_kernel(pieces, *refs):
    parts, out_ref, done_ref = refs[:-2], refs[-2], refs[-1]
    done_ref[...] = jnp.zeros_like(done_ref)
    each = len(parts) // pieces
    steps, width = out_ref.shape[1], out_ref.shape[2] // pieces
    for piece in range(pieces):
        total = parts[piece * each][...]
        for part in parts[piece * each + 1 : (piece + 1) * each]:
            total = total + part[...].astype(jnp.float32)
        out_ref[:, :, piece * width : (piece + 1) * width] = total.astype(jnp.bfloat16).reshape(
            -1, steps, width
        )


def finish(results, steps):
    lines, width = results[0][0].shape
    parts = [part for pieces in results for part in pieces]
    return call(
        functools.partial(finish_kernel, len(results)),
        parts,
        [vmem()] * len(parts),
        out_specs=(vmem(), vmem()),
        out_shape=(
            jax.ShapeDtypeStruct((lines // steps, steps, width * len(results)), jnp.bfloat16),
            jax.ShapeDtypeStruct((8, LANES), jnp.float32),
        ),
        compiler_params=params(4),
        name="finish",
    )


def body(
    queries, fresh_keys, fresh_values, cache_keys, cache_values, page_counts, page_owner, out_weight
):
    tp_size, kv_size = lax.axis_size("tp"), lax.axis_size("kv")
    head_count, pages_here, page_width = cache_keys.shape
    row_count, step_count, query_width = queries.shape
    own_lines = fresh_keys.shape[0] * step_count
    page_len = page_width // HD
    row_lines = row_count * step_count
    head_width = query_width // head_count
    group = head_width // HD
    cap = max(2, (2 * pages_here + tp_size - 1) // tp_size)
    out_width = out_weight.shape[1]
    chunk_lines = row_lines // kv_size
    caches = (cache_keys, cache_values)
    fresh = (fresh_keys, fresh_values)

    paired = head_count == 2 and tp_size == 4 and group % 2 == 0 and cap % 16 == 0
    paired = paired and 3 * group + pages_here <= LANES and 2 * page_len <= row_lines
    chunks = 2 if paired else 1
    part = head_width // chunks
    everything = (0, out_width)

    if paired:
        keys, values, send_last = gather_tokens(1, caches, fresh, page_owner, handing=3, cap=cap)
        near_keys = lax.ppermute(keys, "tp", flip(tp_size, 1))
        got_inner = lax.ppermute(send_last, "tp", [(1, 2), (2, 1)])
        own_keys, own_values, query, bounds = gather_tokens(
            0, caches, fresh, page_owner, queries, page_counts, follows=(send_last,)
        )
        near_values = lax.ppermute(tie(values, bounds), "tp", flip(tp_size, 1))
        own_choice, near_choice = prepare(
            bounds, query, (0, 1), pages_here, page_len, own_lines, step_count
        )
        scored = score(own_choice, own_keys, step_count)
        early_numer = value(scored, own_choice[2], own_values, step_count, 0, 1, False)
        early_max, early_total = scored[2:]
        scored = score(near_choice, near_keys, step_count, (early_max, early_total), 1 << 34)
        payload = [
            value(
                scored,
                near_choice[2],
                near_values,
                step_count,
                chunk,
                chunks,
                True,
                (early_max, early_numer),
                () if chunk else (own_keys, near_keys),
            )
            for chunk in range(chunks)
        ]
        jobs = ((2, True), (1, False), (0, True))
        send_far, send_near, kept = place_pages(
            page_owner, caches, jobs, cap, tp_size, False, (payload[1],)
        )
        blocks = ((True, 1), (False, 0))
        held, held_done = fetch(out_weight, blocks, chunks, head_count, part, payload[1:])
        payload[1] = tie(payload[1], held_done)
        held_last, held_done = fetch(
            out_weight, ((False, 1),), chunks, head_count, part, (held_done,)
        )
        theirs = [lax.ppermute(p, "tp", flip(tp_size, 2)) for p in payload]
        got_near = lax.ppermute(tie(send_near, held_done), "tp", flip(tp_size, 1))
        near_pages = place_near(near_keys, near_values, head_count, cap, tp_size)
        first_part = combine(payload, theirs, 0)
        near_first = lax.ppermute(first_part, "tp", flip(tp_size, 1))
        total = project([first_part], out_weight, None, chunks, head_count, None, everything, None)
        got_far = lax.ppermute(tie(send_far, total), "tp", flip(tp_size, 2))
        got_outer = lax.ppermute(tie(send_last, total), "tp", [(0, 3), (3, 0)])
        second_part = combine(payload, theirs, 1, (got_near, total, got_inner))
        near_second = lax.ppermute(second_part, "tp", flip(tp_size, 1))
        own_parts, near_parts = (first_part, second_part), (near_first, near_second)
        plan = ((0, None, None), (1, None, 0), (1, None, 1), (3, (1, 2), None))
        *settled, settled_done = settle(
            [kept, near_pages, got_near, got_inner], plan, head_count, tp_size * cap, (), (total,)
        )
        total = project(
            [own_parts[1], near_parts[0]],
            held,
            (0, 1),
            chunks,
            head_count,
            total,
            everything,
            None,
            (settled_done,),
        )
        results = []
        for first in (0, out_width // 2):
            columns = (first, out_width // 2)
            keep, send = project(
                [near_parts[1]],
                held_last,
                (0,),
                chunks,
                head_count,
                total,
                columns,
                chunk_lines,
            )
            results.append(sum_heads(keep, send, kv_size))
        attention_out, finished = finish(results, step_count)
        slot_rows = slot_rows_near(
            bounds,
            payload[0],
            theirs[0],
            pages_here,
            3 * group,
            page_len,
            cap,
            (head_count, tp_size * cap),
            step_count,
            (results[1][0],),
        )
        plan = ((2, None, None), (3, (0, 3), None))
        slot_keys, slot_values, _ = settle(
            [got_far, got_outer], plan, head_count, tp_size * cap, settled, (finished,)
        )
        return (attention_out, slot_keys, slot_values, slot_rows)

    def hand_over(cache):
        jobs = tuple((d, True) for d in range(tp_size))
        sent = place_pages(page_owner, (cache,), jobs, cap, tp_size, True)
        got = lax.all_to_all(
            jnp.concatenate(sent), "tp", split_axis=0, concat_axis=0, tiled=True
        )
        return got.transpose(1, 0, 2, 3).reshape(head_count, tp_size * cap, page_width)

    slot_keys, slot_values = hand_over(cache_keys), hand_over(cache_values)
    slot_rows = slot_rows_gathered(page_owner, page_counts, cap)
    attended = []
    for head in range(head_count):
        cut = slice(head, head + 1)
        lanes = slice(head * HD, (head + 1) * HD)
        keys, values, query, bounds = gather_tokens(
            0,
            [cache[cut] for cache in caches],
            [new[:, :, lanes] for new in fresh],
            page_owner[cut],
            queries[:, :, head * head_width : (head + 1) * head_width],
            page_counts,
        )
        (choice,) = prepare(
            bounds, query, (0,), pages_here, page_len, own_lines, step_count
        )
        scored = score(choice, keys, step_count)
        payload = value(scored, choice[2], values, step_count, 0, 1, True)
        raw = payload[:, part:].astype(jnp.float32)
        sums = raw[:, :group] + raw[:, group : 2 * group] + raw[:, 2 * group : 3 * group]
        weight = jnp.exp(sums - lax.pmax(sums, "tp"))
        numer = payload[:, :part].astype(jnp.float32).reshape(row_lines, group, HD)
        numer = lax.psum(numer * weight[..., None], "tp")
        joined = numer / lax.psum(weight, "tp")[..., None]
        attended.append(joined.reshape(row_lines, head_width).astype(jnp.bfloat16))
    keep, send = project(
        [jnp.concatenate(attended, axis=1)], out_weight, None, 1, 1, None, everything, chunk_lines
    )
    attention_out, _ = finish([sum_heads(keep, send, kv_size)], step_count)
    return (attention_out, slot_keys, slot_values, slot_rows)


def solution(mesh):
    return jax.shard_map(
        body,
        mesh=mesh,
        in_specs=(
            P("grp", None, "kv"),
            P(("grp", "tp"), None, "kv"),
            P(("grp", "tp"), None, "kv"),
            P(("grp", "kv"), "tp", None),
            P(("grp", "kv"), "tp", None),
            P("grp"),
            P(("grp", "kv"), "tp"),
            P("kv", "tp"),
        ),
        out_specs=(
            P(("grp", "kv"), None, "tp"),
            P(("grp", "kv"), "tp", None),
            P(("grp", "kv"), "tp", None),
            P(("grp", "kv"), "tp"),
        ),
        check_vma=False,
    )
```

```python
import functools

import jax
import jax.numpy as jnp
from jax import lax
from jax.experimental import pallas as pl
from jax.experimental.pallas import tpu as pltpu
from jax.sharding import PartitionSpec as P

HD = 128
LANES = 128
NEGATIVE = -1e30
HIGHEST = lax.Precision.HIGHEST
MIB = 1024 * 1024


def round_up(value, step):
    return -(-value // step) * step


def flip(size, bit):
    return [(i, i ^ bit) for i in range(size)]


def params(mib):
    return pltpu.CompilerParams(vmem_limit_bytes=mib * MIB)


def in_hbm(*arrays):
    return [pltpu.with_memory_space_constraint(array, pltpu.HBM) for array in arrays]


def vmem():
    return pl.BlockSpec(memory_space=pltpu.VMEM)


def hbm():
    return pl.BlockSpec(memory_space=pltpu.HBM)


def anywhere():
    return pl.BlockSpec(memory_space=pl.ANY)


def call(kernel, operands, in_specs, follows=(), flops=0, **rest):
    count, extra = len(operands), len(follows)

    def without_extra(*refs):
        kernel(*refs[:count], *refs[count + extra :])

    return pl.pallas_call(
        without_extra,
        in_specs=list(in_specs) + [anywhere()] * extra,
        cost_estimate=pl.CostEstimate(flops=flops, bytes_accessed=0, transcendentals=0),
        **rest,
    )(*operands, *follows)


def tie(value, *follows):
    return call(
        lambda value_ref, out_ref: None,
        (value,),
        [anywhere()],
        follows,
        out_specs=anywhere(),
        out_shape=jax.ShapeDtypeStruct(value.shape, value.dtype),
        input_output_aliases={0: 0},
        compiler_params=params(1),
        name="tie",
    )


def earlier_pages(page_count):
    first = lax.broadcasted_iota(jnp.int32, (page_count, page_count), 0)
    second = lax.broadcasted_iota(jnp.int32, (page_count, page_count), 1)
    return (first < second).astype(jnp.bfloat16)


def rank_pages(away, earlier, dest_rows):
    ways = lax.broadcasted_iota(jnp.int32, (dest_rows, away.shape[1]), 0)
    listed = (ways == away).astype(jnp.float32)
    before = jnp.dot(listed.astype(jnp.bfloat16), earlier, preferred_element_type=jnp.float32)
    return jnp.sum(before * listed, axis=0, keepdims=True).astype(jnp.int32)


def slot_picks(owners, me, distances, cap, tp_size):
    head_count, page_count = owners.shape
    earlier = earlier_pages(page_count)
    row = lax.broadcasted_iota(jnp.int32, (cap, page_count), 0)
    picks = []
    for head in range(head_count):
        away = owners[head : head + 1, :] ^ me
        rank = rank_pages(away, earlier, round_up(tp_size, 8))
        picks.append([((away == d) & (rank == row)).astype(jnp.float32) for d in distances])
    return picks


def place_rows(pages_ref, pick, targets):
    width, cap = pages_ref.shape[1], pick[0].shape[0]
    step = min(width, 1024)
    for start in range(0, width, step):
        columns = slice(start, start + step)
        placed = jnp.dot(
            jnp.concatenate(pick).astype(jnp.bfloat16),
            pages_ref[:, columns],
            preferred_element_type=jnp.float32,
        ).astype(jnp.bfloat16)
        for which, target in enumerate(targets):
            target[:, columns] = placed[which * cap : (which + 1) * cap]


def place_kernel(cap, jobs, by_index, tp_size, owner_ref, *refs):
    count = (len(refs) - 2 - len(jobs)) // 2
    sources, targets = refs[:count], refs[count : count + len(jobs)]
    held, owners, arrived = refs[count + len(jobs) : -2], refs[-2], refs[-1]
    head_count = sources[0].shape[0]
    copies = [
        pltpu.make_async_copy(source, target, arrived.at[i])
        for i, (source, target) in enumerate(zip((owner_ref, *sources), (owners, *held)))
    ]
    for copy in copies:
        copy.start()
    copies[0].wait()
    me = 0 if by_index else lax.axis_index("tp")
    own_head = lax.rem(me, head_count)
    picks = slot_picks(owners, me, [d for d, _ in jobs], cap, tp_size)

    def place(index, head, pick, target_of):
        place_rows(held[index].at[head], pick, target_of)

    shared = [i for i, (_, every) in enumerate(jobs) if every]
    single = [i for i, (_, every) in enumerate(jobs) if not every]
    for index in range(count):
        copies[index + 1].wait()
        for head in range(head_count):
            if shared:
                pick = [picks[head][i] for i in shared]
                place(index, head, pick, [targets[i].at[index, head] for i in shared])
        if single:
            pick = []
            for i in single:
                chosen = picks[0][i]
                for head in range(1, head_count):
                    chosen = jnp.where(own_head == head, picks[head][i], chosen)
                pick.append(chosen)
            place(index, own_head, pick, [targets[i].at[index] for i in single])


def place_pages(page_owner, caches, jobs, cap, tp_size, by_index, follows=()):
    head_count, page_count, width = caches[0].shape
    return call(
        functools.partial(place_kernel, cap, jobs, by_index, tp_size),
        in_hbm(page_owner, *caches),
        [hbm()] * (1 + len(caches)),
        follows,
        out_specs=tuple(vmem() for _ in jobs),
        out_shape=tuple(
            jax.ShapeDtypeStruct(
                (len(caches),) + ((head_count,) if every else ()) + (cap, width), jnp.bfloat16
            )
            for _, every in jobs
        ),
        scratch_shapes=[pltpu.VMEM(cache.shape, cache.dtype) for cache in caches]
        + [
            pltpu.VMEM(page_owner.shape, jnp.int32),
            pltpu.SemaphoreType.DMA((1 + len(caches),)),
        ],
        compiler_params=params(8),
        name="place_pages",
    )


def place_near_kernel(tp_size, head_count, keys_ref, values_ref, out_ref):
    cap, width = out_ref.shape[1:]
    pages, page_len = values_ref.shape[0] - 1, values_ref.shape[1]
    me = lax.axis_index("tp")
    head = lax.rem(me, head_count)
    lists = keys_ref[pages + 1].astype(jnp.float32)[:, :pages].astype(jnp.int32)
    owner = lists[0:1]
    for which in range(1, head_count):
        owner = jnp.where(head == which, lists[which : which + 1], owner)
    rank = rank_pages(owner, earlier_pages(pages), round_up(tp_size, 8))
    row = lax.broadcasted_iota(jnp.int32, (cap, pages), 0)
    pick = ((owner == me) & (rank == row)).astype(jnp.bfloat16)
    for index, source in enumerate((keys_ref, values_ref)):
        paged = source[:pages].reshape(pages, page_len * HD)
        out_ref[index] = jnp.dot(pick, paged, preferred_element_type=jnp.float32).astype(
            jnp.bfloat16
        )


def place_near(keys, values, head_count, cap, tp_size):
    page_len = keys.shape[1]
    return call(
        functools.partial(place_near_kernel, tp_size, head_count),
        (keys, values),
        [vmem()] * 2,
        out_specs=vmem(),
        out_shape=jax.ShapeDtypeStruct((2, cap, page_len * HD), jnp.bfloat16),
        compiler_params=params(8),
        name="place_near",
    )


def settle_kernel(plan, *refs):
    count = len(plan)
    parts, arrived = refs[:count], refs[-1]
    key_ref, value_ref, done_ref = refs[-4:-1]
    head_count, cap = key_ref.shape[0], parts[0].shape[-2]
    me = lax.axis_index("tp")

    def copies_of(place):
        distance, _, other = plan[place]
        first = pl.multiple_of((me ^ distance) * cap, cap)
        copies = []
        for index, target in enumerate((key_ref, value_ref)):
            for head in range(head_count if other is None else 1):
                source = parts[place].at[index]
                if other is None:
                    source = source.at[head]
                else:
                    head = lax.rem(me + other, head_count)
                copies.append(
                    pltpu.make_async_copy(
                        source,
                        target.at[head, pl.ds(first, cap)],
                        arrived.at[place * 2 * head_count + len(copies)],
                    )
                )
        return copies

    def move(place, action):
        holders = plan[place][1]
        if holders is None:
            for copy in copies_of(place):
                action(copy)
            return
        holds = functools.reduce(lambda a, b: a | b, [me == holder for holder in holders])

        @pl.when(holds)
        def _():
            for copy in copies_of(place):
                action(copy)

    for place in range(count):
        move(place, lambda copy: copy.start())
    done_ref[...] = jnp.zeros_like(done_ref)
    for place in range(count):
        move(place, lambda copy: copy.wait())


def settle(parts, plan, head_count, slots, settled=(), follows=()):
    width = parts[0].shape[-1]
    shape = jax.ShapeDtypeStruct((head_count, slots, width), jnp.bfloat16)
    count = len(parts)
    return call(
        functools.partial(settle_kernel, plan),
        (*parts, *settled),
        [vmem()] * count + [hbm()] * len(settled),
        follows,
        out_specs=(hbm(), hbm(), vmem()),
        out_shape=(shape, shape, jax.ShapeDtypeStruct((8, LANES), jnp.float32)),
        input_output_aliases={count: 0, count + 1: 1} if settled else {},
        scratch_shapes=[pltpu.SemaphoreType.DMA((2 * count * head_count,))],
        compiler_params=params(6),
        name="settle",
    )


def slot_rows_kernel(
    cap, pages, first_lane, page_len, steps, bounds_ref, own_ref, far_ref, out_ref
):
    head_count, slots = out_ref.shape
    tp_size = slots // cap
    me = lax.axis_index("tp")
    earlier = earlier_pages(pages)
    ends = bounds_ref[1:2, :]
    ids = lax.broadcasted_iota(jnp.int32, (pages, ends.shape[1]), 0)
    row = lax.broadcasted_iota(jnp.int32, (cap, pages), 0)
    ones = jnp.ones((8, ends.shape[1]), jnp.bfloat16)
    lines = [[] for _ in range(head_count)]
    for distance in range(tp_size):
        block = me ^ distance
        marks = lax.dot_general(
            ones,
            (ends <= block * pages + ids).astype(jnp.bfloat16),
            (((1,), (1,)), ((), ())),
            preferred_element_type=jnp.float32,
        )
        marks = marks / steps + 1
        source = own_ref if distance < 2 else far_ref
        line = (distance % 2) * page_len
        notes = source[line : line + page_len, -LANES:].astype(jnp.float32)
        notes = pltpu.roll(notes, LANES - first_lane, axis=1)
        for head in range(head_count):
            owner = notes[head : head + 1, :pages].astype(jnp.int32)
            rank = rank_pages(owner, earlier, round_up(tp_size, 8))
            pick = ((owner == me) & (rank == row)).astype(jnp.bfloat16)
            found = lax.dot_general(
                marks.astype(jnp.bfloat16),
                pick,
                (((1,), (1,)), ((), ())),
                preferred_element_type=jnp.float32,
            )
            found = jnp.concatenate([found, jnp.zeros((8, LANES - cap), jnp.float32)], axis=1)
            lines[head].append(pltpu.roll(found, block * cap, axis=1)[:1])
    for head in range(head_count):
        total = lines[head][0]
        for line in lines[head][1:]:
            total = total + line
        out_ref[head : head + 1, :] = total[:, :slots].astype(jnp.int32) - 1


def slot_rows_near(bounds, own, far, pages, first_lane, page_len, cap, shape, steps, follows):
    return call(
        functools.partial(slot_rows_kernel, cap, pages, first_lane, page_len, steps),
        (bounds, own, far),
        [vmem()] * 3,
        follows,
        out_specs=vmem(),
        out_shape=jax.ShapeDtypeStruct(shape, jnp.int32),
        compiler_params=params(2),
        name="slot_rows",
    )


def slot_rows_gathered(page_owner, page_counts, cap):
    owners = lax.all_gather(page_owner, "tp", axis=0, tiled=False)
    tp_size, head_count, pages_here = owners.shape
    rows = jnp.arange(page_counts.shape[0], dtype=jnp.int32)
    row_ends = jnp.sum(jnp.where(rows[None, :] <= rows[:, None], page_counts[None, :], 0), axis=1)
    ids = jnp.arange(pages_here, dtype=jnp.int32)
    same = (owners[..., :, None] == owners[..., None, :]) & (ids[:, None] < ids[None, :])
    rank = jnp.sum(same.astype(jnp.int32), axis=2)
    blocks = jnp.arange(tp_size, dtype=jnp.int32)
    page_ids = blocks[:, None] * pages_here + ids
    page_row = jnp.sum((row_ends <= page_ids[..., None]).astype(jnp.int32), axis=-1)
    slot = jnp.where(owners == lax.axis_index("tp"), blocks[:, None, None] * cap + rank, -1)
    slot_ids = jnp.arange(tp_size * cap, dtype=jnp.int32)
    marks = jnp.where(slot[..., None] == slot_ids, page_row[:, None, :, None] + 1, 0)
    return jnp.sum(marks, axis=(0, 2)) - 1


def gather_tokens_kernel(other, with_queries, handing, *refs):
    key_ref, value_ref, fresh_key_ref, fresh_value_ref, owner_ref = refs[:5]
    arrived = refs[-1]
    if with_queries:
        all_query_ref, count_ref, *outs, query_ref, bounds_ref = refs[5:11]
        held, fresh, owners, queries, counts = refs[11:16]
    elif handing:
        *outs, hand_ref, held, fresh, owners = refs[5:11]
    else:
        *outs, held, fresh, owners = refs[5:10]
    pages, page_len = key_ref.shape[1], outs[0].shape[1]
    head_count, own_rows, steps = key_ref.shape[0], fresh.shape[1], fresh.shape[2]
    me = lax.axis_index("tp")
    head = lax.rem(me + other, head_count)
    pairs = [
        (owner_ref, owners),
        (fresh_key_ref, fresh.at[0]),
        (fresh_value_ref, fresh.at[1]),
    ]
    if handing:
        pairs += [(key_ref, held.at[0]), (value_ref, held.at[1])]
    else:
        pairs += [(key_ref.at[head], held.at[0, 0]), (value_ref.at[head], held.at[1, 0])]
    if with_queries:
        width = query_ref.shape[1]
        columns = pl.ds(pl.multiple_of(head * width, LANES), width)
        pairs += [(count_ref, counts), (all_query_ref.at[:, :, columns], queries)]
    copies = [
        pltpu.make_async_copy(source, target, arrived.at[i])
        for i, (source, target) in enumerate(pairs)
    ]
    for copy in copies:
        copy.start()
    copies[0].wait()
    outs[0][pages + 1] = owner_page(owners[...], page_len).astype(jnp.bfloat16)
    if handing:
        cap = hand_ref.shape[2]
        picks = slot_picks(owners, me, [handing], cap, lax.axis_size("tp"))
    for i in range(2):
        copies[1 + i].wait()
        new = fresh[i]
        part = new[:, :, :HD]
        for which in range(1, head_count):
            part = jnp.where(head == which, new[:, :, which * HD : (which + 1) * HD], part)
        lines = part.reshape(own_rows * steps, HD)
        if own_rows * steps < page_len:
            spare = jnp.zeros((page_len - own_rows * steps, HD), jnp.bfloat16)
            lines = jnp.concatenate([lines, spare])
        outs[i][pages] = lines
    for i in range(2):
        copies[3 + i].wait()
        paged = held[i, head] if handing else held[i, 0]
        outs[i][:pages] = paged.reshape(pages, page_len, HD)
    if handing:
        for i in range(2):
            for which in range(head_count):
                place_rows(held.at[i, which], picks[which], [hand_ref.at[i, which]])
    if with_queries:
        copies[5].wait()
        row_lines = query_ref.shape[0]
        row = lax.broadcasted_iota(jnp.int32, (1, row_lines), 1) // steps
        starts = jnp.zeros((1, row_lines), jnp.int32)
        ends = jnp.zeros((1, row_lines), jnp.int32)
        for r in range(counts.shape[0]):
            starts = starts + jnp.where(row > r, counts[r], 0)
            ends = ends + jnp.where(row >= r, counts[r], 0)
        line = lax.broadcasted_iota(jnp.int32, (8, row_lines), 0)
        bounds_ref[...] = jnp.where(line == 0, starts, ends)
        copies[6].wait()
        query_ref[...] = queries[...].reshape(row_lines, query_ref.shape[1])


def owner_page(owners, lines):
    head_count, pages = owners.shape
    page = jnp.concatenate(
        [owners.astype(jnp.float32), jnp.zeros((head_count, LANES - pages), jnp.float32)], axis=1
    )
    return jnp.concatenate([page, jnp.zeros((lines - head_count, LANES), jnp.float32)])


def gather_tokens(
    other, caches, fresh, owner, queries=None, counts=None, handing=0, cap=0, follows=()
):
    head_count, pages, width = caches[0].shape
    page_len = width // HD
    with_queries = queries is not None
    operands = [*caches, *fresh, owner]
    out_shape = [
        jax.ShapeDtypeStruct((pages + extra, page_len, HD), jnp.bfloat16) for extra in (2, 1)
    ]
    scratch = [
        pltpu.VMEM((2, head_count if handing else 1, pages, width), jnp.bfloat16),
        pltpu.VMEM((2,) + fresh[0].shape, jnp.bfloat16),
        pltpu.VMEM(owner.shape, jnp.int32),
    ]
    if handing:
        out_shape.append(jax.ShapeDtypeStruct((2, head_count, cap, width), jnp.bfloat16))
    if with_queries:
        operands += [queries, counts]
        rows, steps, query_width = queries.shape
        query_width = query_width // head_count
        out_shape += [
            jax.ShapeDtypeStruct((rows * steps, query_width), jnp.bfloat16),
            jax.ShapeDtypeStruct((8, rows * steps), jnp.int32),
        ]
        scratch += [
            pltpu.VMEM((rows, steps, query_width), jnp.bfloat16),
            pltpu.SMEM(counts.shape, jnp.int32),
        ]
    return call(
        functools.partial(gather_tokens_kernel, other, with_queries, handing),
        in_hbm(*operands),
        [hbm()] * len(operands),
        follows,
        out_specs=[vmem()] * len(out_shape),
        out_shape=out_shape,
        scratch_shapes=scratch + [pltpu.SemaphoreType.DMA((len(operands),))],
        compiler_params=params(6),
        name="gather_tokens",
    )


def membership(bounds, owner, pages, own_lines, member_lines, row_lines, steps):
    query_line = lax.broadcasted_iota(jnp.int32, (1, row_lines), 1)
    starts, ends = bounds[0:1, :], bounds[1:2, :]
    page_lines = pages * steps
    line = lax.broadcasted_iota(jnp.int32, (member_lines, row_lines), 0)
    page = owner * pages + line // steps
    in_row = (starts <= page) & (page < ends) & (line % steps == query_line % steps)
    own_line = line - page_lines
    is_own = (
        (own_line >= 0) & (own_line < own_lines) & (query_line == owner * own_lines + own_line)
    )
    member = (((line < page_lines) & in_row) | is_own).astype(jnp.float32)
    return member, jnp.transpose(member)


def prepare_kernel(steps, own_lines, page_len, neighbours, bounds_ref, query_ref, *refs):
    row_lines = query_ref.shape[0]
    for place, neighbour in enumerate(neighbours):
        chosen_ref, member_ref, turned_ref = refs[3 * place : 3 * place + 3]
        member_lines = member_ref.shape[0]
        pages = (member_lines - round_up(page_len, LANES)) // steps
        member, turned = membership(
            bounds_ref[...],
            lax.axis_index("tp") ^ neighbour,
            pages,
            own_lines,
            member_lines,
            row_lines,
            steps,
        )
        chosen_ref[...] = jnp.dot(
            member.astype(jnp.bfloat16), query_ref[...], preferred_element_type=jnp.float32
        ).astype(jnp.bfloat16)
        member_ref[...] = member
        turned_ref[...] = turned


def prepare(bounds, query, neighbours, pages, page_len, own_lines, steps):
    row_lines, query_width = query.shape
    member_lines = pages * steps + round_up(page_len, LANES)
    shapes = (
        jax.ShapeDtypeStruct((member_lines, query_width), jnp.bfloat16),
        jax.ShapeDtypeStruct((member_lines, row_lines), jnp.float32),
        jax.ShapeDtypeStruct((row_lines, member_lines), jnp.float32),
    )
    out = call(
        functools.partial(prepare_kernel, steps, own_lines, page_len, neighbours),
        (bounds, query),
        [vmem()] * 2,
        out_specs=[vmem()] * (3 * len(neighbours)),
        out_shape=shapes * len(neighbours),
        compiler_params=params(8),
        name="prepare",
    )
    return [out[3 * place : 3 * place + 3] for place in range(len(neighbours))]


def page_batch(pages, page_len):
    return min(pages, max(1, LANES // page_len))


def score_kernel(steps, has_earlier, chosen, member_ref, turned_ref, keys_ref, *refs):
    if has_earlier:
        early_max_ref, early_total_ref = refs[:2]
        refs = refs[2:]
    weights_ref, fresh_ref, max_ref, total_ref, scores, fresh_scores = refs
    row_lines, query_width = turned_ref.shape[0], chosen.shape[1]
    group = query_width // HD
    page_len = keys_ref.shape[1]
    batch = weights_ref.shape[2] // page_len
    blocks, lines = weights_ref.shape[0], batch * steps
    pages = blocks * batch
    spare = member_ref.shape[0] - pages * steps - page_len
    scale = HD ** (-0.5)
    lane = lax.broadcasted_iota(jnp.int32, (1, LANES), 1)
    member, turned = member_ref[...], turned_ref[...]
    is_member = turned > 0

    line = lax.broadcasted_iota(jnp.int32, (group * lines, batch * page_len), 0)
    token = lax.broadcasted_iota(jnp.int32, (group * lines, batch * page_len), 1)
    page_mask = (line % lines) // steps == token // page_len
    line = lax.broadcasted_iota(jnp.int32, (group * page_len, page_len), 0) % page_len
    token = lax.broadcasted_iota(jnp.int32, (group * page_len, page_len), 1)
    fresh_mask = (line // steps == token // steps) & (token % steps <= line % steps)

    def score(first_line, count, keys, mask):
        rows = slice(first_line, first_line + count)
        queries = jnp.concatenate(
            [chosen[rows, g * HD : (g + 1) * HD] for g in range(group)], axis=0
        )
        found = lax.dot_general(
            queries, keys, (((1,), (1,)), ((), ())), preferred_element_type=jnp.float32
        )
        found = jnp.where(mask, found * scale, NEGATIVE)
        largest = jnp.max(found, axis=1, keepdims=True)
        block_max = jnp.zeros((count, LANES), jnp.float32)
        for g in range(group):
            block_max = jnp.where(lane == g, largest[g * count : (g + 1) * count], block_max)
        return found, block_max

    maxima = []
    for block in range(blocks):
        keys = keys_ref[block * batch : (block + 1) * batch].reshape(batch * page_len, HD)
        scores[block], block_max = score(block * lines, lines, keys, page_mask)
        maxima.append(block_max)
    fresh_scores[...], block_max = score(pages * steps, page_len, keys_ref[pages], fresh_mask)
    maxima.append(block_max)
    if spare:
        maxima.append(jnp.zeros((spare, LANES), jnp.float32))

    line_max = jnp.transpose(jnp.concatenate(maxima, axis=0))
    row_max = jnp.full((row_lines, LANES), NEGATIVE, jnp.float32)
    for g in range(group):
        best = jnp.max(
            jnp.where(is_member, line_max[g : g + 1, :], NEGATIVE), axis=1, keepdims=True
        )
        row_max = jnp.where(lane == g, best, row_max)
    if has_earlier:
        row_max = jnp.maximum(row_max, early_max_ref[...])
    spread = jnp.dot(
        member, row_max, precision=HIGHEST, preferred_element_type=jnp.float32
    )

    def weigh(first_line, count, found):
        rows = spread[first_line : first_line + count]
        shift = jnp.concatenate([rows[:, g : g + 1] for g in range(group)], axis=0)
        weights = jnp.exp(jnp.minimum(found - shift, 0.0)).astype(jnp.bfloat16)
        ones = jnp.ones((weights.shape[1], LANES), jnp.bfloat16)
        total = jnp.dot(weights, ones, preferred_element_type=jnp.float32)
        block_total = jnp.zeros((count, LANES), jnp.float32)
        for g in range(group):
            block_total = jnp.where(lane == g, total[g * count : (g + 1) * count], block_total)
        return weights, block_total

    totals = []
    for block in range(blocks):
        weights_ref[block], total = weigh(block * lines, lines, scores[block])
        totals.append(total)
    fresh_ref[...], total = weigh(pages * steps, page_len, fresh_scores[...])
    totals.append(total)
    if spare:
        totals.append(jnp.zeros((spare, LANES), jnp.float32))
    row_total = jnp.dot(
        turned,
        jnp.concatenate(totals, axis=0),
        precision=HIGHEST,
        preferred_element_type=jnp.float32,
    )
    if has_earlier:
        row_total = row_total + early_total_ref[...] * jnp.exp(early_max_ref[...] - row_max)
    max_ref[...] = row_max
    total_ref[...] = row_total


def score(choice, keys, steps, earlier=(), flops=0):
    (member_lines, query_width), row_lines = choice[0].shape, choice[2].shape[0]
    group = query_width // HD
    page_len = keys.shape[1]
    pages = (member_lines - round_up(page_len, LANES)) // steps
    batch = page_batch(pages, page_len)
    blocks = pages // batch
    shapes = ((blocks, group * batch * steps, batch * page_len), (group * page_len, page_len))
    stat = jax.ShapeDtypeStruct((row_lines, LANES), jnp.float32)
    operands = (*choice, keys, *earlier)
    return call(
        functools.partial(score_kernel, steps, bool(earlier)),
        operands,
        [vmem()] * len(operands),
        flops=flops,
        out_specs=[vmem()] * 4,
        out_shape=[jax.ShapeDtypeStruct(shape, jnp.bfloat16) for shape in shapes] + [stat, stat],
        scratch_shapes=[pltpu.VMEM(shape, jnp.float32) for shape in shapes],
        compiler_params=params(12),
        name="score",
    )


def value_kernel(steps, chunk, chunks, has_earlier, has_notes, last, *refs):
    weights_ref, fresh_ref, turned_ref, values_ref, max_ref, total_ref = refs[:6]
    refs = refs[6:]
    if has_earlier:
        early_max_ref, early_numer_ref = refs[:2]
        refs = refs[2:]
    if has_notes:
        own_keys_ref, near_keys_ref = refs[:2]
        refs = refs[2:]
    out_ref, high, low = refs
    row_lines, member_lines = turned_ref.shape
    page_len = values_ref.shape[1]
    blocks, batch = weights_ref.shape[0], weights_ref.shape[2] // page_len
    lines, pages = batch * steps, blocks * batch
    all_groups = weights_ref.shape[1] // lines
    group = all_groups // chunks
    first = chunk * group
    used = pages * steps + page_len

    def gain(first_line, count, weights, values):
        numer = jnp.dot(weights, values, preferred_element_type=jnp.float32)
        rounded = numer.astype(jnp.bfloat16)
        rest = (numer - rounded.astype(jnp.float32)).astype(jnp.bfloat16)
        for g in range(group):
            part = slice(g * count, (g + 1) * count)
            columns = slice(g * HD, (g + 1) * HD)
            high[first_line : first_line + count, columns] = rounded[part]
            low[first_line : first_line + count, columns] = rest[part]

    for block in range(blocks):
        weights = weights_ref[block, first * lines : (first + group) * lines]
        values = values_ref[block * batch : (block + 1) * batch].reshape(batch * page_len, HD)
        gain(block * lines, lines, weights, values)
    weights = fresh_ref[first * page_len : (first + group) * page_len]
    gain(pages * steps, page_len, weights, values_ref[pages])
    if member_lines > used:
        high[used:, :] = jnp.zeros((member_lines - used, group * HD), jnp.bfloat16)
        low[used:, :] = jnp.zeros((member_lines - used, group * HD), jnp.bfloat16)

    lane = lax.broadcasted_iota(jnp.int32, (1, LANES), 1)
    row_max, row_total = max_ref[...], total_ref[...]
    present = row_total > 0
    inverse = jnp.where(present, 1.0 / jnp.where(present, row_total, 1.0), 0.0)
    if has_earlier:
        scale_early = jnp.exp(early_max_ref[...] - row_max)
    if last and chunk == 0:
        log_sum = jnp.where(
            present & (lane < all_groups),
            row_max + jnp.log(jnp.where(present, row_total, 1.0)),
            jnp.where(lane < all_groups, NEGATIVE, 0.0),
        )
        lanes = split_sums(log_sum, all_groups)
        if has_notes:
            lanes = lanes + owner_notes(
                own_keys_ref[pages + 1], near_keys_ref[pages + 1], row_lines, 3 * all_groups
            )
        out_ref[:, group * HD :] = lanes.astype(jnp.bfloat16)
    turned = turned_ref[...].astype(jnp.bfloat16)
    for g in range(group):
        columns = slice(g * HD, (g + 1) * HD)
        which = slice(first + g, first + g + 1)
        numer = jnp.dot(turned, high[:, columns], preferred_element_type=jnp.float32) + jnp.dot(
            turned, low[:, columns], preferred_element_type=jnp.float32
        )
        if has_earlier:
            numer = numer + early_numer_ref[:, columns] * scale_early[:, which]
        if last:
            numer = numer * inverse[:, which]
        out_ref[:, columns] = numer.astype(out_ref.dtype)


def value(scored, turned, values, steps, chunk, chunks, last, earlier=(), notes=(), follows=()):
    row_lines, member_lines = turned.shape
    page_len = values.shape[1]
    group = scored[1].shape[0] // page_len // chunks
    wide = group * HD + (LANES if last and chunk == 0 else 0)
    operands = (*scored[:2], turned, values, *scored[2:], *earlier, *notes)
    return call(
        functools.partial(value_kernel, steps, chunk, chunks, bool(earlier), bool(notes), last),
        operands,
        [vmem()] * len(operands),
        follows,
        out_specs=vmem(),
        out_shape=jax.ShapeDtypeStruct(
            (row_lines, wide), jnp.bfloat16 if last else jnp.float32
        ),
        scratch_shapes=[pltpu.VMEM((member_lines, group * HD), jnp.bfloat16)] * 2,
        compiler_params=params(8),
        name="value",
    )


def split_sums(value, group):
    first = value.astype(jnp.bfloat16).astype(jnp.float32)
    rest = value - first
    second = rest.astype(jnp.bfloat16).astype(jnp.float32)
    third = rest - second
    return first + pltpu.roll(second, group, axis=1) + pltpu.roll(third, 2 * group, axis=1)


def owner_notes(own, near_page, row_lines, first_lane):
    lines = near_page.shape[0]
    notes = jnp.concatenate(
        [
            own.astype(jnp.float32),
            near_page.astype(jnp.float32),
            jnp.zeros((row_lines - 2 * lines, LANES), jnp.float32),
        ]
    )
    return pltpu.roll(notes, first_lane, axis=1)


def join_sums(parts, group):
    parts = parts.astype(jnp.float32)
    return (
        parts
        + pltpu.roll(parts, LANES - group, axis=1)
        + pltpu.roll(parts, LANES - 2 * group, axis=1)
    )


def combine_kernel(group, first, sums_ref, their_sums_ref, mine_ref, theirs_ref, out_ref):
    sums = join_sums(sums_ref[:, -LANES:], group)
    their_sums = join_sums(their_sums_ref[:, -LANES:], group)
    largest = jnp.maximum(sums, their_sums)
    weight = jnp.exp(sums - largest)
    their_weight = jnp.exp(their_sums - largest)
    inverse = 1.0 / (weight + their_weight)
    weight = weight * inverse
    their_weight = their_weight * inverse
    for place in range(out_ref.shape[1] // HD):
        g = first + place
        columns = slice(place * HD, (place + 1) * HD)
        out_ref[:, columns] = (
            mine_ref[:, columns].astype(jnp.float32) * weight[:, g : g + 1]
            + theirs_ref[:, columns].astype(jnp.float32) * their_weight[:, g : g + 1]
        ).astype(jnp.bfloat16)


def combine(mine, theirs, chunk, follows=()):
    row_lines, width = mine[0].shape
    width -= LANES
    group = width // HD * len(mine)
    return call(
        functools.partial(combine_kernel, group, chunk * width // HD),
        (mine[0], theirs[0], mine[chunk], theirs[chunk]),
        [vmem()] * 4,
        follows,
        out_specs=vmem(),
        out_shape=jax.ShapeDtypeStruct((row_lines, width), jnp.bfloat16),
        compiler_params=params(4),
        name="combine",
    )


def block_row(own, chunk, chunks, head_count, depth):
    head = lax.rem(lax.axis_index("tp") + (0 if own else 1), head_count)
    return pl.multiple_of((head * chunks + chunk) * depth, depth)


def fetch_kernel(blocks, chunks, head_count, weight_ref, held_ref, done_ref, arrived):
    depth = held_ref.shape[0] // len(blocks)
    pieces = arrived.shape[0] // len(blocks)
    size = depth // pieces
    copies = []
    for place, (own, chunk) in enumerate(blocks):
        base = block_row(own, chunk, chunks, head_count, depth)
        for piece in range(pieces):
            copies.append(
                pltpu.make_async_copy(
                    weight_ref.at[pl.ds(pl.multiple_of(base + piece * size, size), size)],
                    held_ref.at[pl.ds(place * depth + piece * size, size)],
                    arrived.at[place * pieces + piece],
                )
            )
    for copy in copies:
        copy.start()
    done_ref[...] = jnp.zeros_like(done_ref)
    for copy in copies:
        copy.wait()


def fetch(weight, blocks, chunks, head_count, depth, follows):
    pieces = 4
    return call(
        functools.partial(fetch_kernel, blocks, chunks, head_count),
        in_hbm(weight),
        [hbm()],
        follows,
        out_specs=(vmem(), vmem()),
        out_shape=(
            pltpu.VMEM((len(blocks) * depth, weight.shape[1]), weight.dtype),
            jax.ShapeDtypeStruct((8, LANES), jnp.float32),
        ),
        scratch_shapes=[pltpu.SemaphoreType.DMA((len(blocks) * pieces,))],
        compiler_params=params(1),
        name="fetch",
    )


def project_kernel(parts, has_total, chunk_lines, first, offsets, chunks, head_count, *refs):
    input_refs, weight_ref, refs = refs[:parts], refs[parts], refs[parts + 1 :]
    streamed = offsets is None
    if streamed:
        held, arrived = refs[-2:]
        refs = refs[:-2]
    outs = refs[1:] if has_total else refs
    depth, width = input_refs[0].shape[1], outs[0].shape[-1]
    block = min(width, 512)
    count = width // block

    def piece(index):
        return pltpu.make_async_copy(
            weight_ref.at[
                pl.ds(block_row(True, 0, chunks, head_count, depth), depth),
                pl.ds(first + index * block, block),
            ],
            held.at[:, pl.ds(index * block, block)],
            arrived.at[index],
        )

    if streamed:
        for index in range(count):
            piece(index).start()
    for index in range(count):
        start = index * block
        columns = slice(first + start, first + start + block)
        product = refs[0][:, columns] if has_total else 0.0
        if streamed:
            piece(index).wait()
            product = product + jnp.dot(
                input_refs[0][...],
                held[:, start : start + block],
                preferred_element_type=jnp.float32,
            )
        else:
            for input_ref, offset in zip(input_refs, offsets):
                product = product + jnp.dot(
                    input_ref[...],
                    weight_ref[offset * depth : (offset + 1) * depth, columns],
                    preferred_element_type=jnp.float32,
                )
        if chunk_lines is None:
            outs[0][:, start : start + block] = product
            continue
        core = lax.rem(lax.axis_index("kv"), 2)
        keep_ref, send_ref = outs
        for pair in range(keep_ref.shape[0]):
            even = product[2 * pair * chunk_lines : (2 * pair + 1) * chunk_lines]
            odd = product[(2 * pair + 1) * chunk_lines : (2 * pair + 2) * chunk_lines]
            keep_ref[pair, :, start : start + block] = jnp.where(core == 0, even, odd)
            send_ref[pair, :, start : start + block] = jnp.where(core == 0, odd, even).astype(
                send_ref.dtype
            )


def project(inputs, weight, offsets, chunks, head_count, total, columns, chunk_lines, follows=()):
    row_lines, depth = inputs[0].shape
    first, width = columns
    in_specs = [vmem()] * len(inputs) + [hbm() if offsets is None else vmem()]
    operands = [*inputs, *(in_hbm(weight) if offsets is None else [weight])]
    if total is not None:
        in_specs.append(vmem())
        operands.append(total)
    if chunk_lines is None:
        out_shape = jax.ShapeDtypeStruct((row_lines, width), jnp.float32)
        out_specs = vmem()
    else:
        pairs = row_lines // (2 * chunk_lines)
        shape = (pairs, chunk_lines, width)
        out_shape = (
            jax.ShapeDtypeStruct(shape, jnp.float32),
            jax.ShapeDtypeStruct(shape, jnp.bfloat16),
        )
        out_specs = (vmem(), vmem())
    scratch = []
    if offsets is None:
        scratch = [
            pltpu.VMEM((depth, width), weight.dtype),
            pltpu.SemaphoreType.DMA((max(1, width // 512),)),
        ]
    return call(
        functools.partial(
            project_kernel,
            len(inputs),
            total is not None,
            chunk_lines,
            first,
            offsets,
            chunks,
            head_count,
        ),
        operands,
        in_specs,
        follows,
        out_specs=out_specs,
        out_shape=out_shape,
        scratch_shapes=scratch,
        compiler_params=params(16 if offsets is None else 8),
        name="project",
    )


def add_core_kernel(keep_ref, got_ref, own_ref, *send_refs):
    half = lax.axis_index("kv") // 2
    own_ref[...] = keep_ref[half] + got_ref[half].astype(jnp.float32)
    for step, send_ref in enumerate(send_refs, 1):
        part = keep_ref[half ^ step] + got_ref[half ^ step].astype(jnp.float32)
        send_ref[...] = part.astype(send_ref.dtype)


def sum_heads(keep, send, kv_size):
    got = lax.ppermute(send, "kv", flip(kv_size, 1))
    shape = keep.shape[1:]
    own, *sends = call(
        add_core_kernel,
        (keep, got),
        [vmem(), vmem()],
        out_specs=[vmem()] * (kv_size // 2),
        out_shape=[jax.ShapeDtypeStruct(shape, jnp.float32)]
        + [jax.ShapeDtypeStruct(shape, jnp.bfloat16)] * (kv_size // 2 - 1),
        compiler_params=params(4),
        name="add_core",
    )
    return [own] + [
        lax.ppermute(part, "kv", flip(kv_size, 2 * step)) for step, part in enumerate(sends, 1)
    ]


def finish_kernel(pieces, *refs):
    parts, out_ref, done_ref = refs[:-2], refs[-2], refs[-1]
    done_ref[...] = jnp.zeros_like(done_ref)
    each = len(parts) // pieces
    steps, width = out_ref.shape[1], out_ref.shape[2] // pieces
    for piece in range(pieces):
        total = parts[piece * each][...]
        for part in parts[piece * each + 1 : (piece + 1) * each]:
            total = total + part[...].astype(jnp.float32)
        out_ref[:, :, piece * width : (piece + 1) * width] = total.astype(jnp.bfloat16).reshape(
            -1, steps, width
        )


def finish(results, steps):
    lines, width = results[0][0].shape
    parts = [part for pieces in results for part in pieces]
    return call(
        functools.partial(finish_kernel, len(results)),
        parts,
        [vmem()] * len(parts),
        out_specs=(vmem(), vmem()),
        out_shape=(
            jax.ShapeDtypeStruct((lines // steps, steps, width * len(results)), jnp.bfloat16),
            jax.ShapeDtypeStruct((8, LANES), jnp.float32),
        ),
        compiler_params=params(4),
        name="finish",
    )


def body(
    queries, fresh_keys, fresh_values, cache_keys, cache_values, page_counts, page_owner, out_weight
):
    tp_size, kv_size = lax.axis_size("tp"), lax.axis_size("kv")
    head_count, pages_here, page_width = cache_keys.shape
    row_count, step_count, query_width = queries.shape
    own_lines = fresh_keys.shape[0] * step_count
    page_len = page_width // HD
    row_lines = row_count * step_count
    head_width = query_width // head_count
    group = head_width // HD
    cap = max(2, (2 * pages_here + tp_size - 1) // tp_size)
    out_width = out_weight.shape[1]
    chunk_lines = row_lines // kv_size
    caches = (cache_keys, cache_values)
    fresh = (fresh_keys, fresh_values)

    paired = head_count == 2 and tp_size == 4 and group % 2 == 0 and cap % 16 == 0
    paired = paired and 3 * group + pages_here <= LANES and 2 * page_len <= row_lines
    chunks = 2 if paired else 1
    part = head_width // chunks
    everything = (0, out_width)

    if paired:
        keys, values, send_last = gather_tokens(1, caches, fresh, page_owner, handing=3, cap=cap)
        near_keys = lax.ppermute(keys, "tp", flip(tp_size, 1))
        got_inner = lax.ppermute(send_last, "tp", [(1, 2), (2, 1)])
        own_keys, own_values, query, bounds = gather_tokens(
            0, caches, fresh, page_owner, queries, page_counts, follows=(send_last,)
        )
        near_values = lax.ppermute(tie(values, bounds), "tp", flip(tp_size, 1))
        own_choice, near_choice = prepare(
            bounds, query, (0, 1), pages_here, page_len, own_lines, step_count
        )
        scored = score(own_choice, own_keys, step_count)
        early_numers = [
            value(scored, own_choice[2], own_values, step_count, chunk, chunks, False)
            for chunk in range(chunks)
        ]
        early_max, early_total = scored[2:]
        scored = score(near_choice, near_keys, step_count, (early_max, early_total), 1 << 34)
        payload = [
            value(
                scored,
                near_choice[2],
                near_values,
                step_count,
                chunk,
                chunks,
                True,
                (early_max, early_numers[chunk]),
                () if chunk else (own_keys, near_keys),
            )
            for chunk in range(chunks)
        ]
        jobs = ((2, True), (1, False), (0, True))
        send_far, send_near, kept = place_pages(
            page_owner, caches, jobs, cap, tp_size, False, (payload[1],)
        )
        blocks = ((True, 1), (False, 0))
        held, held_done = fetch(out_weight, blocks, chunks, head_count, part, payload[1:])
        payload[1] = tie(payload[1], held_done)
        held_last, held_done = fetch(
            out_weight, ((False, 1),), chunks, head_count, part, (held_done,)
        )
        theirs = [lax.ppermute(p, "tp", flip(tp_size, 2)) for p in payload]
        got_near = lax.ppermute(tie(send_near, held_done), "tp", flip(tp_size, 1))
        near_pages = place_near(near_keys, near_values, head_count, cap, tp_size)
        first_part = combine(payload, theirs, 0)
        near_first = lax.ppermute(first_part, "tp", flip(tp_size, 1))
        total = project([first_part], out_weight, None, chunks, head_count, None, everything, None)
        got_far = lax.ppermute(tie(send_far, total), "tp", flip(tp_size, 2))
        got_outer = lax.ppermute(tie(send_last, total), "tp", [(0, 3), (3, 0)])
        second_part = combine(payload, theirs, 1, (got_near, total, got_inner))
        near_second = lax.ppermute(second_part, "tp", flip(tp_size, 1))
        own_parts, near_parts = (first_part, second_part), (near_first, near_second)
        plan = ((0, None, None), (1, None, 0), (1, None, 1), (3, (1, 2), None))
        *settled, settled_done = settle(
            [kept, near_pages, got_near, got_inner], plan, head_count, tp_size * cap, (), (total,)
        )
        total = project(
            [own_parts[1], near_parts[0]],
            held,
            (0, 1),
            chunks,
            head_count,
            total,
            everything,
            None,
            (settled_done,),
        )
        results = []
        for first in (0, out_width // 2):
            columns = (first, out_width // 2)
            keep, send = project(
                [near_parts[1]],
                held_last,
                (0,),
                chunks,
                head_count,
                total,
                columns,
                chunk_lines,
            )
            results.append(sum_heads(keep, send, kv_size))
        attention_out, finished = finish(results, step_count)
        slot_rows = slot_rows_near(
            bounds,
            payload[0],
            theirs[0],
            pages_here,
            3 * group,
            page_len,
            cap,
            (head_count, tp_size * cap),
            step_count,
            (results[1][0],),
        )
        plan = ((2, None, None), (3, (0, 3), None))
        slot_keys, slot_values, _ = settle(
            [got_far, got_outer], plan, head_count, tp_size * cap, settled, (finished,)
        )
        return (attention_out, slot_keys, slot_values, slot_rows)

    def hand_over(cache):
        jobs = tuple((d, True) for d in range(tp_size))
        sent = place_pages(page_owner, (cache,), jobs, cap, tp_size, True)
        got = lax.all_to_all(
            jnp.concatenate(sent), "tp", split_axis=0, concat_axis=0, tiled=True
        )
        return got.transpose(1, 0, 2, 3).reshape(head_count, tp_size * cap, page_width)

    slot_keys, slot_values = hand_over(cache_keys), hand_over(cache_values)
    slot_rows = slot_rows_gathered(page_owner, page_counts, cap)
    attended = []
    for head in range(head_count):
        cut = slice(head, head + 1)
        lanes = slice(head * HD, (head + 1) * HD)
        keys, values, query, bounds = gather_tokens(
            0,
            [cache[cut] for cache in caches],
            [new[:, :, lanes] for new in fresh],
            page_owner[cut],
            queries[:, :, head * head_width : (head + 1) * head_width],
            page_counts,
        )
        (choice,) = prepare(
            bounds, query, (0,), pages_here, page_len, own_lines, step_count
        )
        scored = score(choice, keys, step_count)
        payload = value(scored, choice[2], values, step_count, 0, 1, True)
        raw = payload[:, part:].astype(jnp.float32)
        sums = raw[:, :group] + raw[:, group : 2 * group] + raw[:, 2 * group : 3 * group]
        weight = jnp.exp(sums - lax.pmax(sums, "tp"))
        numer = payload[:, :part].astype(jnp.float32).reshape(row_lines, group, HD)
        numer = lax.psum(numer * weight[..., None], "tp")
        joined = numer / lax.psum(weight, "tp")[..., None]
        attended.append(joined.reshape(row_lines, head_width).astype(jnp.bfloat16))
    keep, send = project(
        [jnp.concatenate(attended, axis=1)], out_weight, None, 1, 1, None, everything, chunk_lines
    )
    attention_out, _ = finish([sum_heads(keep, send, kv_size)], step_count)
    return (attention_out, slot_keys, slot_values, slot_rows)


def solution(mesh):
    return jax.shard_map(
        body,
        mesh=mesh,
        in_specs=(
            P("grp", None, "kv"),
            P(("grp", "tp"), None, "kv"),
            P(("grp", "tp"), None, "kv"),
            P(("grp", "kv"), "tp", None),
            P(("grp", "kv"), "tp", None),
            P("grp"),
            P(("grp", "kv"), "tp"),
            P("kv", "tp"),
        ),
        out_specs=(
            P(("grp", "kv"), None, "tp"),
            P(("grp", "kv"), "tp", None),
            P(("grp", "kv"), "tp", None),
            P(("grp", "kv"), "tp"),
        ),
        check_vma=False,
    )
```

```python
import functools

import jax
import jax.numpy as jnp
from jax import lax
from jax.experimental import pallas as pl
from jax.experimental.pallas import tpu as pltpu
from jax.sharding import PartitionSpec as P

HD = 128
LANES = 128
NEGATIVE = -1e30
HIGHEST = lax.Precision.HIGHEST
MIB = 1024 * 1024


def round_up(value, step):
    return -(-value // step) * step


def flip(size, bit):
    return [(i, i ^ bit) for i in range(size)]


def params(mib):
    return pltpu.CompilerParams(vmem_limit_bytes=mib * MIB)


def in_hbm(*arrays):
    return [pltpu.with_memory_space_constraint(array, pltpu.HBM) for array in arrays]


def vmem():
    return pl.BlockSpec(memory_space=pltpu.VMEM)


def hbm():
    return pl.BlockSpec(memory_space=pltpu.HBM)


def anywhere():
    return pl.BlockSpec(memory_space=pl.ANY)


def call(kernel, operands, in_specs, follows=(), flops=0, **rest):
    count, extra = len(operands), len(follows)

    def without_extra(*refs):
        kernel(*refs[:count], *refs[count + extra :])

    return pl.pallas_call(
        without_extra,
        in_specs=list(in_specs) + [anywhere()] * extra,
        cost_estimate=pl.CostEstimate(flops=flops, bytes_accessed=0, transcendentals=0),
        **rest,
    )(*operands, *follows)


def tie(value, *follows):
    return call(
        lambda value_ref, out_ref: None,
        (value,),
        [anywhere()],
        follows,
        out_specs=anywhere(),
        out_shape=jax.ShapeDtypeStruct(value.shape, value.dtype),
        input_output_aliases={0: 0},
        compiler_params=params(1),
        name="tie",
    )


def earlier_pages(page_count):
    first = lax.broadcasted_iota(jnp.int32, (page_count, page_count), 0)
    second = lax.broadcasted_iota(jnp.int32, (page_count, page_count), 1)
    return (first < second).astype(jnp.bfloat16)


def rank_pages(away, earlier, dest_rows):
    ways = lax.broadcasted_iota(jnp.int32, (dest_rows, away.shape[1]), 0)
    listed = (ways == away).astype(jnp.float32)
    before = jnp.dot(listed.astype(jnp.bfloat16), earlier, preferred_element_type=jnp.float32)
    return jnp.sum(before * listed, axis=0, keepdims=True).astype(jnp.int32)


def slot_picks(owners, me, distances, cap, tp_size):
    head_count, page_count = owners.shape
    earlier = earlier_pages(page_count)
    row = lax.broadcasted_iota(jnp.int32, (cap, page_count), 0)
    picks = []
    for head in range(head_count):
        away = owners[head : head + 1, :] ^ me
        rank = rank_pages(away, earlier, round_up(tp_size, 8))
        picks.append([((away == d) & (rank == row)).astype(jnp.float32) for d in distances])
    return picks


def place_rows(pages_ref, pick, targets):
    width, cap = pages_ref.shape[1], pick[0].shape[0]
    step = min(width, 1024)
    for start in range(0, width, step):
        columns = slice(start, start + step)
        placed = jnp.dot(
            jnp.concatenate(pick).astype(jnp.bfloat16),
            pages_ref[:, columns],
            preferred_element_type=jnp.float32,
        ).astype(jnp.bfloat16)
        for which, target in enumerate(targets):
            target[:, columns] = placed[which * cap : (which + 1) * cap]


def place_kernel(cap, jobs, by_index, tp_size, owner_ref, *refs):
    count = (len(refs) - 2 - len(jobs)) // 2
    sources, targets = refs[:count], refs[count : count + len(jobs)]
    held, owners, arrived = refs[count + len(jobs) : -2], refs[-2], refs[-1]
    head_count = sources[0].shape[0]
    copies = [
        pltpu.make_async_copy(source, target, arrived.at[i])
        for i, (source, target) in enumerate(zip((owner_ref, *sources), (owners, *held)))
    ]
    for copy in copies:
        copy.start()
    copies[0].wait()
    me = 0 if by_index else lax.axis_index("tp")
    own_head = lax.rem(me, head_count)
    picks = slot_picks(owners, me, [d for d, _ in jobs], cap, tp_size)

    def place(index, head, pick, target_of):
        place_rows(held[index].at[head], pick, target_of)

    shared = [i for i, (_, every) in enumerate(jobs) if every]
    single = [i for i, (_, every) in enumerate(jobs) if not every]
    for index in range(count):
        copies[index + 1].wait()
        for head in range(head_count):
            if shared:
                pick = [picks[head][i] for i in shared]
                place(index, head, pick, [targets[i].at[index, head] for i in shared])
        if single:
            pick = []
            for i in single:
                chosen = picks[0][i]
                for head in range(1, head_count):
                    chosen = jnp.where(own_head == head, picks[head][i], chosen)
                pick.append(chosen)
            place(index, own_head, pick, [targets[i].at[index] for i in single])


def place_pages(page_owner, caches, jobs, cap, tp_size, by_index, follows=()):
    head_count, page_count, width = caches[0].shape
    return call(
        functools.partial(place_kernel, cap, jobs, by_index, tp_size),
        in_hbm(page_owner, *caches),
        [hbm()] * (1 + len(caches)),
        follows,
        out_specs=tuple(vmem() for _ in jobs),
        out_shape=tuple(
            jax.ShapeDtypeStruct(
                (len(caches),) + ((head_count,) if every else ()) + (cap, width), jnp.bfloat16
            )
            for _, every in jobs
        ),
        scratch_shapes=[pltpu.VMEM(cache.shape, cache.dtype) for cache in caches]
        + [
            pltpu.VMEM(page_owner.shape, jnp.int32),
            pltpu.SemaphoreType.DMA((1 + len(caches),)),
        ],
        compiler_params=params(8),
        name="place_pages",
    )


def place_near_kernel(tp_size, head_count, keys_ref, values_ref, out_ref):
    cap, width = out_ref.shape[1:]
    pages, page_len = values_ref.shape[0] - 1, values_ref.shape[1]
    me = lax.axis_index("tp")
    head = lax.rem(me, head_count)
    lists = keys_ref[pages + 1].astype(jnp.float32)[:, :pages].astype(jnp.int32)
    owner = lists[0:1]
    for which in range(1, head_count):
        owner = jnp.where(head == which, lists[which : which + 1], owner)
    rank = rank_pages(owner, earlier_pages(pages), round_up(tp_size, 8))
    row = lax.broadcasted_iota(jnp.int32, (cap, pages), 0)
    pick = ((owner == me) & (rank == row)).astype(jnp.bfloat16)
    for index, source in enumerate((keys_ref, values_ref)):
        paged = source[:pages].reshape(pages, page_len * HD)
        out_ref[index] = jnp.dot(pick, paged, preferred_element_type=jnp.float32).astype(
            jnp.bfloat16
        )


def place_near(keys, values, head_count, cap, tp_size):
    page_len = keys.shape[1]
    return call(
        functools.partial(place_near_kernel, tp_size, head_count),
        (keys, values),
        [vmem()] * 2,
        out_specs=vmem(),
        out_shape=jax.ShapeDtypeStruct((2, cap, page_len * HD), jnp.bfloat16),
        compiler_params=params(8),
        name="place_near",
    )


def settle_kernel(plan, *refs):
    count = len(plan)
    parts, arrived = refs[:count], refs[-1]
    key_ref, value_ref, done_ref = refs[-4:-1]
    head_count, cap = key_ref.shape[0], parts[0].shape[-2]
    me = lax.axis_index("tp")

    def copies_of(place):
        distance, _, other = plan[place]
        first = pl.multiple_of((me ^ distance) * cap, cap)
        copies = []
        for index, target in enumerate((key_ref, value_ref)):
            if other is None:
                slots = target.at[:, pl.ds(first, cap)]
            else:
                slots = target.at[lax.rem(me + other, head_count), pl.ds(first, cap)]
            copies.append(
                pltpu.make_async_copy(
                    parts[place].at[index],
                    slots,
                    arrived.at[place * 2 * head_count + len(copies)],
                )
            )
        return copies

    def move(place, action):
        holders = plan[place][1]
        if holders is None:
            for copy in copies_of(place):
                action(copy)
            return
        holds = functools.reduce(lambda a, b: a | b, [me == holder for holder in holders])

        @pl.when(holds)
        def _():
            for copy in copies_of(place):
                action(copy)

    for place in range(count):
        move(place, lambda copy: copy.start())
    done_ref[...] = jnp.zeros_like(done_ref)
    for place in range(count):
        move(place, lambda copy: copy.wait())


def settle(parts, plan, head_count, slots, settled=(), follows=()):
    width = parts[0].shape[-1]
    shape = jax.ShapeDtypeStruct((head_count, slots, width), jnp.bfloat16)
    count = len(parts)
    return call(
        functools.partial(settle_kernel, plan),
        (*parts, *settled),
        [vmem()] * count + [hbm()] * len(settled),
        follows,
        out_specs=(hbm(), hbm(), vmem()),
        out_shape=(shape, shape, jax.ShapeDtypeStruct((8, LANES), jnp.float32)),
        input_output_aliases={count: 0, count + 1: 1} if settled else {},
        scratch_shapes=[pltpu.SemaphoreType.DMA((2 * count * head_count,))],
        compiler_params=params(6),
        name="settle",
    )


def slot_rows_kernel(
    cap, pages, first_lane, page_len, steps, bounds_ref, own_ref, far_ref, out_ref
):
    head_count, slots = out_ref.shape
    tp_size = slots // cap
    me = lax.axis_index("tp")
    earlier = earlier_pages(pages)
    ends = bounds_ref[1:2, :]
    ids = lax.broadcasted_iota(jnp.int32, (pages, ends.shape[1]), 0)
    row = lax.broadcasted_iota(jnp.int32, (cap, pages), 0)
    ones = jnp.ones((8, ends.shape[1]), jnp.bfloat16)
    lines = [[] for _ in range(head_count)]
    for distance in range(tp_size):
        block = me ^ distance
        marks = lax.dot_general(
            ones,
            (ends <= block * pages + ids).astype(jnp.bfloat16),
            (((1,), (1,)), ((), ())),
            preferred_element_type=jnp.float32,
        )
        marks = marks / steps + 1
        source = own_ref if distance < 2 else far_ref
        line = (distance % 2) * page_len
        notes = source[line : line + page_len, -LANES:].astype(jnp.float32)
        notes = pltpu.roll(notes, LANES - first_lane, axis=1)
        for head in range(head_count):
            owner = notes[head : head + 1, :pages].astype(jnp.int32)
            rank = rank_pages(owner, earlier, round_up(tp_size, 8))
            pick = ((owner == me) & (rank == row)).astype(jnp.bfloat16)
            found = lax.dot_general(
                marks.astype(jnp.bfloat16),
                pick,
                (((1,), (1,)), ((), ())),
                preferred_element_type=jnp.float32,
            )
            found = jnp.concatenate([found, jnp.zeros((8, LANES - cap), jnp.float32)], axis=1)
            lines[head].append(pltpu.roll(found, block * cap, axis=1)[:1])
    for head in range(head_count):
        total = lines[head][0]
        for line in lines[head][1:]:
            total = total + line
        out_ref[head : head + 1, :] = total[:, :slots].astype(jnp.int32) - 1


def slot_rows_near(bounds, own, far, pages, first_lane, page_len, cap, shape, steps, follows):
    return call(
        functools.partial(slot_rows_kernel, cap, pages, first_lane, page_len, steps),
        (bounds, own, far),
        [vmem()] * 3,
        follows,
        out_specs=vmem(),
        out_shape=jax.ShapeDtypeStruct(shape, jnp.int32),
        compiler_params=params(2),
        name="slot_rows",
    )


def slot_rows_gathered(page_owner, page_counts, cap):
    owners = lax.all_gather(page_owner, "tp", axis=0, tiled=False)
    tp_size, head_count, pages_here = owners.shape
    rows = jnp.arange(page_counts.shape[0], dtype=jnp.int32)
    row_ends = jnp.sum(jnp.where(rows[None, :] <= rows[:, None], page_counts[None, :], 0), axis=1)
    ids = jnp.arange(pages_here, dtype=jnp.int32)
    same = (owners[..., :, None] == owners[..., None, :]) & (ids[:, None] < ids[None, :])
    rank = jnp.sum(same.astype(jnp.int32), axis=2)
    blocks = jnp.arange(tp_size, dtype=jnp.int32)
    page_ids = blocks[:, None] * pages_here + ids
    page_row = jnp.sum((row_ends <= page_ids[..., None]).astype(jnp.int32), axis=-1)
    slot = jnp.where(owners == lax.axis_index("tp"), blocks[:, None, None] * cap + rank, -1)
    slot_ids = jnp.arange(tp_size * cap, dtype=jnp.int32)
    marks = jnp.where(slot[..., None] == slot_ids, page_row[:, None, :, None] + 1, 0)
    return jnp.sum(marks, axis=(0, 2)) - 1


def gather_tokens_kernel(other, with_queries, handing, *refs):
    key_ref, value_ref, fresh_key_ref, fresh_value_ref, owner_ref = refs[:5]
    arrived = refs[-1]
    if with_queries:
        all_query_ref, count_ref, *outs, query_ref, bounds_ref = refs[5:11]
        held, fresh, owners, queries, counts = refs[11:16]
    elif handing:
        *outs, hand_ref, held, fresh, owners = refs[5:11]
    else:
        *outs, held, fresh, owners = refs[5:10]
    pages, page_len = key_ref.shape[1], outs[0].shape[1]
    head_count, own_rows, steps = key_ref.shape[0], fresh.shape[1], fresh.shape[2]
    me = lax.axis_index("tp")
    head = lax.rem(me + other, head_count)
    pairs = [
        (owner_ref, owners),
        (fresh_key_ref, fresh.at[0]),
        (fresh_value_ref, fresh.at[1]),
    ]
    if handing:
        pairs += [(key_ref, held.at[0]), (value_ref, held.at[1])]
    else:
        pairs += [(key_ref.at[head], held.at[0, 0]), (value_ref.at[head], held.at[1, 0])]
    if with_queries:
        width = query_ref.shape[1]
        columns = pl.ds(pl.multiple_of(head * width, LANES), width)
        pairs += [(count_ref, counts), (all_query_ref.at[:, :, columns], queries)]
    copies = [
        pltpu.make_async_copy(source, target, arrived.at[i])
        for i, (source, target) in enumerate(pairs)
    ]
    for copy in copies:
        copy.start()
    copies[0].wait()
    outs[0][pages + 1] = owner_page(owners[...], page_len).astype(jnp.bfloat16)
    if handing:
        cap = hand_ref.shape[2]
        picks = slot_picks(owners, me, [handing], cap, lax.axis_size("tp"))
    for i in range(2):
        copies[1 + i].wait()
        new = fresh[i]
        part = new[:, :, :HD]
        for which in range(1, head_count):
            part = jnp.where(head == which, new[:, :, which * HD : (which + 1) * HD], part)
        lines = part.reshape(own_rows * steps, HD)
        if own_rows * steps < page_len:
            spare = jnp.zeros((page_len - own_rows * steps, HD), jnp.bfloat16)
            lines = jnp.concatenate([lines, spare])
        outs[i][pages] = lines
    for i in range(2):
        copies[3 + i].wait()
        paged = held[i, head] if handing else held[i, 0]
        outs[i][:pages] = paged.reshape(pages, page_len, HD)
    if handing:
        for i in range(2):
            for which in range(head_count):
                place_rows(held.at[i, which], picks[which], [hand_ref.at[i, which]])
    if with_queries:
        copies[5].wait()
        row_lines = query_ref.shape[0]
        row = lax.broadcasted_iota(jnp.int32, (1, row_lines), 1) // steps
        starts = jnp.zeros((1, row_lines), jnp.int32)
        ends = jnp.zeros((1, row_lines), jnp.int32)
        for r in range(counts.shape[0]):
            starts = starts + jnp.where(row > r, counts[r], 0)
            ends = ends + jnp.where(row >= r, counts[r], 0)
        line = lax.broadcasted_iota(jnp.int32, (8, row_lines), 0)
        bounds_ref[...] = jnp.where(line == 0, starts, ends)
        copies[6].wait()
        query_ref[...] = queries[...].reshape(row_lines, query_ref.shape[1])


def owner_page(owners, lines):
    head_count, pages = owners.shape
    page = jnp.concatenate(
        [owners.astype(jnp.float32), jnp.zeros((head_count, LANES - pages), jnp.float32)], axis=1
    )
    return jnp.concatenate([page, jnp.zeros((lines - head_count, LANES), jnp.float32)])


def gather_tokens(
    other, caches, fresh, owner, queries=None, counts=None, handing=0, cap=0, follows=()
):
    head_count, pages, width = caches[0].shape
    page_len = width // HD
    with_queries = queries is not None
    operands = [*caches, *fresh, owner]
    out_shape = [
        jax.ShapeDtypeStruct((pages + extra, page_len, HD), jnp.bfloat16) for extra in (2, 1)
    ]
    scratch = [
        pltpu.VMEM((2, head_count if handing else 1, pages, width), jnp.bfloat16),
        pltpu.VMEM((2,) + fresh[0].shape, jnp.bfloat16),
        pltpu.VMEM(owner.shape, jnp.int32),
    ]
    if handing:
        out_shape.append(jax.ShapeDtypeStruct((2, head_count, cap, width), jnp.bfloat16))
    if with_queries:
        operands += [queries, counts]
        rows, steps, query_width = queries.shape
        query_width = query_width // head_count
        out_shape += [
            jax.ShapeDtypeStruct((rows * steps, query_width), jnp.bfloat16),
            jax.ShapeDtypeStruct((8, rows * steps), jnp.int32),
        ]
        scratch += [
            pltpu.VMEM((rows, steps, query_width), jnp.bfloat16),
            pltpu.SMEM(counts.shape, jnp.int32),
        ]
    return call(
        functools.partial(gather_tokens_kernel, other, with_queries, handing),
        in_hbm(*operands),
        [hbm()] * len(operands),
        follows,
        out_specs=[vmem()] * len(out_shape),
        out_shape=out_shape,
        scratch_shapes=scratch + [pltpu.SemaphoreType.DMA((len(operands),))],
        compiler_params=params(6),
        name="gather_tokens",
    )


def membership(bounds, owner, pages, own_lines, member_lines, row_lines, steps):
    query_line = lax.broadcasted_iota(jnp.int32, (1, row_lines), 1)
    starts, ends = bounds[0:1, :], bounds[1:2, :]
    page_lines = pages * steps
    line = lax.broadcasted_iota(jnp.int32, (member_lines, row_lines), 0)
    page = owner * pages + line // steps
    in_row = (starts <= page) & (page < ends) & (line % steps == query_line % steps)
    own_line = line - page_lines
    is_own = (
        (own_line >= 0) & (own_line < own_lines) & (query_line == owner * own_lines + own_line)
    )
    member = (((line < page_lines) & in_row) | is_own).astype(jnp.float32)
    return member, jnp.transpose(member)


def prepare_kernel(steps, own_lines, page_len, neighbours, bounds_ref, query_ref, *refs):
    row_lines = query_ref.shape[0]
    for place, neighbour in enumerate(neighbours):
        chosen_ref, member_ref, turned_ref = refs[3 * place : 3 * place + 3]
        member_lines = member_ref.shape[0]
        pages = (member_lines - round_up(page_len, LANES)) // steps
        member, turned = membership(
            bounds_ref[...],
            lax.axis_index("tp") ^ neighbour,
            pages,
            own_lines,
            member_lines,
            row_lines,
            steps,
        )
        chosen_ref[...] = jnp.dot(
            member.astype(jnp.bfloat16), query_ref[...], preferred_element_type=jnp.float32
        ).astype(jnp.bfloat16)
        member_ref[...] = member
        turned_ref[...] = turned


def prepare(bounds, query, neighbours, pages, page_len, own_lines, steps):
    row_lines, query_width = query.shape
    member_lines = pages * steps + round_up(page_len, LANES)
    shapes = (
        jax.ShapeDtypeStruct((member_lines, query_width), jnp.bfloat16),
        jax.ShapeDtypeStruct((member_lines, row_lines), jnp.float32),
        jax.ShapeDtypeStruct((row_lines, member_lines), jnp.float32),
    )
    out = call(
        functools.partial(prepare_kernel, steps, own_lines, page_len, neighbours),
        (bounds, query),
        [vmem()] * 2,
        out_specs=[vmem()] * (3 * len(neighbours)),
        out_shape=shapes * len(neighbours),
        compiler_params=params(8),
        name="prepare",
    )
    return [out[3 * place : 3 * place + 3] for place in range(len(neighbours))]


def page_batch(pages, page_len):
    return min(pages, max(1, LANES // page_len))


def score_kernel(steps, has_earlier, chosen, member_ref, turned_ref, keys_ref, *refs):
    if has_earlier:
        early_max_ref, early_total_ref = refs[:2]
        refs = refs[2:]
    weights_ref, fresh_ref, max_ref, total_ref, scores, fresh_scores = refs
    row_lines, query_width = turned_ref.shape[0], chosen.shape[1]
    group = query_width // HD
    page_len = keys_ref.shape[1]
    batch = weights_ref.shape[2] // page_len
    blocks, lines = weights_ref.shape[0], batch * steps
    pages = blocks * batch
    spare = member_ref.shape[0] - pages * steps - page_len
    scale = HD ** (-0.5)
    lane = lax.broadcasted_iota(jnp.int32, (1, LANES), 1)
    member, turned = member_ref[...], turned_ref[...]
    is_member = turned > 0

    line = lax.broadcasted_iota(jnp.int32, (group * lines, batch * page_len), 0)
    token = lax.broadcasted_iota(jnp.int32, (group * lines, batch * page_len), 1)
    page_mask = (line % lines) // steps == token // page_len
    line = lax.broadcasted_iota(jnp.int32, (group * page_len, page_len), 0) % page_len
    token = lax.broadcasted_iota(jnp.int32, (group * page_len, page_len), 1)
    fresh_mask = (line // steps == token // steps) & (token % steps <= line % steps)

    def score(first_line, count, keys, mask):
        rows = slice(first_line, first_line + count)
        queries = jnp.concatenate(
            [chosen[rows, g * HD : (g + 1) * HD] for g in range(group)], axis=0
        )
        found = lax.dot_general(
            queries, keys, (((1,), (1,)), ((), ())), preferred_element_type=jnp.float32
        )
        found = jnp.where(mask, found * scale, NEGATIVE)
        largest = jnp.max(found, axis=1, keepdims=True)
        block_max = jnp.zeros((count, LANES), jnp.float32)
        for g in range(group):
            block_max = jnp.where(lane == g, largest[g * count : (g + 1) * count], block_max)
        return found, block_max

    maxima = []
    for block in range(blocks):
        keys = keys_ref[block * batch : (block + 1) * batch].reshape(batch * page_len, HD)
        scores[block], block_max = score(block * lines, lines, keys, page_mask)
        maxima.append(block_max)
    fresh_scores[...], block_max = score(pages * steps, page_len, keys_ref[pages], fresh_mask)
    maxima.append(block_max)
    if spare:
        maxima.append(jnp.zeros((spare, LANES), jnp.float32))

    line_max = jnp.transpose(jnp.concatenate(maxima, axis=0))
    row_max = jnp.full((row_lines, LANES), NEGATIVE, jnp.float32)
    for g in range(group):
        best = jnp.max(
            jnp.where(is_member, line_max[g : g + 1, :], NEGATIVE), axis=1, keepdims=True
        )
        row_max = jnp.where(lane == g, best, row_max)
    if has_earlier:
        row_max = jnp.maximum(row_max, early_max_ref[...])
    spread = jnp.dot(
        member, row_max, precision=HIGHEST, preferred_element_type=jnp.float32
    )

    def weigh(first_line, count, found):
        rows = spread[first_line : first_line + count]
        shift = jnp.concatenate([rows[:, g : g + 1] for g in range(group)], axis=0)
        weights = jnp.exp(jnp.minimum(found - shift, 0.0)).astype(jnp.bfloat16)
        ones = jnp.ones((weights.shape[1], LANES), jnp.bfloat16)
        total = jnp.dot(weights, ones, preferred_element_type=jnp.float32)
        block_total = jnp.zeros((count, LANES), jnp.float32)
        for g in range(group):
            block_total = jnp.where(lane == g, total[g * count : (g + 1) * count], block_total)
        return weights, block_total

    totals = []
    for block in range(blocks):
        weights_ref[block], total = weigh(block * lines, lines, scores[block])
        totals.append(total)
    fresh_ref[...], total = weigh(pages * steps, page_len, fresh_scores[...])
    totals.append(total)
    if spare:
        totals.append(jnp.zeros((spare, LANES), jnp.float32))
    row_total = jnp.dot(
        turned,
        jnp.concatenate(totals, axis=0),
        precision=HIGHEST,
        preferred_element_type=jnp.float32,
    )
    if has_earlier:
        row_total = row_total + early_total_ref[...] * jnp.exp(early_max_ref[...] - row_max)
    max_ref[...] = row_max
    total_ref[...] = row_total


def score(choice, keys, steps, earlier=(), flops=0):
    (member_lines, query_width), row_lines = choice[0].shape, choice[2].shape[0]
    group = query_width // HD
    page_len = keys.shape[1]
    pages = (member_lines - round_up(page_len, LANES)) // steps
    batch = page_batch(pages, page_len)
    blocks = pages // batch
    shapes = ((blocks, group * batch * steps, batch * page_len), (group * page_len, page_len))
    stat = jax.ShapeDtypeStruct((row_lines, LANES), jnp.float32)
    operands = (*choice, keys, *earlier)
    return call(
        functools.partial(score_kernel, steps, bool(earlier)),
        operands,
        [vmem()] * len(operands),
        flops=flops,
        out_specs=[vmem()] * 4,
        out_shape=[jax.ShapeDtypeStruct(shape, jnp.bfloat16) for shape in shapes] + [stat, stat],
        scratch_shapes=[pltpu.VMEM(shape, jnp.float32) for shape in shapes],
        compiler_params=params(12),
        name="score",
    )


def value_kernel(steps, chunk, chunks, has_earlier, has_notes, last, *refs):
    weights_ref, fresh_ref, turned_ref, values_ref, max_ref, total_ref = refs[:6]
    refs = refs[6:]
    if has_earlier:
        early_max_ref, early_numer_ref = refs[:2]
        refs = refs[2:]
    if has_notes:
        own_keys_ref, near_keys_ref = refs[:2]
        refs = refs[2:]
    out_ref, high, low = refs
    row_lines, member_lines = turned_ref.shape
    page_len = values_ref.shape[1]
    blocks, batch = weights_ref.shape[0], weights_ref.shape[2] // page_len
    lines, pages = batch * steps, blocks * batch
    all_groups = weights_ref.shape[1] // lines
    group = all_groups // chunks
    first = chunk * group
    used = pages * steps + page_len

    def gain(first_line, count, weights, values):
        numer = jnp.dot(weights, values, preferred_element_type=jnp.float32)
        rounded = numer.astype(jnp.bfloat16)
        rest = (numer - rounded.astype(jnp.float32)).astype(jnp.bfloat16)
        for g in range(group):
            part = slice(g * count, (g + 1) * count)
            columns = slice(g * HD, (g + 1) * HD)
            high[first_line : first_line + count, columns] = rounded[part]
            low[first_line : first_line + count, columns] = rest[part]

    for block in range(blocks):
        weights = weights_ref[block, first * lines : (first + group) * lines]
        values = values_ref[block * batch : (block + 1) * batch].reshape(batch * page_len, HD)
        gain(block * lines, lines, weights, values)
    weights = fresh_ref[first * page_len : (first + group) * page_len]
    gain(pages * steps, page_len, weights, values_ref[pages])
    if member_lines > used:
        high[used:, :] = jnp.zeros((member_lines - used, group * HD), jnp.bfloat16)
        low[used:, :] = jnp.zeros((member_lines - used, group * HD), jnp.bfloat16)

    lane = lax.broadcasted_iota(jnp.int32, (1, LANES), 1)
    row_max, row_total = max_ref[...], total_ref[...]
    present = row_total > 0
    inverse = jnp.where(present, 1.0 / jnp.where(present, row_total, 1.0), 0.0)
    if has_earlier:
        scale_early = jnp.exp(early_max_ref[...] - row_max)
    if last and chunk == 0:
        log_sum = jnp.where(
            present & (lane < all_groups),
            row_max + jnp.log(jnp.where(present, row_total, 1.0)),
            jnp.where(lane < all_groups, NEGATIVE, 0.0),
        )
        lanes = split_sums(log_sum, all_groups)
        if has_notes:
            lanes = lanes + owner_notes(
                own_keys_ref[pages + 1], near_keys_ref[pages + 1], row_lines, 3 * all_groups
            )
        out_ref[:, group * HD :] = lanes.astype(jnp.bfloat16)
    turned = turned_ref[...].astype(jnp.bfloat16)
    for g in range(group):
        columns = slice(g * HD, (g + 1) * HD)
        which = slice(first + g, first + g + 1)
        numer = jnp.dot(turned, high[:, columns], preferred_element_type=jnp.float32) + jnp.dot(
            turned, low[:, columns], preferred_element_type=jnp.float32
        )
        if has_earlier:
            numer = numer + early_numer_ref[:, columns] * scale_early[:, which]
        if last:
            numer = numer * inverse[:, which]
        out_ref[:, columns] = numer.astype(out_ref.dtype)


def value(scored, turned, values, steps, chunk, chunks, last, earlier=(), notes=(), follows=()):
    row_lines, member_lines = turned.shape
    page_len = values.shape[1]
    group = scored[1].shape[0] // page_len // chunks
    wide = group * HD + (LANES if last and chunk == 0 else 0)
    operands = (*scored[:2], turned, values, *scored[2:], *earlier, *notes)
    return call(
        functools.partial(value_kernel, steps, chunk, chunks, bool(earlier), bool(notes), last),
        operands,
        [vmem()] * len(operands),
        follows,
        out_specs=vmem(),
        out_shape=jax.ShapeDtypeStruct(
            (row_lines, wide), jnp.bfloat16 if last else jnp.float32
        ),
        scratch_shapes=[pltpu.VMEM((member_lines, group * HD), jnp.bfloat16)] * 2,
        compiler_params=params(8),
        name="value",
    )


def split_sums(value, group):
    first = value.astype(jnp.bfloat16).astype(jnp.float32)
    rest = value - first
    second = rest.astype(jnp.bfloat16).astype(jnp.float32)
    third = rest - second
    return first + pltpu.roll(second, group, axis=1) + pltpu.roll(third, 2 * group, axis=1)


def owner_notes(own, near_page, row_lines, first_lane):
    lines = near_page.shape[0]
    notes = jnp.concatenate(
        [
            own.astype(jnp.float32),
            near_page.astype(jnp.float32),
            jnp.zeros((row_lines - 2 * lines, LANES), jnp.float32),
        ]
    )
    return pltpu.roll(notes, first_lane, axis=1)


def join_sums(parts, group):
    parts = parts.astype(jnp.float32)
    return (
        parts
        + pltpu.roll(parts, LANES - group, axis=1)
        + pltpu.roll(parts, LANES - 2 * group, axis=1)
    )


def combine_kernel(group, first, sums_ref, their_sums_ref, mine_ref, theirs_ref, out_ref):
    sums = join_sums(sums_ref[:, -LANES:], group)
    their_sums = join_sums(their_sums_ref[:, -LANES:], group)
    largest = jnp.maximum(sums, their_sums)
    weight = jnp.exp(sums - largest)
    their_weight = jnp.exp(their_sums - largest)
    inverse = 1.0 / (weight + their_weight)
    weight = weight * inverse
    their_weight = their_weight * inverse
    for place in range(out_ref.shape[1] // HD):
        g = first + place
        columns = slice(place * HD, (place + 1) * HD)
        out_ref[:, columns] = (
            mine_ref[:, columns].astype(jnp.float32) * weight[:, g : g + 1]
            + theirs_ref[:, columns].astype(jnp.float32) * their_weight[:, g : g + 1]
        ).astype(jnp.bfloat16)


def combine(mine, theirs, chunk, follows=()):
    row_lines, width = mine[0].shape
    width -= LANES
    group = width // HD * len(mine)
    return call(
        functools.partial(combine_kernel, group, chunk * width // HD),
        (mine[0], theirs[0], mine[chunk], theirs[chunk]),
        [vmem()] * 4,
        follows,
        out_specs=vmem(),
        out_shape=jax.ShapeDtypeStruct((row_lines, width), jnp.bfloat16),
        compiler_params=params(4),
        name="combine",
    )


def block_row(own, chunk, chunks, head_count, depth):
    head = lax.rem(lax.axis_index("tp") + (0 if own else 1), head_count)
    return pl.multiple_of((head * chunks + chunk) * depth, depth)


def fetch_kernel(blocks, chunks, head_count, weight_ref, held_ref, done_ref, arrived):
    depth = held_ref.shape[0] // len(blocks)
    pieces = arrived.shape[0] // len(blocks)
    size = depth // pieces
    copies = []
    for place, (own, chunk) in enumerate(blocks):
        base = block_row(own, chunk, chunks, head_count, depth)
        for piece in range(pieces):
            copies.append(
                pltpu.make_async_copy(
                    weight_ref.at[pl.ds(pl.multiple_of(base + piece * size, size), size)],
                    held_ref.at[pl.ds(place * depth + piece * size, size)],
                    arrived.at[place * pieces + piece],
                )
            )
    for copy in copies:
        copy.start()
    done_ref[...] = jnp.zeros_like(done_ref)
    for copy in copies:
        copy.wait()


def fetch(weight, blocks, chunks, head_count, depth, follows):
    pieces = 4
    return call(
        functools.partial(fetch_kernel, blocks, chunks, head_count),
        in_hbm(weight),
        [hbm()],
        follows,
        out_specs=(vmem(), vmem()),
        out_shape=(
            pltpu.VMEM((len(blocks) * depth, weight.shape[1]), weight.dtype),
            jax.ShapeDtypeStruct((8, LANES), jnp.float32),
        ),
        scratch_shapes=[pltpu.SemaphoreType.DMA((len(blocks) * pieces,))],
        compiler_params=params(1),
        name="fetch",
    )


def project_kernel(parts, has_total, chunk_lines, first, offsets, chunks, head_count, *refs):
    input_refs, weight_ref, refs = refs[:parts], refs[parts], refs[parts + 1 :]
    streamed = offsets is None
    if streamed:
        held, arrived = refs[-2:]
        refs = refs[:-2]
    outs = refs[1:] if has_total else refs
    depth, width = input_refs[0].shape[1], outs[0].shape[-1]
    block = min(width, 512)
    count = width // block

    def piece(index):
        return pltpu.make_async_copy(
            weight_ref.at[
                pl.ds(block_row(True, 0, chunks, head_count, depth), depth),
                pl.ds(first + index * block, block),
            ],
            held.at[:, pl.ds(index * block, block)],
            arrived.at[index],
        )

    if streamed:
        for index in range(count):
            piece(index).start()
    for index in range(count):
        start = index * block
        columns = slice(first + start, first + start + block)
        product = refs[0][:, columns] if has_total else 0.0
        if streamed:
            piece(index).wait()
            product = product + jnp.dot(
                input_refs[0][...],
                held[:, start : start + block],
                preferred_element_type=jnp.float32,
            )
        else:
            for input_ref, offset in zip(input_refs, offsets):
                product = product + jnp.dot(
                    input_ref[...],
                    weight_ref[offset * depth : (offset + 1) * depth, columns],
                    preferred_element_type=jnp.float32,
                )
        if chunk_lines is None:
            outs[0][:, start : start + block] = product
            continue
        core = lax.rem(lax.axis_index("kv"), 2)
        keep_ref, send_ref = outs
        for pair in range(keep_ref.shape[0]):
            even = product[2 * pair * chunk_lines : (2 * pair + 1) * chunk_lines]
            odd = product[(2 * pair + 1) * chunk_lines : (2 * pair + 2) * chunk_lines]
            keep_ref[pair, :, start : start + block] = jnp.where(core == 0, even, odd)
            send_ref[pair, :, start : start + block] = jnp.where(core == 0, odd, even).astype(
                send_ref.dtype
            )


def project(inputs, weight, offsets, chunks, head_count, total, columns, chunk_lines, follows=()):
    row_lines, depth = inputs[0].shape
    first, width = columns
    in_specs = [vmem()] * len(inputs) + [hbm() if offsets is None else vmem()]
    operands = [*inputs, *(in_hbm(weight) if offsets is None else [weight])]
    if total is not None:
        in_specs.append(vmem())
        operands.append(total)
    if chunk_lines is None:
        out_shape = jax.ShapeDtypeStruct((row_lines, width), jnp.float32)
        out_specs = vmem()
    else:
        pairs = row_lines // (2 * chunk_lines)
        shape = (pairs, chunk_lines, width)
        out_shape = (
            jax.ShapeDtypeStruct(shape, jnp.float32),
            jax.ShapeDtypeStruct(shape, jnp.bfloat16),
        )
        out_specs = (vmem(), vmem())
    scratch = []
    if offsets is None:
        scratch = [
            pltpu.VMEM((depth, width), weight.dtype),
            pltpu.SemaphoreType.DMA((max(1, width // 512),)),
        ]
    return call(
        functools.partial(
            project_kernel,
            len(inputs),
            total is not None,
            chunk_lines,
            first,
            offsets,
            chunks,
            head_count,
        ),
        operands,
        in_specs,
        follows,
        out_specs=out_specs,
        out_shape=out_shape,
        scratch_shapes=scratch,
        compiler_params=params(16 if offsets is None else 8),
        name="project",
    )


def add_core_kernel(keep_ref, got_ref, own_ref, *send_refs):
    half = lax.axis_index("kv") // 2
    own_ref[...] = keep_ref[half] + got_ref[half].astype(jnp.float32)
    for step, send_ref in enumerate(send_refs, 1):
        part = keep_ref[half ^ step] + got_ref[half ^ step].astype(jnp.float32)
        send_ref[...] = part.astype(send_ref.dtype)


def sum_heads(keep, send, kv_size):
    got = lax.ppermute(send, "kv", flip(kv_size, 1))
    shape = keep.shape[1:]
    own, *sends = call(
        add_core_kernel,
        (keep, got),
        [vmem(), vmem()],
        out_specs=[vmem()] * (kv_size // 2),
        out_shape=[jax.ShapeDtypeStruct(shape, jnp.float32)]
        + [jax.ShapeDtypeStruct(shape, jnp.bfloat16)] * (kv_size // 2 - 1),
        compiler_params=params(4),
        name="add_core",
    )
    return [own] + [
        lax.ppermute(part, "kv", flip(kv_size, 2 * step)) for step, part in enumerate(sends, 1)
    ]


def finish_kernel(pieces, *refs):
    parts, out_ref, done_ref = refs[:-2], refs[-2], refs[-1]
    done_ref[...] = jnp.zeros_like(done_ref)
    each = len(parts) // pieces
    steps, width = out_ref.shape[1], out_ref.shape[2] // pieces
    for piece in range(pieces):
        total = parts[piece * each][...]
        for part in parts[piece * each + 1 : (piece + 1) * each]:
            total = total + part[...].astype(jnp.float32)
        out_ref[:, :, piece * width : (piece + 1) * width] = total.astype(jnp.bfloat16).reshape(
            -1, steps, width
        )


def finish(results, steps):
    lines, width = results[0][0].shape
    parts = [part for pieces in results for part in pieces]
    return call(
        functools.partial(finish_kernel, len(results)),
        parts,
        [vmem()] * len(parts),
        out_specs=(vmem(), vmem()),
        out_shape=(
            jax.ShapeDtypeStruct((lines // steps, steps, width * len(results)), jnp.bfloat16),
            jax.ShapeDtypeStruct((8, LANES), jnp.float32),
        ),
        compiler_params=params(4),
        name="finish",
    )


def body(
    queries, fresh_keys, fresh_values, cache_keys, cache_values, page_counts, page_owner, out_weight
):
    tp_size, kv_size = lax.axis_size("tp"), lax.axis_size("kv")
    head_count, pages_here, page_width = cache_keys.shape
    row_count, step_count, query_width = queries.shape
    own_lines = fresh_keys.shape[0] * step_count
    page_len = page_width // HD
    row_lines = row_count * step_count
    head_width = query_width // head_count
    group = head_width // HD
    cap = max(2, (2 * pages_here + tp_size - 1) // tp_size)
    out_width = out_weight.shape[1]
    chunk_lines = row_lines // kv_size
    caches = (cache_keys, cache_values)
    fresh = (fresh_keys, fresh_values)

    paired = head_count == 2 and tp_size == 4 and group % 2 == 0 and cap % 16 == 0
    paired = paired and 3 * group + pages_here <= LANES and 2 * page_len <= row_lines
    chunks = 2 if paired else 1
    part = head_width // chunks
    everything = (0, out_width)

    if paired:
        keys, values, send_last = gather_tokens(1, caches, fresh, page_owner, handing=3, cap=cap)
        near_keys = lax.ppermute(keys, "tp", flip(tp_size, 1))
        got_inner = lax.ppermute(send_last, "tp", [(1, 2), (2, 1)])
        own_keys, own_values, query, bounds = gather_tokens(
            0, caches, fresh, page_owner, queries, page_counts, follows=(send_last,)
        )
        near_values = lax.ppermute(tie(values, bounds), "tp", flip(tp_size, 1))
        own_choice, near_choice = prepare(
            bounds, query, (0, 1), pages_here, page_len, own_lines, step_count
        )
        scored = score(own_choice, own_keys, step_count)
        early_numers = [
            value(scored, own_choice[2], own_values, step_count, chunk, chunks, False)
            for chunk in range(chunks)
        ]
        early_max, early_total = scored[2:]
        scored = score(near_choice, near_keys, step_count, (early_max, early_total), 1 << 34)
        payload = [
            value(
                scored,
                near_choice[2],
                near_values,
                step_count,
                chunk,
                chunks,
                True,
                (early_max, early_numers[chunk]),
                () if chunk else (own_keys, near_keys),
            )
            for chunk in range(chunks)
        ]
        jobs = ((2, True), (1, False), (0, True))
        send_far, send_near, kept = place_pages(
            page_owner, caches, jobs, cap, tp_size, False, (payload[1],)
        )
        blocks = ((True, 1), (False, 0))
        held, held_done = fetch(out_weight, blocks, chunks, head_count, part, payload[1:])
        payload[1] = tie(payload[1], held_done)
        held_last, held_done = fetch(
            out_weight, ((False, 1),), chunks, head_count, part, (held_done,)
        )
        theirs = [lax.ppermute(p, "tp", flip(tp_size, 2)) for p in payload]
        got_near = lax.ppermute(tie(send_near, held_done), "tp", flip(tp_size, 1))
        near_pages = place_near(near_keys, near_values, head_count, cap, tp_size)
        first_part = combine(payload, theirs, 0)
        near_first = lax.ppermute(first_part, "tp", flip(tp_size, 1))
        total = project([first_part], out_weight, None, chunks, head_count, None, everything, None)
        got_far = lax.ppermute(tie(send_far, total), "tp", flip(tp_size, 2))
        got_outer = lax.ppermute(tie(send_last, total), "tp", [(0, 3), (3, 0)])
        second_part = combine(payload, theirs, 1, (got_near, total, got_inner))
        near_second = lax.ppermute(second_part, "tp", flip(tp_size, 1))
        own_parts, near_parts = (first_part, second_part), (near_first, near_second)
        plan = ((0, None, None), (1, None, 0), (1, None, 1), (3, (1, 2), None))
        *settled, settled_done = settle(
            [kept, near_pages, got_near, got_inner], plan, head_count, tp_size * cap, (), (total,)
        )
        total = project(
            [own_parts[1], near_parts[0]],
            held,
            (0, 1),
            chunks,
            head_count,
            total,
            everything,
            None,
            (settled_done,),
        )
        results = []
        for first in (0, out_width // 2):
            columns = (first, out_width // 2)
            keep, send = project(
                [near_parts[1]],
                held_last,
                (0,),
                chunks,
                head_count,
                total,
                columns,
                chunk_lines,
            )
            results.append(sum_heads(keep, send, kv_size))
        attention_out, finished = finish(results, step_count)
        slot_rows = slot_rows_near(
            bounds,
            payload[0],
            theirs[0],
            pages_here,
            3 * group,
            page_len,
            cap,
            (head_count, tp_size * cap),
            step_count,
            (results[1][0],),
        )
        plan = ((2, None, None), (3, (0, 3), None))
        slot_keys, slot_values, _ = settle(
            [got_far, got_outer], plan, head_count, tp_size * cap, settled, (finished,)
        )
        return (attention_out, slot_keys, slot_values, slot_rows)

    def hand_over(cache):
        jobs = tuple((d, True) for d in range(tp_size))
        sent = place_pages(page_owner, (cache,), jobs, cap, tp_size, True)
        got = lax.all_to_all(
            jnp.concatenate(sent), "tp", split_axis=0, concat_axis=0, tiled=True
        )
        return got.transpose(1, 0, 2, 3).reshape(head_count, tp_size * cap, page_width)

    slot_keys, slot_values = hand_over(cache_keys), hand_over(cache_values)
    slot_rows = slot_rows_gathered(page_owner, page_counts, cap)
    attended = []
    for head in range(head_count):
        cut = slice(head, head + 1)
        lanes = slice(head * HD, (head + 1) * HD)
        keys, values, query, bounds = gather_tokens(
            0,
            [cache[cut] for cache in caches],
            [new[:, :, lanes] for new in fresh],
            page_owner[cut],
            queries[:, :, head * head_width : (head + 1) * head_width],
            page_counts,
        )
        (choice,) = prepare(
            bounds, query, (0,), pages_here, page_len, own_lines, step_count
        )
        scored = score(choice, keys, step_count)
        payload = value(scored, choice[2], values, step_count, 0, 1, True)
        raw = payload[:, part:].astype(jnp.float32)
        sums = raw[:, :group] + raw[:, group : 2 * group] + raw[:, 2 * group : 3 * group]
        weight = jnp.exp(sums - lax.pmax(sums, "tp"))
        numer = payload[:, :part].astype(jnp.float32).reshape(row_lines, group, HD)
        numer = lax.psum(numer * weight[..., None], "tp")
        joined = numer / lax.psum(weight, "tp")[..., None]
        attended.append(joined.reshape(row_lines, head_width).astype(jnp.bfloat16))
    keep, send = project(
        [jnp.concatenate(attended, axis=1)], out_weight, None, 1, 1, None, everything, chunk_lines
    )
    attention_out, _ = finish([sum_heads(keep, send, kv_size)], step_count)
    return (attention_out, slot_keys, slot_values, slot_rows)


def solution(mesh):
    return jax.shard_map(
        body,
        mesh=mesh,
        in_specs=(
            P("grp", None, "kv"),
            P(("grp", "tp"), None, "kv"),
            P(("grp", "tp"), None, "kv"),
            P(("grp", "kv"), "tp", None),
            P(("grp", "kv"), "tp", None),
            P("grp"),
            P(("grp", "kv"), "tp"),
            P("kv", "tp"),
        ),
        out_specs=(
            P(("grp", "kv"), None, "tp"),
            P(("grp", "kv"), "tp", None),
            P(("grp", "kv"), "tp", None),
            P(("grp", "kv"), "tp"),
        ),
        check_vma=False,
    )
```
